128 devices in a mesh: pb: 8 (over x, z_lo), ka: 8 (over y, core), ha: 2 (over z_hi).
Axes of the slice: x: 4, y: 4, z: 4 (z_hi: 2, z_lo: 2; z = z_hi * 2 + z_lo), core: 2. Of those that a mesh axis runs over, the one named last changes fastest.
Arguments:
- query_states: bfloat16 [8192, 4096], P(('pb', 'ka'), 'ha'), parts along dimension 1, may hold values from -6 to 6
- key_states: bfloat16 [8192, 2048], P(('ka', 'pb'), 'ha'), parts along dimension 1, may hold values from -6 to 6
- value_states: bfloat16 [8192, 2048], P(('ka', 'pb'), 'ha'), parts along dimension 1, may hold values from -6 to 6
- attn_output: bfloat16 [8192, 4096], P(('pb', 'ka'), 'ha'), parts along dimension 1, may hold values from -6 to 6
- output_grad: bfloat16 [8192, 4096], P(('pb', 'ka'), 'ha'), parts along dimension 1, may hold values from -48 to 48
- logsumexp: float32 [32, 8192], P('ha', ('pb', 'ka')), parts along dimension 0, as said below
- block_order: int32 [32], P('ha'), parts along dimension 0, may hold values from 0 to 15, as said below
- doc_lengths: int32 [8], P('ha'), parts along dimension 0, may hold values from 512 to 4096, as said below
Outputs:
- query_grad: bfloat16 [8192, 4096], P(('pb', 'ka'), 'ha'), parts along dimension 1
- key_grad: bfloat16 [8192, 2048], P(('ka', 'pb'), 'ha'), parts along dimension 1
- value_grad: bfloat16 [8192, 2048], P(('ka', 'pb'), 'ha'), parts along dimension 1
The draws below stay inside these ranges and needn't reach their ends.
There are 2 independent parts, one for each index of `ha`. The reference program is written for one: setup_inputs(seed, part) draws one part's arguments, and reference() takes and returns one part's arrays. A program takes and returns all parts, laid end to end along the dimension named above; each array names one. Nothing has to cross between parts.
Inputs may be any that keep to these rules, and one draw needn't show every extreme that they name: `block_order`: slots 2i and 2i + 1 hold blocks b and 15 - b for some b; every block stands in one slot. `doc_lengths`: the lengths sum to 8192. logsumexp[h, r] minus the log of the number of positions of its document up to and including row r's position lies between -0.5 and 1.5.
All inputs are finite; a program needn't handle non-finite values.
Results may differ from the reference program's by a relative error of at most 0.0051.
Values may be sent and summed in bfloat16 or wider, within the bound.
A program may use at most 128 MiB of HBM per device.

```python
import jax
import jax.numpy as jnp
from jax import lax

QH = 2
KVH = 8
HD = 128
L = 8192
NBLK = 16
BLK = 512


def shared_layout(base):
    pair_key = jax.random.fold_in(base, 101)
    flip_key = jax.random.fold_in(base, 102)
    split_key = jax.random.fold_in(base, 103)
    shuffle_key = jax.random.fold_in(base, 104)
    firsts = jax.random.permutation(pair_key, NBLK // 2).astype(jnp.int32)
    flips = jax.random.randint(flip_key, (NBLK // 2,), 0, 2, dtype=jnp.int32)
    mirrored = NBLK - 1 - firsts
    even_slots = jnp.where(flips == 1, mirrored, firsts)
    odd_slots = jnp.where(flips == 1, firsts, mirrored)
    ordering = jnp.stack([even_slots, odd_slots], axis=1).reshape(NBLK).astype(jnp.int32)
    middle = jax.random.randint(split_key, (), L // 16, 3 * L // 8 + 1, dtype=jnp.int32)
    pieces = jnp.stack([jnp.full((), L // 2, jnp.int32), jnp.full((), L // 16, jnp.int32), middle, 7 * L // 16 - middle]).astype(jnp.int32)
    lengths = jax.random.permutation(shuffle_key, pieces).astype(jnp.int32)
    return (ordering, lengths)


def draw_block_order(key, part):
    ordering, lengths = shared_layout(key)
    return ordering


def draw_doc_lengths(key, part):
    ordering, lengths = shared_layout(key)
    return lengths


def draw_logsumexp(key, part):
    ordering, lengths = shared_layout(key)
    key = jax.random.fold_in(key, 7)
    row_ids = jnp.arange(L, dtype=jnp.int32)
    positions = ordering[row_ids // BLK] * BLK + row_ids % BLK
    ends = jnp.cumsum(lengths).astype(jnp.int32)
    starts = ends - lengths
    segments = jnp.sum((positions[:, None] >= ends[None, :]).astype(jnp.int32), axis=1)
    visible = (positions - starts[segments] + 1).astype(jnp.float32)
    offsets = jax.random.uniform(key, (QH * KVH, L), jnp.float32, minval=-0.5, maxval=1.5)
    return (jnp.log(visible)[None, :] + offsets).astype(jnp.float32)


def steps_of(own_key, dims, cuts, least, high):
    loudness, own = 1.0, jax.random.fold_in(own_key, 6)
    for dim, shards_of in cuts:
        steps = jnp.exp(jax.random.uniform(jax.random.fold_in(own, dim), (shards_of,), jnp.float32, least / len(cuts), high / len(cuts)))
        loudness = loudness * jnp.repeat(steps, dims[dim] // shards_of).reshape([-1 if axis == dim else 1 for axis in range(len(dims))])
    return loudness


def bell_draw(rng, extent, deviation, limit, split=(), held_as=jnp.bfloat16):
    array = jax.random.normal(rng, extent, jnp.float32) * deviation
    if len(split) > 0:
        array = steps_of(rng, extent, split, -0.22, 0.18) * array
    return jnp.clip(array, min=-limit, max=limit).astype(held_as)


def setup_inputs(seed: int = 0, part: int = 0) -> dict:
    keys = jax.random.split(jax.random.key(seed), 9)
    own_keys = jax.random.split(jax.random.fold_in(keys[8], part), 9)
    query_states = bell_draw(own_keys[0], (L, QH * KVH * HD), 1.0, 6.0, ((0, 64),))
    key_states = bell_draw(own_keys[1], (L, KVH * HD), 1.0, 6.0, ((0, 64),))
    value_states = bell_draw(own_keys[2], (L, KVH * HD), 1.0, 6.0, ((0, 64),))
    attn_output = bell_draw(own_keys[3], (L, QH * KVH * HD), 1.0, 6.0, ((0, 64),))
    output_grad = bell_draw(own_keys[4], (L, QH * KVH * HD), 8.0, 48.0, ((0, 64),))
    logsumexp = draw_logsumexp(jax.random.fold_in(jax.random.fold_in(keys[8], part), 71), part)
    block_order = draw_block_order(jax.random.fold_in(jax.random.fold_in(keys[8], part), 71), part)
    doc_lengths = draw_doc_lengths(jax.random.fold_in(jax.random.fold_in(keys[8], part), 71), part)
    return {"query_states": query_states, "key_states": key_states, "value_states": value_states, "attn_output": attn_output, "output_grad": output_grad, "logsumexp": logsumexp, "block_order": block_order, "doc_lengths": doc_lengths}


softcap = 50.0
score_scale = 144.0 ** -0.5


def reference(query_states, key_states, value_states, attn_output, output_grad, logsumexp, block_order, doc_lengths):
    total_rows = query_states.shape[0]
    heads = QH * KVH
    row_ids = jnp.arange(total_rows, dtype=jnp.int32)
    positions = (block_order[row_ids // BLK] * BLK + row_ids % BLK).astype(jnp.int32)
    ends = jnp.cumsum(doc_lengths).astype(jnp.int32)
    order_rows = jnp.argsort(positions, stable=True).astype(jnp.int32)
    seg_sorted = jnp.sum((row_ids[:, None] >= ends[None, :]).astype(jnp.int32), axis=1)
    queries = query_states[order_rows]
    keys_sorted = key_states[order_rows]
    values_sorted = value_states[order_rows]
    grads = output_grad[order_rows]
    saved = attn_output[order_rows]
    lse_sorted = logsumexp[:, order_rows]
    delta = jnp.sum(grads.reshape(total_rows, heads, HD).astype(jnp.float32) * saved.reshape(total_rows, heads, HD).astype(jnp.float32), axis=2).T
    acc_key = jnp.zeros((total_rows, KVH * HD), jnp.float32)
    acc_value = jnp.zeros((total_rows, KVH * HD), jnp.float32)
    query_parts = []
    for block_index in range(NBLK):
        start = block_index * BLK
        stop = start + BLK
        key_rows = keys_sorted[:stop]
        value_rows = values_sorted[:stop]
        query_rows = queries[start:stop]
        grad_rows = grads[start:stop]
        key_ids = jnp.arange(stop, dtype=jnp.int32)
        query_ids = start + jnp.arange(BLK, dtype=jnp.int32)
        allowed = (key_ids[None, :] <= query_ids[:, None]) & (seg_sorted[None, :stop] == seg_sorted[start:stop][:, None])
        lse_rows = lse_sorted[:, start:stop]
        delta_rows = delta[:, start:stop]

        def head_step(carry, head_index):
            part_key, part_value = carry
            column = head_index * HD
            kv_column = (head_index // QH) * HD
            query_head = lax.dynamic_slice_in_dim(query_rows, column, HD, 1)
            grad_head = lax.dynamic_slice_in_dim(grad_rows, column, HD, 1)
            key_head = lax.dynamic_slice_in_dim(key_rows, kv_column, HD, 1)
            value_head = lax.dynamic_slice_in_dim(value_rows, kv_column, HD, 1)
            lse_head = lax.dynamic_index_in_dim(lse_rows, head_index, 0, keepdims=False)
            delta_head = lax.dynamic_index_in_dim(delta_rows, head_index, 0, keepdims=False)
            raw = jnp.dot(query_head, key_head.T, preferred_element_type=jnp.float32) * score_scale
            capped = softcap * jnp.tanh(raw / softcap)
            prob = jnp.where(allowed, jnp.exp(capped - lse_head[:, None]), jnp.float32(0.0))
            prob_low = prob.astype(jnp.bfloat16)
            dprob = jnp.dot(grad_head, value_head.T, preferred_element_type=jnp.float32)
            ratio = capped / softcap
            dscore = (prob * (dprob - delta_head[:, None]) * (1.0 - ratio * ratio) * score_scale).astype(jnp.bfloat16)
            query_head_grad = jnp.dot(dscore, key_head, preferred_element_type=jnp.float32).astype(jnp.bfloat16)
            corner = (jnp.int32(0), kv_column.astype(jnp.int32))
            old_key = lax.dynamic_slice(part_key, corner, (stop, HD))
            old_value = lax.dynamic_slice(part_value, corner, (stop, HD))
            part_key = lax.dynamic_update_slice(part_key, old_key + jnp.dot(dscore.T, query_head, preferred_element_type=jnp.float32), corner)
            part_value = lax.dynamic_update_slice(part_value, old_value + jnp.dot(prob_low.T, grad_head, preferred_element_type=jnp.float32), corner)
            return (part_key, part_value), query_head_grad

        start_carry = (jnp.zeros((stop, KVH * HD), jnp.float32), jnp.zeros((stop, KVH * HD), jnp.float32))
        (part_key, part_value), head_grads = lax.scan(head_step, start_carry, jnp.arange(heads, dtype=jnp.int32))
        acc_key = acc_key.at[:stop].add(part_key)
        acc_value = acc_value.at[:stop].add(part_value)
        query_parts.append(jnp.transpose(head_grads, (1, 0, 2)).reshape(BLK, heads * HD))
    query_sorted = jnp.concatenate(query_parts, axis=0)
    query_grad = query_sorted[positions]
    key_grad = acc_key[positions].astype(jnp.bfloat16)
    value_grad = acc_value[positions].astype(jnp.bfloat16)
    return query_grad, key_grad, value_grad
```

```python
from functools import partial
import math

import jax
import jax.numpy as jnp
from jax import lax
from jax.experimental import pallas as pl
from jax.experimental.pallas import tpu as pltpu
from jax.sharding import PartitionSpec as P

HD = 128
BLK = 512
ROWS = 128
NX, NY = 4, 4
BF16 = jnp.bfloat16
F32 = jnp.float32

softcap = 50.0
score_scale = 144.0 ** (-0.5)
log2e = math.log2(math.e)

Y_ORDER = (0, 1, 3, 2)


def place():
    pb, ka = lax.axis_index("pb"), lax.axis_index("ka")
    return pb // 2, pb % 2, ka // 2, ka % 2


def device(x, z, y, c):
    return {"pb": 2 * x + z, "ka": 2 * y + c}


def remote(src, dst, send, recv, to):
    return pltpu.make_async_remote_copy(
        src_ref=src,
        dst_ref=dst,
        send_sem=send,
        recv_sem=recv,
        device_id=to,
        device_id_type=pl.DeviceIdType.MESH,
    )


def enter(x, z, y, c):
    barrier = pltpu.get_barrier_semaphore()
    for dy in range(NY):
        for dz in range(2):
            for dc in range(2):
                if (dy, dz, dc) != (0, 0, 0):
                    to = device(x, (z + dz) % 2, (y + dy) % NY, (c + dc) % 2)
                    pl.semaphore_signal(barrier, inc=1, device_id=to, device_id_type=pl.DeviceIdType.MESH)
    for dx in (1, 3):
        to = device((x + dx) % NX, z, y, c)
        pl.semaphore_signal(barrier, inc=1, device_id=to, device_id_type=pl.DeviceIdType.MESH)
    pl.semaphore_wait(barrier, 17)


def columns(head):
    return pl.ds(pl.multiple_of(head * HD, HD), HD)


def rows_at(start, count):
    return pl.ds(pl.multiple_of(start, ROWS), count)


def gather_kernel(
    q_ref, k_ref, v_ref, o_ref, g_ref, lse_ref,
    qh_ref, gh_ref, kv_ref, aux_ref,
    o_v, g_v, aux_v,
    load_sem, kv_send, kv_recv, x_send, x_recv, x2_send, x2_recv, sib_send, sib_recv, q_send, q_recv,
):
    x, z, y, c = place()
    loads = [
        pltpu.make_async_copy(o_ref, o_v, load_sem.at[0]),
        pltpu.make_async_copy(g_ref, g_v, load_sem.at[1]),
    ]
    for load in loads:
        load.start()
    enter(x, z, y, c)

    sibling = device(x, z, y, 1 - c)
    right, left = device((x + 1) % NX, z, y, c), device((x + 3) % NX, z, y, c)
    own_rows = rows_at((2 * y + c) * 1024 + (2 * x + z) * ROWS, ROWS)
    sends = []

    kv_copies = {}
    for dy in Y_ORDER:
        for dz in range(2):
            ty, tz = (y + dy) % NY, (z + dz) % 2
            for part, ref in enumerate((k_ref, v_ref)):
                src = ref.at[:, columns(2 * ty + tz)]
                dst = kv_ref.at[own_rows, pl.ds(part * HD, HD)]
                at = (dy * 2 + dz) * 2 + part
                if dy == 0 and dz == 0:
                    copy = pltpu.make_async_copy(src, dst, kv_recv.at[at])
                else:
                    copy = remote(src, dst, kv_send.at[at], kv_recv.at[at], device(x, tz, ty, c))
                    sends.append(copy)
                copy.start()
                kv_copies[dy, dz, part] = copy

    def kv_block(plane, dy):
        return rows_at((2 * ((y + NY - dy) % NY) + c) * 1024 + 2 * plane * ROWS, 2 * ROWS)

    def to_sibling(step, dy, rows):
        at = step * NY + dy
        copy = remote(kv_ref.at[rows, :], kv_ref.at[rows, :], sib_send.at[at], sib_recv.at[at], sibling)
        copy.start()
        sends.append(copy)
        return copy

    first, sib, q_copies = {}, [], []
    for dy in Y_ORDER:
        for dz in range(2):
            for part in range(2):
                copy = kv_copies[dy, dz, part]
                if dy == 0 and dz == 0:
                    copy.wait()
                else:
                    copy.wait_recv()
        rows = kv_block(x, dy)
        for way, to in ((0, right), (1, left)):
            at = way * NY + dy
            copy = remote(kv_ref.at[rows, :], kv_ref.at[rows, :], x_send.at[at], x_recv.at[at], to)
            copy.start()
            sends.append(copy)
            first[way, dy] = copy
        sib.append(to_sibling(0, dy, rows))
        for dz in range(2):
            for dc in range(2):
                ty, tz, tc = (y + dy) % NY, (z + dz) % 2, (c + dc) % 2
                head = 2 * (2 * ty + tz) + tc
                for part, (ref, out) in enumerate(((q_ref, qh_ref), (g_ref, gh_ref))):
                    src = ref.at[:, columns(head)]
                    dst = out.at[rows_at(z * 1024 + (2 * y + c) * ROWS, ROWS), :]
                    at = ((dy * 2 + dz) * 2 + dc) * 3 + part
                    if (dy, dz, dc) == (0, 0, 0):
                        copy = pltpu.make_async_copy(src, dst, q_recv.at[at])
                    else:
                        copy = remote(src, dst, q_send.at[at], q_recv.at[at], device(x, tz, ty, tc))
                        sends.append(copy)
                    copy.start()
                    q_copies.append(copy)

    for load in loads:
        load.wait()
    for h in range(16):
        cols = pl.ds(h * HD, HD)
        prod = g_v[:, cols].astype(F32) * o_v[:, cols].astype(F32)
        delta = jnp.sum(prod.T, axis=0, keepdims=True)
        lse = lse_ref[h : h + 1, :] * log2e
        aux_v[h] = jnp.concatenate([lse, delta, jnp.zeros((6, ROWS), F32)], axis=0)
    for dy in Y_ORDER:
        for dz in range(2):
            for dc in range(2):
                ty, tz, tc = (y + dy) % NY, (z + dz) % 2, (c + dc) % 2
                head = 2 * (2 * ty + tz) + tc
                src = aux_v.at[head]
                dst = aux_ref.at[z * 8 + 2 * y + c]
                at = ((dy * 2 + dz) * 2 + dc) * 3 + 2
                if (dy, dz, dc) == (0, 0, 0):
                    copy = pltpu.make_async_copy(src, dst, q_recv.at[at])
                else:
                    copy = remote(src, dst, q_send.at[at], q_recv.at[at], device(x, tz, ty, tc))
                    sends.append(copy)
                copy.start()
                q_copies.append(copy)

    second = {}
    for dy in Y_ORDER:
        for way, (plane, to) in enumerate((((x + 3) % NX, right), ((x + 1) % NX, left))):
            first[way, dy].wait_recv()
            rows = kv_block(plane, dy)
            at = way * NY + dy
            part = kv_ref.at[rows, pl.ds(way * HD, HD)]
            copy = remote(part, part, x2_send.at[at], x2_recv.at[at], to)
            copy.start()
            sends.append(copy)
            second[way, dy] = copy
            sib.append(to_sibling(1 + way, dy, rows))
    for dy in Y_ORDER:
        second[0, dy].wait_recv()
        second[1, dy].wait_recv()
        sib.append(to_sibling(3, dy, kv_block((x + 2) % NX, dy)))
    for index, copy in enumerate(q_copies):
        if index < 2 or index == 32:
            copy.wait()
        else:
            copy.wait_recv()
    for copy in sib:
        copy.wait_recv()
    for copy in sends:
        copy.wait_send()


def gather(q, k, v, o, g, lse):
    hbm = pl.BlockSpec(memory_space=pl.ANY)
    dma = pltpu.SemaphoreType.DMA
    return pl.pallas_call(
        gather_kernel,
        out_shape=(
            jax.ShapeDtypeStruct((2048, HD), BF16),
            jax.ShapeDtypeStruct((2048, HD), BF16),
            jax.ShapeDtypeStruct((8192, 2 * HD), BF16),
            jax.ShapeDtypeStruct((16, 8, ROWS), F32),
        ),
        in_specs=[hbm] * 5 + [pl.BlockSpec(memory_space=pltpu.VMEM)],
        out_specs=(hbm,) * 4,
        scratch_shapes=[
            pltpu.VMEM((ROWS, 2048), BF16),
            pltpu.VMEM((ROWS, 2048), BF16),
            pltpu.VMEM((16, 8, ROWS), F32),
            dma((2,)),
            dma((16,)), dma((16,)),
            dma((8,)), dma((8,)),
            dma((8,)), dma((8,)),
            dma((16,)), dma((16,)),
            dma((48,)), dma((48,)),
        ],
        compiler_params=pltpu.CompilerParams(collective_id=0, has_side_effects=True, vmem_limit_bytes=32 << 20),
        name="gather_heads",
    )(q, k, v, o, g, lse)


def nt(a, b):
    return lax.dot_general(a, b, (((1,), (1,)), ((), ())), preferred_element_type=F32)


def tn(a, b):
    return lax.dot_general(a, b, (((0,), (0,)), ((), ())), preferred_element_type=F32)


def tile_kernel(
    order_ref, lens_ref, q_ref, g_ref, kv_ref, aux_ref,
    dq_ref, dkv_ref,
    acc_q, acc_kv, rows_f, rows_i,
):
    x = lax.axis_index("pb") // 2
    starts = [lens_ref[0], lens_ref[0] + lens_ref[1], lens_ref[0] + lens_ref[1] + lens_ref[2]]

    def low_of(p):
        low = jnp.zeros_like(p)
        for start in starts:
            low = jnp.where(p >= start, start, low)
        return low

    acc_q[...] = jnp.zeros_like(acc_q)
    query_block = [order_ref[4 * x + i] for i in range(4)]
    query_low = [low_of(query_block[i] * BLK) for i in range(4)]
    for i in range(4):
        for part in range(2):
            rows_f[i, part : part + 1, :] = jnp.concatenate(
                [aux_ref[4 * i + j, part : part + 1, :] for j in range(4)], axis=1
            )
        pos = query_block[i] * BLK + lax.broadcasted_iota(jnp.int32, (1, BLK), 1)
        rows_i[i, 0:1, :] = pos
        rows_i[i, 1:2, :] = low_of(pos)

    def key_step(slot, _):
        key_block = order_ref[slot]
        key_row = pl.multiple_of(slot * BLK, BLK)
        acc_kv[...] = jnp.zeros_like(acc_kv)
        for i in range(4):
            needed = jnp.logical_and(key_block <= query_block[i], key_block * BLK + (BLK - 1) >= query_low[i])

            @pl.when(needed)
            def _():
                q = q_ref[i * BLK : (i + 1) * BLK, :]
                g = g_ref[i * BLK : (i + 1) * BLK, :]
                lse, delta = rows_f[i, 0:1, :], rows_f[i, 1:2, :]
                qpos, qlow = rows_i[i, 0:1, :], rows_i[i, 1:2, :]
                for sub in range(2):
                    size = BLK // 2
                    off = sub * size
                    k = kv_ref[pl.ds(key_row + off, size), 0:HD]
                    v = kv_ref[pl.ds(key_row + off, size), HD : 2 * HD]
                    kpos = key_block * BLK + off + lax.broadcasted_iota(jnp.int32, (size, BLK), 0)
                    allowed = (kpos <= qpos) & (kpos >= qlow)
                    t = jnp.tanh(nt(k, q) * (score_scale / softcap))
                    p = jnp.where(allowed, jnp.exp2(t * (softcap * log2e) - lse), 0.0)
                    ds = p * (nt(v, g) - delta) * ((1.0 - t * t) * score_scale)
                    ds = ds.astype(BF16)
                    acc_kv[off : off + size, 0:HD] += jnp.dot(ds, q, preferred_element_type=F32)
                    acc_kv[off : off + size, HD : 2 * HD] += jnp.dot(
                        p.astype(BF16), g, preferred_element_type=F32
                    )
                    acc_q[i * BLK : (i + 1) * BLK, :] += tn(ds, k)

        dkv_ref[pl.ds(key_row, BLK), :] = acc_kv[...].astype(BF16)
        return 0

    lax.fori_loop(0, 16, key_step, 0)
    dq_ref[...] = acc_q[...].astype(BF16)


def tiles(order, lens, q, g, kv, aux):
    smem = pl.BlockSpec(memory_space=pltpu.SMEM)
    vmem = pl.BlockSpec(memory_space=pltpu.VMEM)
    return pl.pallas_call(
        tile_kernel,
        out_shape=(
            jax.ShapeDtypeStruct((2048, HD), BF16),
            jax.ShapeDtypeStruct((8192, 2 * HD), BF16),
        ),
        in_specs=[smem, smem] + [vmem] * 4,
        out_specs=(vmem, vmem),
        scratch_shapes=[
            pltpu.VMEM((2048, HD), F32),
            pltpu.VMEM((BLK, 2 * HD), F32),
            pltpu.VMEM((4, 8, BLK), F32),
            pltpu.VMEM((4, 8, BLK), jnp.int32),
        ],
        compiler_params=pltpu.CompilerParams(vmem_limit_bytes=48 << 20),
        name="tiles",
    )(order, lens, q, g, kv, aux)


def scatter_kernel(
    dq_ref, dkv_ref,
    dq_out, dk_out, dv_out,
    own, sib, send2, land2, send1, land1, fin,
    own_sem, sib_send, sib_recv, s2_send, s2_recv, s1_send, s1_recv, f_send, f_recv, q_send, q_recv,
):
    x, z, y, c = place()
    head = 2 * y + z
    enter(x, z, y, c)
    sibling = device(x, z, y, 1 - c)
    right, left = device((x + 1) % NX, z, y, c), device((x + 3) % NX, z, y, c)
    planes = [(x + 2) % NX, (x + 1) % NX, (x + 3) % NX, x]
    ys = [(y + dy) % NY for dy in (2, 1, 3, 0)]
    sends = []

    own_copies, sib_copies = {}, {}
    for r, plane in enumerate(planes):
        for n, ty in enumerate(ys):
            at = r * NY + n
            copy = remote(
                dkv_ref.at[ty, 1 - c, plane], sib.at[r, n], sib_send.at[at], sib_recv.at[at], sibling
            )
            copy.start()
            sends.append(copy)
            sib_copies[r, n] = copy
            copy = pltpu.make_async_copy(dkv_ref.at[ty, c, plane], own.at[r, n], own_sem.at[at])
            copy.start()
            own_copies[r, n] = copy

    q_copies = []
    for dy in Y_ORDER:
        for dz in range(2):
            for dc in range(2):
                ty, tz, tc = (y + dy) % NY, (z + dz) % 2, (c + dc) % 2
                src = dq_ref.at[rows_at(tz * 1024 + (2 * ty + tc) * ROWS, ROWS), :]
                dst = dq_out.at[:, columns(2 * head + c)]
                at = (dy * 2 + dz) * 2 + dc
                if at == 0:
                    copy = pltpu.make_async_copy(src, dst, q_recv.at[at])
                else:
                    copy = remote(src, dst, q_send.at[at], q_recv.at[at], device(x, tz, ty, tc))
                    sends.append(copy)
                copy.start()
                q_copies.append(copy)

    def arrived(r, n):
        own_copies[r, n].wait()
        sib_copies[r, n].wait_recv()

    def pair_sum(r, n, part):
        cols = pl.ds(part * HD, HD)
        return own[r, n, :, cols].astype(F32) + sib[r, n, :, cols].astype(F32)

    copies2 = {}
    for n in range(NY):
        arrived(0, n)
        for part, to in enumerate((right, left)):
            send2[part, n] = pair_sum(0, n, part).astype(BF16)
            at = part * NY + n
            copy = remote(send2.at[part, n], land2.at[part, n], s2_send.at[at], s2_recv.at[at], to)
            copy.start()
            sends.append(copy)
            copies2[part, n] = copy

    copies1 = {}

    def send_on(way, n, part, to):
        at = (way * 2 + part) * NY + n
        copy = remote(send1.at[way, part, n], land1.at[way, part, n], s1_send.at[at], s1_recv.at[at], to)
        copy.start()
        sends.append(copy)
        copies1[way, part, n] = copy

    for n in range(NY):
        for way, to in enumerate((right, left)):
            arrived(1 + way, n)
            part = 1 - way
            send1[way, part, n] = pair_sum(1 + way, n, part).astype(BF16)
            send_on(way, n, part, to)
    for n in range(NY):
        for way, to in enumerate((right, left)):
            part = way
            copies2[part, n].wait_recv()
            send1[way, part, n] = (pair_sum(1 + way, n, part) + land2[part, n].astype(F32)).astype(BF16)
            send_on(way, n, part, to)

    f_copies = []
    for n in range(NY):
        arrived(3, n)
        for part, out in ((0, dk_out), (1, dv_out)):
            for way in range(2):
                copies1[way, part, n].wait_recv()
            total = pair_sum(3, n, part) + land1[0, part, n].astype(F32) + land1[1, part, n].astype(F32)
            fin[part, n] = total.astype(BF16)
            for dz in range(2):
                tz = (z + dz) % 2
                src = fin.at[part, n, rows_at(tz * ROWS, ROWS), :]
                dst = out.at[:, columns(head)]
                at = (n * 2 + part) * 2 + dz
                if n == NY - 1 and dz == 0:
                    copy = pltpu.make_async_copy(src, dst, f_recv.at[at])
                    copy.start()
                    f_copies.append((True, copy))
                else:
                    copy = remote(src, dst, f_send.at[at], f_recv.at[at], device(x, tz, ys[n], c))
                    copy.start()
                    sends.append(copy)
                    f_copies.append((False, copy))

    for index, copy in enumerate(q_copies):
        if index == 0:
            copy.wait()
        else:
            copy.wait_recv()
    for local, copy in f_copies:
        if local:
            copy.wait()
        else:
            copy.wait_recv()
    for copy in sends:
        copy.wait_send()


def scatter(dq, dkv):
    hbm = pl.BlockSpec(memory_space=pl.ANY)
    dma = pltpu.SemaphoreType.DMA
    return pl.pallas_call(
        scatter_kernel,
        out_shape=(
            jax.ShapeDtypeStruct((ROWS, 2048), BF16),
            jax.ShapeDtypeStruct((ROWS, 1024), BF16),
            jax.ShapeDtypeStruct((ROWS, 1024), BF16),
        ),
        in_specs=[hbm] * 2,
        out_specs=(hbm,) * 3,
        scratch_shapes=[
            pltpu.VMEM((4, NY, 256, 256), BF16),
            pltpu.VMEM((4, NY, 256, 256), BF16),
            pltpu.VMEM((2, NY, 256, HD), BF16),
            pltpu.VMEM((2, NY, 256, HD), BF16),
            pltpu.VMEM((2, 2, NY, 256, HD), BF16),
            pltpu.VMEM((2, 2, NY, 256, HD), BF16),
            pltpu.VMEM((2, NY, 256, HD), BF16),
            dma((16,)),
            dma((16,)), dma((16,)),
            dma((8,)), dma((8,)),
            dma((16,)), dma((16,)),
            dma((16,)), dma((16,)),
            dma((16,)), dma((16,)),
        ],
        compiler_params=pltpu.CompilerParams(collective_id=1, has_side_effects=True, vmem_limit_bytes=32 << 20),
        name="scatter_grads",
    )(dq, dkv)


def body(
    query_states,
    key_states,
    value_states,
    attn_output,
    output_grad,
    logsumexp,
    block_order,
    doc_lengths,
):
    q, g, kv, aux = gather(query_states, key_states, value_states, attn_output, output_grad, logsumexp)
    dq, dkv = tiles(block_order, doc_lengths, q, g, kv, aux)
    return scatter(dq, dkv.reshape(NY, 2, NX, 256, 2 * HD))


def solution(mesh):
    placed = (
        P(("pb", "ka"), "ha"),
        P(("ka", "pb"), "ha"),
        P(("ka", "pb"), "ha"),
        P(("pb", "ka"), "ha"),
        P(("pb", "ka"), "ha"),
        P("ha", ("pb", "ka")),
        P("ha"),
        P("ha"),
    )
    return jax.shard_map(
        body,
        mesh=mesh,
        in_specs=placed,
        out_specs=(P(("pb", "ka"), "ha"), P(("ka", "pb"), "ha"), P(("ka", "pb"), "ha")),
        check_vma=False,
    )
```

```python
from functools import partial
import math

import jax
import jax.numpy as jnp
from jax import lax
from jax.experimental import pallas as pl
from jax.experimental.pallas import tpu as pltpu
from jax.sharding import PartitionSpec as P

HD = 128
BLK = 512
ROWS = 128
NX, NY = 4, 4
VMEM_LIMIT = 60 << 20
BF16 = jnp.bfloat16
F32 = jnp.float32

softcap = 50.0
score_scale = 144.0 ** (-0.5)
log2e = math.log2(math.e)

ORDER = (0, 1, 3, 2)
QT = 256


def place():
    pb, ka = lax.axis_index("pb"), lax.axis_index("ka")
    return pb // 2, pb % 2, ka // 2, ka % 2


def device(x, z, y, c):
    return {"pb": 2 * x + z, "ka": 2 * y + c}


def remote(src, dst, send, recv, to):
    return pltpu.make_async_remote_copy(
        src_ref=src,
        dst_ref=dst,
        send_sem=send,
        recv_sem=recv,
        device_id=to,
        device_id_type=pl.DeviceIdType.MESH,
    )


def enter(x, z, y, c):
    barrier = pltpu.get_barrier_semaphore()
    for dx in range(NX):
        for dz in range(2):
            for dc in range(2):
                if (dx, dz, dc) != (0, 0, 0):
                    to = device((x + dx) % NX, (z + dz) % 2, y, (c + dc) % 2)
                    pl.semaphore_signal(barrier, inc=1, device_id=to, device_id_type=pl.DeviceIdType.MESH)
    for dy in (1, 3):
        to = device(x, z, (y + dy) % NY, c)
        pl.semaphore_signal(barrier, inc=1, device_id=to, device_id_type=pl.DeviceIdType.MESH)
    pl.semaphore_wait(barrier, 17)


def columns(head):
    return pl.ds(pl.multiple_of(head * HD, HD), HD)


def rows_at(start, count):
    return pl.ds(pl.multiple_of(start, ROWS), count)


def gather_kernel(
    q_ref, k_ref, v_ref, o_ref, g_ref, lse_ref,
    qh_ref, gh_ref, qt_ref, gt_ref, lb_ref, db_ref, kv_ref,
    o_v, g_v, aux_v, qh_v, gh_v, auxh_v, qt_v, gt_v, lb_v, db_v,
    load_sem, kv_send, kv_recv, y_send, y_recv, y2_send, y2_recv, sib_send, sib_recv, q_send, q_recv, out_sem,
):
    x, z, y, c = place()
    loads = [
        pltpu.make_async_copy(o_ref, o_v, load_sem.at[0]),
        pltpu.make_async_copy(g_ref, g_v, load_sem.at[1]),
    ]
    for load in loads:
        load.start()
    enter(x, z, y, c)

    sibling = device(x, z, y, 1 - c)
    up, down = device(x, z, (y + 1) % NY, c), device(x, z, (y + 3) % NY, c)
    own_rows = rows_at((2 * y + c) * 1024 + (2 * x + z) * ROWS, ROWS)
    sends = []

    kv_copies = {}
    for dx in ORDER:
        for dz in range(2):
            tx, tz = (x + dx) % NX, (z + dz) % 2
            for part, ref in enumerate((k_ref, v_ref)):
                src = ref.at[:, columns(2 * tx + tz)]
                dst = kv_ref.at[own_rows, pl.ds(part * HD, HD)]
                at = (dx * 2 + dz) * 2 + part
                if dx == 0 and dz == 0:
                    copy = pltpu.make_async_copy(src, dst, kv_recv.at[at])
                else:
                    copy = remote(src, dst, kv_send.at[at], kv_recv.at[at], device(tx, tz, y, c))
                    sends.append(copy)
                copy.start()
                kv_copies[dx, dz, part] = copy

    def kv_block(plane, dx):
        return rows_at((2 * plane + c) * 1024 + ((x + NX - dx) % NX) * 2 * ROWS, 2 * ROWS)

    def to_sibling(step, dx, rows):
        at = step * NX + dx
        copy = remote(kv_ref.at[rows, :], kv_ref.at[rows, :], sib_send.at[at], sib_recv.at[at], sibling)
        copy.start()
        sends.append(copy)
        return copy

    def each_target(dx):
        for dz in range(2):
            for dc in range(2):
                tx, tz, tc = (x + dx) % NX, (z + dz) % 2, (c + dc) % 2
                yield (dx * 2 + dz) * 2 + dc, 2 * (2 * tx + tz) + tc, device(tx, tz, y, tc)

    first, sib, q_copies, q_local = {}, [], [], []

    def head_copy(src, dst, at, sem, to):
        if at == 0:
            copy = pltpu.make_async_copy(src, dst, q_recv.at[sem])
            q_local.append(copy)
        else:
            copy = remote(src, dst, q_send.at[sem], q_recv.at[sem], to)
            sends.append(copy)
            q_copies.append(copy)
        copy.start()

    for dx in ORDER:
        for dz in range(2):
            for part in range(2):
                copy = kv_copies[dx, dz, part]
                if dx == 0 and dz == 0:
                    copy.wait()
                else:
                    copy.wait_recv()
        rows = kv_block(y, dx)
        for way, to in ((0, up), (1, down)):
            at = way * NX + dx
            copy = remote(kv_ref.at[rows, :], kv_ref.at[rows, :], y_send.at[at], y_recv.at[at], to)
            copy.start()
            sends.append(copy)
            first[way, dx] = copy
        sib.append(to_sibling(0, dx, rows))
        for at, head, to in each_target(dx):
            for part, (ref, out) in enumerate(((q_ref, qh_v), (g_ref, gh_v))):
                src = ref.at[:, columns(head)]
                dst = out.at[2 * x + z, rows_at(c * ROWS, ROWS), :]
                head_copy(src, dst, at, at * 3 + part, to)

    for load in loads:
        load.wait()
    for h in range(16):
        cols = pl.ds(h * HD, HD)
        prod = g_v[:, cols].astype(F32) * o_v[:, cols].astype(F32)
        delta = jnp.sum(prod.T, axis=0, keepdims=True)
        lse = lse_ref[h : h + 1, :] * log2e
        aux_v[h] = jnp.concatenate([lse, delta, jnp.zeros((6, ROWS), F32)], axis=0)
    for dx in ORDER:
        for at, head, to in each_target(dx):
            head_copy(aux_v.at[head], auxh_v.at[2 * (2 * x + z) + c], at, at * 3 + 2, to)

    second = {}
    for dx in ORDER:
        for way, (plane, to) in enumerate((((y + 3) % NY, up), ((y + 1) % NY, down))):
            first[way, dx].wait_recv()
            rows = kv_block(plane, dx)
            at = way * NX + dx
            part = kv_ref.at[rows, pl.ds(way * HD, HD)]
            copy = remote(part, part, y2_send.at[at], y2_recv.at[at], to)
            copy.start()
            sends.append(copy)
            second[way, dx] = copy
            sib.append(to_sibling(1 + way, dx, rows))

    for copy in q_local:
        copy.wait()
    for copy in q_copies:
        copy.wait_recv()
    outs = [
        pltpu.make_async_copy(qh_v, qh_ref, out_sem.at[0]),
        pltpu.make_async_copy(gh_v, gh_ref, out_sem.at[1]),
    ]
    for i in range(8):
        qt_v[i] = qh_v[i].T
        gt_v[i] = gh_v[i].T
    for i in range(16):
        for row, out in ((0, lb_v), (1, db_v)):
            out[i] = jnp.broadcast_to(auxh_v[i, row : row + 1, :], (ROWS, ROWS)).T
    outs += [
        pltpu.make_async_copy(qt_v, qt_ref, out_sem.at[2]),
        pltpu.make_async_copy(gt_v, gt_ref, out_sem.at[3]),
        pltpu.make_async_copy(lb_v, lb_ref, out_sem.at[4]),
        pltpu.make_async_copy(db_v, db_ref, out_sem.at[5]),
    ]
    for copy in outs:
        copy.start()

    for dx in ORDER:
        second[0, dx].wait_recv()
        second[1, dx].wait_recv()
        sib.append(to_sibling(3, dx, kv_block((y + 2) % NY, dx)))
    for copy in sib:
        copy.wait_recv()
    for copy in sends:
        copy.wait_send()
    for copy in outs:
        copy.wait()


def gather(q, k, v, o, g, lse):
    hbm = pl.BlockSpec(memory_space=pl.ANY)
    dma = pltpu.SemaphoreType.DMA
    half = jax.ShapeDtypeStruct((8, QT, HD), BF16)
    turned = jax.ShapeDtypeStruct((8, HD, QT), BF16)
    spread = jax.ShapeDtypeStruct((16, ROWS, ROWS), F32)
    return pl.pallas_call(
        gather_kernel,
        out_shape=(half, half, turned, turned, spread, spread, jax.ShapeDtypeStruct((8192, 2 * HD), BF16)),
        in_specs=[hbm] * 5 + [pl.BlockSpec(memory_space=pltpu.VMEM)],
        out_specs=(hbm,) * 7,
        scratch_shapes=[
            pltpu.VMEM((ROWS, 2048), BF16),
            pltpu.VMEM((ROWS, 2048), BF16),
            pltpu.VMEM((16, 8, ROWS), F32),
            pltpu.VMEM((8, QT, HD), BF16),
            pltpu.VMEM((8, QT, HD), BF16),
            pltpu.VMEM((16, 8, ROWS), F32),
            pltpu.VMEM((8, HD, QT), BF16),
            pltpu.VMEM((8, HD, QT), BF16),
            pltpu.VMEM((16, ROWS, ROWS), F32),
            pltpu.VMEM((16, ROWS, ROWS), F32),
            dma((2,)),
            dma((16,)), dma((16,)),
            dma((8,)), dma((8,)),
            dma((8,)), dma((8,)),
            dma((16,)), dma((16,)),
            dma((48,)), dma((48,)),
            dma((6,)),
        ],
        compiler_params=pltpu.CompilerParams(collective_id=0, has_side_effects=True, vmem_limit_bytes=VMEM_LIMIT),
        name="gather_heads",
    )(q, k, v, o, g, lse)


def nt(a, b):
    return lax.dot_general(a, b, (((1,), (1,)), ((), ())), preferred_element_type=F32)


def nn(a, b):
    return jnp.dot(a, b, preferred_element_type=F32)


def tile_kernel(
    order_ref, lens_ref, qh_ref, gh_ref, qt_ref, gt_ref, lb_ref, db_ref, kv_ref,
    dq_ref, dkv_ref,
    q_v, g_v, qt_v, gt_v, lb_v, db_v, kv_v, acc_q, acc_k, acc_v, dq_v, dkv_v,
    s_a, s_b, dp_a, dp_b, p_a, p_b, ds_a, ds_b, tile_q, tile_k, tile_at, tile_cut, sems,
):
    y = lax.axis_index("ka") // 2
    loads = [
        pltpu.make_async_copy(src, dst, sems.at[n])
        for n, (src, dst) in enumerate(
            ((qh_ref, q_v), (gh_ref, g_v), (kv_ref, kv_v), (lb_ref, lb_v), (db_ref, db_v), (qt_ref, qt_v), (gt_ref, gt_v))
        )
    ]
    for load in loads:
        load.start()
    starts = [lens_ref[0], lens_ref[0] + lens_ref[1], lens_ref[0] + lens_ref[1] + lens_ref[2]]

    def low_of(p):
        low = jnp.zeros_like(p)
        for start in starts:
            low = jnp.where(p >= start, start, low)
        return low

    base = [order_ref[2 * i + y // 2] * BLK + (y % 2) * QT for i in range(8)]
    first_low = [low_of(base[i]) for i in range(8)]
    last_low = [low_of(base[i] + (QT - 1)) for i in range(8)]

    def list_slot(slot, count):
        key = order_ref[slot] * BLK
        for i in range(8):
            needed = jnp.logical_and(key < base[i] + QT, key + BLK > first_low[i])
            whole = jnp.logical_and(key + BLK <= base[i] + 1, key >= last_low[i])
            tile_q[count] = i
            tile_k[count] = slot
            tile_at[count] = key - base[i]
            tile_cut[count] = jnp.where(whole, 0, 1)
            count = count + needed.astype(jnp.int32)
        return count

    count = lax.fori_loop(0, 16, list_slot, 0)
    tile_q[count] = 0
    tile_k[count] = 0
    tile_at[count] = 1 << 20
    tile_cut[count] = 1
    pairs = (count + 1) // 2
    last = 2 * pairs - 1

    acc_q[...] = jnp.zeros_like(acc_q)

    def clear(slot, _):
        acc_k[slot] = jnp.zeros((HD, BLK), F32)
        acc_v[slot] = jnp.zeros((HD, BLK), F32)
        return 0

    lax.fori_loop(0, 16, clear, 0)
    for load in loads:
        load.wait()

    def scores(t, s_ref, dp_ref):
        i, rows = tile_q[t], pl.ds(pl.multiple_of(tile_k[t] * BLK, BLK), BLK)
        s_ref[...] = nt(q_v[i], kv_v[rows, 0:HD])
        dp_ref[...] = nt(g_v[i], kv_v[rows, HD : 2 * HD])

    def weigh(t, s_ref, dp_ref, p_ref, ds_ref, cut):
        i, at = tile_q[t], tile_at[t]
        if cut:
            query_base = order_ref[2 * i + y // 2] * BLK + (y % 2) * QT
        step = 16
        for r in range(0, QT, step):
            j, rr = r // ROWS, r % ROWS
            lse = lb_v[2 * i + j, rr : rr + step, :]
            delta = db_v[2 * i + j, rr : rr + step, :]
            lse = jnp.concatenate([lse] * (BLK // HD), axis=1)
            delta = jnp.concatenate([delta] * (BLK // HD), axis=1)
            th = jnp.tanh(s_ref[r : r + step, :] * (score_scale / softcap))
            p = jnp.exp2(th * (softcap * log2e) - lse)
            if cut:
                row = lax.broadcasted_iota(jnp.int32, (step, HD), 0) + r
                low = low_of(row + query_base) - query_base
                row = jnp.concatenate([row] * (BLK // HD), axis=1)
                low = jnp.concatenate([low] * (BLK // HD), axis=1)
                key = lax.broadcasted_iota(jnp.int32, (step, BLK), 1) + at
                p = jnp.where((key <= row) & (key >= low), p, 0.0)
            ds = p * (dp_ref[r : r + step, :] - delta) * ((1.0 - th * th) * score_scale)
            p_ref[r : r + step, :] = p.astype(BF16)
            ds_ref[r : r + step, :] = ds.astype(BF16)

    def gradients(t, p_ref, ds_ref):
        i, slot = tile_q[t], tile_k[t]
        rows = pl.ds(pl.multiple_of(slot * BLK, BLK), BLK)
        acc_v[slot] += nn(gt_v[i], p_ref[...])
        acc_k[slot] += nn(qt_v[i], ds_ref[...])
        acc_q[i] += nn(ds_ref[...], kv_v[rows, 0:HD])

    buffers = ((s_a, dp_a, p_a, ds_a), (s_b, dp_b, p_b, ds_b))

    def step(t, parity):
        s0, dp0, p0, ds0 = buffers[parity]
        s1, dp1, p1, ds1 = buffers[1 - parity]
        middle = jnp.minimum(t + 1, last)

        def whole_step(cut):
            gradients(t, p0, ds0)
            scores(jnp.minimum(t + 2, last), s0, dp0)
            weigh(middle, s1, dp1, p1, ds1, cut)

        pl.when(tile_cut[middle] == 0)(lambda: whole_step(False))
        pl.when(tile_cut[middle] != 0)(lambda: whole_step(True))

    scores(0, s_a, dp_a)
    scores(1, s_b, dp_b)
    weigh(0, s_a, dp_a, p_a, ds_a, True)

    def pair(n, _):
        step(2 * n, 0)
        step(2 * n + 1, 1)
        return 0

    lax.fori_loop(0, pairs, pair, 0)

    dq_v[...] = acc_q[...].astype(BF16)
    out_q = pltpu.make_async_copy(dq_v, dq_ref, sems.at[0])
    out_q.start()

    def finish(slot, _):
        for half in range(2):
            cols = slice(half * QT, (half + 1) * QT)
            dkv_v[2 * slot + half, 0] = acc_k[slot, :, cols].astype(BF16)
            dkv_v[2 * slot + half, 1] = acc_v[slot, :, cols].astype(BF16)
        return 0

    lax.fori_loop(0, 16, finish, 0)
    out_kv = pltpu.make_async_copy(dkv_v, dkv_ref, sems.at[1])
    out_kv.start()
    out_q.wait()
    out_kv.wait()


def tiles(order, lens, *arrays):
    smem = pl.BlockSpec(memory_space=pltpu.SMEM)
    hbm = pl.BlockSpec(memory_space=pl.ANY)
    wide = pltpu.VMEM((QT, BLK), F32)
    narrow = pltpu.VMEM((QT, BLK), BF16)
    listed = pltpu.SMEM((136,), jnp.int32)
    return pl.pallas_call(
        tile_kernel,
        out_shape=(
            jax.ShapeDtypeStruct((8, QT, HD), BF16),
            jax.ShapeDtypeStruct((32, 2, HD, QT), BF16),
        ),
        in_specs=[smem, smem] + [hbm] * 7,
        out_specs=(hbm, hbm),
        scratch_shapes=[
            pltpu.VMEM((8, QT, HD), BF16),
            pltpu.VMEM((8, QT, HD), BF16),
            pltpu.VMEM((8, HD, QT), BF16),
            pltpu.VMEM((8, HD, QT), BF16),
            pltpu.VMEM((16, ROWS, ROWS), F32),
            pltpu.VMEM((16, ROWS, ROWS), F32),
            pltpu.VMEM((8192, 2 * HD), BF16),
            pltpu.VMEM((8, QT, HD), F32),
            pltpu.VMEM((16, HD, BLK), F32),
            pltpu.VMEM((16, HD, BLK), F32),
            pltpu.VMEM((8, QT, HD), BF16),
            pltpu.VMEM((32, 2, HD, QT), BF16),
            wide, wide, wide, wide,
            narrow, narrow, narrow, narrow,
            listed, listed, listed, listed,
            pltpu.SemaphoreType.DMA((7,)),
        ],
        compiler_params=pltpu.CompilerParams(vmem_limit_bytes=VMEM_LIMIT),
        name="tiles",
    )(order, lens, *arrays)


def scatter_kernel(
    dq_ref, dkv_ref,
    dq_out, dk_out, dv_out,
    own, sib, send2, land2, send1, land1, fin,
    own_sem, sib_send, sib_recv, s2_send, s2_recv, s1_send, s1_recv, f_send, f_recv, q_send, q_recv,
):
    x, z, y, c = place()
    head = 2 * x + z
    enter(x, z, y, c)
    sibling = device(x, z, y, 1 - c)
    up, down = device(x, z, (y + 1) % NY, c), device(x, z, (y + 3) % NY, c)
    planes = [(y + 2) % NY, (y + 1) % NY, (y + 3) % NY, y]
    xs = [(x + dx) % NX for dx in (2, 1, 3, 0)]
    sends = []

    own_copies, sib_copies = {}, {}
    for r, plane in enumerate(planes):
        for n, tx in enumerate(xs):
            at = r * NX + n
            copy = remote(
                dkv_ref.at[plane, 1 - c, tx], sib.at[r, n], sib_send.at[at], sib_recv.at[at], sibling
            )
            copy.start()
            sends.append(copy)
            sib_copies[r, n] = copy
            copy = pltpu.make_async_copy(dkv_ref.at[plane, c, tx], own.at[r, n], own_sem.at[at])
            copy.start()
            own_copies[r, n] = copy

    q_copies = []
    for dx in ORDER:
        for dz in range(2):
            for dc in range(2):
                tx, tz, tc = (x + dx) % NX, (z + dz) % 2, (c + dc) % 2
                src = dq_ref.at[2 * tx + tz, rows_at(tc * ROWS, ROWS), :]
                dst = dq_out.at[:, columns(2 * head + c)]
                at = (dx * 2 + dz) * 2 + dc
                if at == 0:
                    copy = pltpu.make_async_copy(src, dst, q_recv.at[at])
                else:
                    copy = remote(src, dst, q_send.at[at], q_recv.at[at], device(tx, tz, y, tc))
                    sends.append(copy)
                copy.start()
                q_copies.append(copy)

    def arrived(r, n):
        own_copies[r, n].wait()
        sib_copies[r, n].wait_recv()

    def pair_sum(r, n, part):
        return own[r, n, part].astype(F32) + sib[r, n, part].astype(F32)

    copies2 = {}
    for n in range(NX):
        arrived(0, n)
        for part, to in enumerate((up, down)):
            send2[part, n] = pair_sum(0, n, part).astype(BF16)
            at = part * NX + n
            copy = remote(send2.at[part, n], land2.at[part, n], s2_send.at[at], s2_recv.at[at], to)
            copy.start()
            sends.append(copy)
            copies2[part, n] = copy

    copies1 = {}

    def send_on(way, n, part, to):
        at = (way * 2 + part) * NX + n
        copy = remote(send1.at[way, part, n], land1.at[way, part, n], s1_send.at[at], s1_recv.at[at], to)
        copy.start()
        sends.append(copy)
        copies1[way, part, n] = copy

    for n in range(NX):
        for way, to in enumerate((up, down)):
            arrived(1 + way, n)
            part = 1 - way
            send1[way, part, n] = pair_sum(1 + way, n, part).astype(BF16)
            send_on(way, n, part, to)
    for n in range(NX):
        for way, to in enumerate((up, down)):
            part = way
            copies2[part, n].wait_recv()
            send1[way, part, n] = (pair_sum(1 + way, n, part) + land2[part, n].astype(F32)).astype(BF16)
            send_on(way, n, part, to)

    f_copies = []
    for n in range(NX):
        arrived(3, n)
        for part, out in ((0, dk_out), (1, dv_out)):
            for way in range(2):
                copies1[way, part, n].wait_recv()
            total = pair_sum(3, n, part) + land1[0, part, n].astype(F32) + land1[1, part, n].astype(F32)
            fin[part, n] = total.T.astype(BF16)
            for dz in range(2):
                tz = (z + dz) % 2
                src = fin.at[part, n, rows_at(tz * ROWS, ROWS), :]
                dst = out.at[:, columns(head)]
                at = (n * 2 + part) * 2 + dz
                if n == NX - 1 and dz == 0:
                    copy = pltpu.make_async_copy(src, dst, f_recv.at[at])
                    copy.start()
                    f_copies.append((True, copy))
                else:
                    copy = remote(src, dst, f_send.at[at], f_recv.at[at], device(xs[n], tz, y, c))
                    copy.start()
                    sends.append(copy)
                    f_copies.append((False, copy))

    for index, copy in enumerate(q_copies):
        if index == 0:
            copy.wait()
        else:
            copy.wait_recv()
    for local, copy in f_copies:
        if local:
            copy.wait()
        else:
            copy.wait_recv()
    for copy in sends:
        copy.wait_send()


def scatter(dq, dkv):
    hbm = pl.BlockSpec(memory_space=pl.ANY)
    dma = pltpu.SemaphoreType.DMA
    return pl.pallas_call(
        scatter_kernel,
        out_shape=(
            jax.ShapeDtypeStruct((ROWS, 2048), BF16),
            jax.ShapeDtypeStruct((ROWS, 1024), BF16),
            jax.ShapeDtypeStruct((ROWS, 1024), BF16),
        ),
        in_specs=[hbm] * 2,
        out_specs=(hbm,) * 3,
        scratch_shapes=[
            pltpu.VMEM((4, NX, 2, HD, QT), BF16),
            pltpu.VMEM((4, NX, 2, HD, QT), BF16),
            pltpu.VMEM((2, NX, HD, QT), BF16),
            pltpu.VMEM((2, NX, HD, QT), BF16),
            pltpu.VMEM((2, 2, NX, HD, QT), BF16),
            pltpu.VMEM((2, 2, NX, HD, QT), BF16),
            pltpu.VMEM((2, NX, QT, HD), BF16),
            dma((16,)),
            dma((16,)), dma((16,)),
            dma((8,)), dma((8,)),
            dma((16,)), dma((16,)),
            dma((16,)), dma((16,)),
            dma((16,)), dma((16,)),
        ],
        compiler_params=pltpu.CompilerParams(collective_id=1, has_side_effects=True, vmem_limit_bytes=VMEM_LIMIT),
        name="scatter_grads",
    )(dq, dkv)


def body(
    query_states,
    key_states,
    value_states,
    attn_output,
    output_grad,
    logsumexp,
    block_order,
    doc_lengths,
):
    arrays = gather(query_states, key_states, value_states, attn_output, output_grad, logsumexp)
    dq, dkv = tiles(block_order, doc_lengths, *arrays)
    return scatter(dq, dkv.reshape(NY, 2, NX, 2, HD, QT))


def solution(mesh):
    placed = (
        P(("pb", "ka"), "ha"),
        P(("ka", "pb"), "ha"),
        P(("ka", "pb"), "ha"),
        P(("pb", "ka"), "ha"),
        P(("pb", "ka"), "ha"),
        P("ha", ("pb", "ka")),
        P("ha"),
        P("ha"),
    )
    return jax.shard_map(
        body,
        mesh=mesh,
        in_specs=placed,
        out_specs=(P(("pb", "ka"), "ha"), P(("ka", "pb"), "ha"), P(("ka", "pb"), "ha")),
        check_vma=False,
    )
```

```python
from functools import partial
import math

import jax
import jax.numpy as jnp
from jax import lax
from jax.experimental import pallas as pl
from jax.experimental.pallas import tpu as pltpu
from jax.sharding import PartitionSpec as P

HD = 128
BLK = 512
ROWS = 128
NX, NY = 4, 4
VMEM_LIMIT = 60 << 20
BF16 = jnp.bfloat16
F32 = jnp.float32

softcap = 50.0
score_scale = 144.0 ** (-0.5)
log2e = math.log2(math.e)

ORDER = (0, 1, 3, 2)
CHUNKS = ((0, 0), (0, 1), (1, 0), (3, 0), (1, 1), (3, 1), (2, 0), (2, 1))
QT = 256
KT = 256
STEP = 32


def place():
    pb, ka = lax.axis_index("pb"), lax.axis_index("ka")
    return pb // 2, pb % 2, ka // 2, ka % 2


def device(x, z, y, c):
    return {"pb": 2 * x + z, "ka": 2 * y + c}


def remote(src, dst, send, recv, to):
    return pltpu.make_async_remote_copy(
        src_ref=src,
        dst_ref=dst,
        send_sem=send,
        recv_sem=recv,
        device_id=to,
        device_id_type=pl.DeviceIdType.MESH,
    )


def enter(x, z, y, c):
    barrier = pltpu.get_barrier_semaphore()
    for dx in range(NX):
        for dz in range(2):
            for dc in range(2):
                if (dx, dz, dc) != (0, 0, 0):
                    to = device((x + dx) % NX, (z + dz) % 2, y, (c + dc) % 2)
                    pl.semaphore_signal(barrier, inc=1, device_id=to, device_id_type=pl.DeviceIdType.MESH)
    for dy in (1, 3):
        to = device(x, z, (y + dy) % NY, c)
        pl.semaphore_signal(barrier, inc=1, device_id=to, device_id_type=pl.DeviceIdType.MESH)
    pl.semaphore_wait(barrier, 17)


def columns(head, count=1):
    return pl.ds(pl.multiple_of(head * HD, HD), count * HD)


def rows_at(start, count):
    return pl.ds(pl.multiple_of(start, ROWS), count)


def gather_kernel(
    q_ref, k_ref, v_ref, o_ref, g_ref, lse_ref,
    q2_ref, g2_ref, qt_ref, gt_ref, lb_ref, db_ref, kv_ref,
    o_v, g_v, aux_v, qh_v, gh_v, auxh_v, q2_v, g2_v, qt_v, gt_v, lb_v, db_v,
    load_sem, kv_send, kv_recv, y_send, y_recv, y2_send, y2_recv, q_send, q_recv, s_send, s_recv,
    a_send, a_recv, out_sem,
):
    x, z, y, c = place()
    loads = [
        pltpu.make_async_copy(o_ref, o_v, load_sem.at[0]),
        pltpu.make_async_copy(g_ref, g_v, load_sem.at[1]),
    ]
    for load in loads:
        load.start()
    enter(x, z, y, c)

    sibling = device(x, z, y, 1 - c)
    up, down = device(x, z, (y + 1) % NY, c), device(x, z, (y + 3) % NY, c)
    sends = []

    def send(src, dst, send_sem, recv_sem, to):
        copy = remote(src, dst, send_sem, recv_sem, to)
        copy.start()
        sends.append(copy)
        return copy

    def keep(src, dst, sem):
        copy = pltpu.make_async_copy(src, dst, sem)
        copy.start()
        return copy

    kv_copies = {}
    for dx in ORDER:
        for dz in range(2):
            tx, tz = (x + dx) % NX, (z + dz) % 2
            for part, ref in enumerate((k_ref, v_ref)):
                src = ref.at[:, columns(2 * tx + tz)]
                dst = kv_ref.at[y, c, x // 2, rows_at(z * ROWS, ROWS), pl.ds(part * HD, HD)]
                at = (dx * 2 + dz) * 2 + part
                if at < 2:
                    kv_copies[dx, dz, part] = keep(src, dst, kv_recv.at[at])
                else:
                    to = device(tx, tz, y, (c + dx) % 2)
                    kv_copies[dx, dz, part] = send(src, dst, kv_send.at[at], kv_recv.at[at], to)

    def block(plane, dx):
        return plane, (c + dx) % 2, ((x + NX - dx) % NX) // 2

    first, q_copies = {}, {}
    for dx in ORDER:
        for dz in range(2):
            for part in range(2):
                copy = kv_copies[dx, dz, part]
                if dx == 0 and dz == 0:
                    copy.wait()
                else:
                    copy.wait_recv()
        rows = kv_ref.at[block(y, dx)]
        for way, to in ((0, up), (1, down)):
            at = way * NX + dx
            first[way, dx] = send(rows, rows, y_send.at[at], y_recv.at[at], to)
        for j, (jx, jz) in enumerate(CHUNKS):
            if jx != dx:
                continue
            tx, tz = (x + jx) % NX, (z + jz) % 2
            for kind, (ref, out) in enumerate(((q_ref, qh_v), (g_ref, gh_v))):
                src = ref.at[:, columns(2 * (2 * tx + tz), 2)]
                dst = out.at[2 * x + z, rows_at(c * ROWS, ROWS), :]
                at = 2 * j + kind
                if j == 0:
                    q_copies[j, kind] = keep(src, dst, q_recv.at[at])
                else:
                    q_copies[j, kind] = send(src, dst, q_send.at[at], q_recv.at[at], device(tx, tz, y, c))

    for load in loads:
        load.wait()
    for h in range(8):
        rows = [lse_ref[2 * h : 2 * h + 2, :] * log2e]
        for n in range(2):
            cols = pl.ds((2 * h + n) * HD, HD)
            prod = g_v[:, cols].astype(F32) * o_v[:, cols].astype(F32)
            rows.append(jnp.sum(prod.T, axis=0, keepdims=True))
        aux_v[h] = jnp.concatenate(rows + [jnp.zeros((4, ROWS), F32)], axis=0)
    a_copies = []
    for j, (dx, dz) in enumerate(CHUNKS):
        tx, tz = (x + dx) % NX, (z + dz) % 2
        for dc in range(2):
            src, dst, at = aux_v.at[2 * tx + tz], auxh_v.at[2 * (2 * x + z) + c], 2 * j + dc
            if at == 0:
                a_copies.append(keep(src, dst, a_recv.at[at]))
            else:
                a_copies.append(send(src, dst, a_send.at[at], a_recv.at[at], device(tx, tz, y, (c + dc) % 2)))

    second = {}
    for dx in ORDER:
        for way, (plane, to) in enumerate((((y + 3) % NY, up), ((y + 1) % NY, down))):
            first[way, dx].wait_recv()
            at = way * NX + dx
            half = kv_ref.at[block(plane, dx)].at[:, pl.ds(way * HD, HD)]
            second[way, dx] = send(half, half, y2_send.at[at], y2_recv.at[at], to)

    for n, copy in enumerate(a_copies):
        if n == 0:
            copy.wait()
        else:
            copy.wait_recv()
    outs, passed = [], {}
    for j in range(len(CHUNKS) + 1):
        if j < len(CHUNKS):
            dx, dz = CHUNKS[j]
            i = 2 * ((x + NX - dx) % NX) + (z + 2 - dz) % 2
            for kind, out in enumerate((qh_v, gh_v)):
                if j == 0:
                    q_copies[j, kind].wait()
                else:
                    q_copies[j, kind].wait_recv()
                rows = out.at[i, rows_at(c * ROWS, ROWS), :]
                at = 2 * j + kind
                passed[j, kind] = send(rows, rows, s_send.at[at], s_recv.at[at], sibling)
        if j > 0:
            dx, dz = CHUNKS[j - 1]
            i = 2 * ((x + NX - dx) % NX) + (z + 2 - dz) % 2
            for kind in range(2):
                passed[j - 1, kind].wait_recv()
            for h in range(2):
                rows = slice(h * QT, (h + 1) * QT)
                for whole, split, turned in ((qh_v, q2_v, qt_v), (gh_v, g2_v, gt_v)):
                    part = whole[i, :, h * HD : (h + 1) * HD]
                    split[i, rows, :] = part
                    turned[i, :, rows] = part.T
            for n in range(2):
                spread = auxh_v[2 * i + n].T
                for h in range(2):
                    rows = slice(h * QT + n * ROWS, h * QT + (n + 1) * ROWS)
                    lb_v[i, rows, :] = jnp.broadcast_to(spread[:, h : h + 1], (ROWS, HD))
                    db_v[i, rows, :] = jnp.broadcast_to(spread[:, 2 + h : 3 + h], (ROWS, HD))
            for n, (src, dst) in enumerate(
                ((q2_v, q2_ref), (g2_v, g2_ref), (qt_v, qt_ref), (gt_v, gt_ref), (lb_v, lb_ref), (db_v, db_ref))
            ):
                outs.append(keep(src.at[i], dst.at[i], out_sem.at[j - 1, n]))

    for copy in second.values():
        copy.wait_recv()
    for copy in sends:
        copy.wait_send()
    for copy in outs:
        copy.wait()


def gather(q, k, v, o, g, lse):
    hbm = pl.BlockSpec(memory_space=pl.ANY)
    dma = pltpu.SemaphoreType.DMA
    split = (8, 2 * QT, HD)
    turned = (8, HD, 2 * QT)
    return pl.pallas_call(
        gather_kernel,
        out_shape=tuple(
            jax.ShapeDtypeStruct(shape, kind)
            for shape, kind in (
                (split, BF16), (split, BF16), (turned, BF16), (turned, BF16), (split, F32), (split, F32),
                ((NY, 2, 2, KT, 2 * HD), BF16),
            )
        ),
        in_specs=[hbm] * 5 + [pl.BlockSpec(memory_space=pltpu.VMEM)],
        out_specs=(hbm,) * 7,
        scratch_shapes=[
            pltpu.VMEM((ROWS, 2048), BF16),
            pltpu.VMEM((ROWS, 2048), BF16),
            pltpu.VMEM((8, 8, ROWS), F32),
            pltpu.VMEM((8, QT, 2 * HD), BF16),
            pltpu.VMEM((8, QT, 2 * HD), BF16),
            pltpu.VMEM((16, 8, ROWS), F32),
            pltpu.VMEM(split, BF16),
            pltpu.VMEM(split, BF16),
            pltpu.VMEM(turned, BF16),
            pltpu.VMEM(turned, BF16),
            pltpu.VMEM(split, F32),
            pltpu.VMEM(split, F32),
            dma((2,)),
            dma((16,)), dma((16,)),
            dma((8,)), dma((8,)),
            dma((8,)), dma((8,)),
            dma((16,)), dma((16,)),
            dma((16,)), dma((16,)),
            dma((16,)), dma((16,)),
            dma((8, 6)),
        ],
        compiler_params=pltpu.CompilerParams(collective_id=0, has_side_effects=True, vmem_limit_bytes=VMEM_LIMIT),
        name="gather_heads",
    )(q, k, v, o, g, lse)


def nt(a, b):
    return lax.dot_general(a, b, (((1,), (1,)), ((), ())), preferred_element_type=F32)


def nn(a, b):
    return jnp.dot(a, b, preferred_element_type=F32)


def tile_kernel(part, *refs):
    if part == 0:
        (order_ref, lens_ref, q2_ref, g2_ref, qt_ref, gt_ref, lb_ref, db_ref, kv_ref, dq_ref, *dkv_refs), refs = (
            refs[:14], refs[14:],
        )
    else:
        (order_ref, lens_ref, q2_ref, g2_ref, qt_ref, gt_ref, lb_ref, db_ref, kv_ref, old_ref, dq_ref, *dkv_refs), refs = (
            refs[:12], refs[12:],
        )
    (
        q_v, g_v, qt_v, gt_v, lb_v, db_v, kv_v, acc_q, acc_k, acc_v, dq_v, dkv_v,
        s_a, s_b, dp_a, dp_b, p_a, p_b, ds_a, ds_b, tile_q, tile_k, tile_at, tile_cut, sems,
    ) = refs
    x, z, y, c = place()
    core = (c + part) % 2
    loads = [
        pltpu.make_async_copy(src, dst, sems.at[n])
        for n, (src, dst) in enumerate(
            (
                (kv_ref.at[:, core], kv_v), (q2_ref, q_v), (g2_ref, g_v),
                (lb_ref, lb_v), (db_ref, db_v), (qt_ref, qt_v), (gt_ref, gt_v),
            )
        )
    ]
    if part == 1:
        loads.append(pltpu.make_async_copy(old_ref, acc_q, sems.at[7]))
    for load in loads:
        load.start()
    starts = [lens_ref[0], lens_ref[0] + lens_ref[1], lens_ref[0] + lens_ref[1] + lens_ref[2]]

    def low_of(p):
        low = jnp.zeros_like(p)
        for start in starts:
            low = jnp.where(p >= start, start, low)
        return low

    base = [order_ref[2 * i + y // 2] * BLK + (y % 2) * QT for i in range(8)]
    first_low = [low_of(base[i]) for i in range(8)]
    last_low = [low_of(base[i] + (QT - 1)) for i in range(8)]

    def list_slot(slot, count):
        stored = 4 * (slot // 2) + 2 * core + slot % 2
        key = order_ref[stored] * BLK + ((x + c + core) % 2) * KT
        for i in range(8):
            needed = jnp.logical_and(key < base[i] + QT, key + KT > first_low[i])
            whole = jnp.logical_and(key + KT <= base[i] + 1, key >= last_low[i])
            tile_q[count] = i
            tile_k[count] = slot
            tile_at[count] = key - base[i]
            tile_cut[count] = jnp.where(whole, 0, 1)
            count = count + needed.astype(jnp.int32)
        return count

    count = lax.fori_loop(0, 8, list_slot, 0)
    for n in range(2):
        tile_q[count + n] = 0
        tile_k[count + n] = 0
        tile_at[count + n] = 1 << 20
        tile_cut[count + n] = 1
    pairs = (count + 1) // 2
    last = jnp.maximum(2 * pairs - 1, 1)

    for slot in range(8):
        acc_k[slot] = jnp.zeros((HD, KT), F32)
        acc_v[slot] = jnp.zeros((HD, KT), F32)
    if part == 0:

        def clear(i, _):
            acc_q[i] = jnp.zeros((2 * QT, HD), F32)
            return 0

        lax.fori_loop(0, 8, clear, 0)

    def keys(t):
        return kv_v[tile_k[t] // 2, tile_k[t] % 2, :, 0:HD]

    def values(t):
        return kv_v[tile_k[t] // 2, tile_k[t] % 2, :, HD : 2 * HD]

    def scores(t, s_ref, dp_ref):
        i = tile_q[t]

        def piece(out, left, right, h):
            rows = slice(h * QT, (h + 1) * QT)
            out[rows, :] = nt(left[i, rows, :], right(t))

        return [
            partial(piece, out, left, right, h)
            for out, left, right in ((s_ref, q_v, keys), (dp_ref, g_v, values))
            for h in range(2)
        ]

    def weigh(t, s_ref, dp_ref, p_ref, ds_ref, cut):
        i, at = tile_q[t], tile_at[t]
        if cut:
            query_base = order_ref[2 * i + y // 2] * BLK + (y % 2) * QT
        step = STEP

        def piece(r):
            lse = lb_v[i, r : r + step, :]
            delta = db_v[i, r : r + step, :]
            lse = jnp.concatenate([lse] * (KT // HD), axis=1)
            delta = jnp.concatenate([delta] * (KT // HD), axis=1)
            th = jnp.tanh(s_ref[r : r + step, :] * (score_scale / softcap))
            p = jnp.exp2(th * (softcap * log2e) - lse)
            if cut:
                row = lax.broadcasted_iota(jnp.int32, (step, HD), 0) + r % QT
                low = low_of(row + query_base) - query_base
                row = jnp.concatenate([row] * (KT // HD), axis=1)
                low = jnp.concatenate([low] * (KT // HD), axis=1)
                key = lax.broadcasted_iota(jnp.int32, (step, KT), 1) + at
                p = jnp.where((key <= row) & (key >= low), p, 0.0)
            ds = p * (dp_ref[r : r + step, :] - delta) * ((1.0 - th * th) * score_scale)
            p_ref[r : r + step, :] = p.astype(BF16)
            ds_ref[r : r + step, :] = ds.astype(BF16)

        return [partial(piece, r) for r in range(0, 2 * QT, step)]

    def gradients(t, p_ref, ds_ref):
        i, slot = tile_q[t], tile_k[t]

        def key_piece(out, left, right):
            out[slot] += nn(left[i], right[...])

        def query_piece(h):
            rows = slice(h * QT, (h + 1) * QT)
            acc_q[i, rows, :] += nn(ds_ref[rows, :], keys(t))

        return [
            partial(key_piece, acc_v, gt_v, p_ref),
            partial(key_piece, acc_k, qt_v, ds_ref),
            partial(query_piece, 0),
            partial(query_piece, 1),
        ]

    def run(*lists):
        marked = [((n + 0.5) / len(pieces), m, piece) for m, pieces in enumerate(lists) for n, piece in enumerate(pieces)]
        for _, _, piece in sorted(marked, key=lambda entry: entry[:2]):
            piece()

    buffers = ((s_a, dp_a, p_a, ds_a), (s_b, dp_b, p_b, ds_b))

    def step(t, parity):
        s0, dp0, p0, ds0 = buffers[parity]
        s1, dp1, p1, ds1 = buffers[1 - parity]
        middle = jnp.minimum(t + 1, last)

        def whole_step(cut):
            run(
                scores(jnp.minimum(t + 2, last), s0, dp0) + gradients(t, p0, ds0),
                weigh(middle, s1, dp1, p1, ds1, cut),
            )

        pl.when(tile_cut[middle] == 0)(lambda: whole_step(False))
        pl.when(tile_cut[middle] != 0)(lambda: whole_step(True))

    for load in loads[:3]:
        load.wait()
    run(scores(0, s_a, dp_a))
    for load in loads[3:5]:
        load.wait()
    run(scores(1, s_b, dp_b), weigh(0, s_a, dp_a, p_a, ds_a, True))
    for load in loads[5:]:
        load.wait()

    def pair(n, _):
        step(2 * n, 0)
        step(2 * n + 1, 1)
        return 0

    lax.fori_loop(0, pairs, pair, 0)

    outs = []
    if part == 0:
        outs.append(pltpu.make_async_copy(acc_q, dq_ref, sems.at[0]))
        outs[0].start()
    for d in range(NY):
        plane = (y + d) % NY
        for h in range(2):
            dkv_v[d, h, 0] = acc_k[2 * plane + h].astype(BF16)
            dkv_v[d, h, 1] = acc_v[2 * plane + h].astype(BF16)
        out = dkv_refs[d] if part == 0 else dkv_refs[0].at[d]
        outs.append(pltpu.make_async_copy(dkv_v.at[d], out, sems.at[1 + d]))
        outs[-1].start()
    if part == 1:

        def narrow(i, _):
            for h in range(2):
                dq_v[h, i] = acc_q[i, h * QT : (h + 1) * QT, :].astype(BF16)
            return 0

        lax.fori_loop(0, 8, narrow, 0)
        outs.append(pltpu.make_async_copy(dq_v, dq_ref, sems.at[0]))
        outs[-1].start()
    for out in outs:
        out.wait()


def tiles(part, order, lens, arrays, old=()):
    smem = pl.BlockSpec(memory_space=pltpu.SMEM)
    hbm = pl.BlockSpec(memory_space=pl.ANY)
    split = (8, 2 * QT, HD)
    turned = (8, HD, 2 * QT)
    wide = pltpu.VMEM((2 * QT, KT), F32)
    narrow = pltpu.VMEM((2 * QT, KT), BF16)
    listed = pltpu.SMEM((72,), jnp.int32)
    sums = (2, 2, HD, KT)
    if part == 0:
        out_shape = (jax.ShapeDtypeStruct(split, F32),) + (jax.ShapeDtypeStruct(sums, BF16),) * NY
    else:
        out_shape = (jax.ShapeDtypeStruct((2, 8, QT, HD), BF16), jax.ShapeDtypeStruct((NY,) + sums, BF16))
    return pl.pallas_call(
        partial(tile_kernel, part),
        out_shape=out_shape,
        in_specs=[smem, smem] + [hbm] * (len(arrays) + len(old)),
        out_specs=(hbm,) * len(out_shape),
        scratch_shapes=[
            pltpu.VMEM(split, BF16),
            pltpu.VMEM(split, BF16),
            pltpu.VMEM(turned, BF16),
            pltpu.VMEM(turned, BF16),
            pltpu.VMEM(split, F32),
            pltpu.VMEM(split, F32),
            pltpu.VMEM((NY, 2, KT, 2 * HD), BF16),
            pltpu.VMEM(split, F32),
            pltpu.VMEM((8, HD, KT), F32),
            pltpu.VMEM((8, HD, KT), F32),
            pltpu.VMEM((2, 8, QT, HD), BF16),
            pltpu.VMEM((NY,) + sums, BF16),
            wide, wide, wide, wide,
            narrow, narrow, narrow, narrow,
            listed, listed, listed, listed,
            pltpu.SemaphoreType.DMA((8,)),
        ],
        compiler_params=pltpu.CompilerParams(vmem_limit_bytes=VMEM_LIMIT),
        cost_estimate=pl.CostEstimate(flops=6 * 10**9, bytes_accessed=16 << 20, transcendentals=4 << 20),
        name="tiles_a" if part == 0 else "tiles_b",
    )(order, lens, *arrays, *old)


def scatter_kernel(
    dq_ref, dkv_ref, a0_ref, a1_ref, a2_ref, a3_ref,
    dq_out, dk_out, dv_out,
    own, near, land2, send1, land1, fin, mine, theirs, dq_v,
    load_sem, near_sem, mine_sem, sib_send, sib_recv, s2_send, s2_recv, s1_send, s1_recv, f_send, f_recv, q_send, q_recv,
):
    x, z, y, c = place()
    head = 2 * x + z
    loads = [pltpu.make_async_copy(dkv_ref.at[d], own.at[d], load_sem.at[d]) for d in range(NY)]
    near_loads = [
        pltpu.make_async_copy(ref, near.at[n], near_sem.at[n]) for n, ref in enumerate((a0_ref, a1_ref, a2_ref, a3_ref))
    ]
    mine_load = pltpu.make_async_copy(dq_ref.at[c], mine, mine_sem)
    for load in [mine_load] + loads + near_loads:
        load.start()
    enter(x, z, y, c)
    sibling = device(x, z, y, 1 - c)
    ways = (device(x, z, (y + 1) % NY, c), device(x, z, (y + 3) % NY, c))
    sends = []

    def send(src, dst, send_sem, recv_sem, to):
        copy = remote(src, dst, send_sem, recv_sem, to)
        copy.start()
        sends.append(copy)
        return copy

    copies2, copies1 = {}, {}
    for h in range(2):
        for part, to in enumerate(ways):
            at = part * 2 + h
            copies2[part, h] = send(dkv_ref.at[2, h, part], land2.at[part, h], s2_send.at[at], s2_recv.at[at], to)
    sib_copy = send(dq_ref.at[1 - c], theirs, sib_send, sib_recv, sibling)
    for h in range(2):
        for way, to in enumerate(ways):
            part = 1 - way
            at = (way * 2 + part) * 2 + h
            copies1[way, part, h] = send(
                dkv_ref.at[1 + 2 * way, h, part], land1.at[way, part, h], s1_send.at[at], s1_recv.at[at], to
            )

    mine_load.wait()
    sib_copy.wait_recv()
    q_copies = []
    for dx, dz in CHUNKS:
        tx, tz = (x + dx) % NX, (z + dz) % 2
        i = 2 * tx + tz
        dq_v[i] = (mine[i].astype(F32) + theirs[i].astype(F32)).astype(BF16)
        for dc in range(2):
            tc = (c + dc) % 2
            src = dq_v.at[i, rows_at(tc * ROWS, ROWS), :]
            dst = dq_out.at[:, columns(2 * head + c)]
            at = (dx * 2 + dz) * 2 + dc
            if at == 0:
                copy = pltpu.make_async_copy(src, dst, q_recv.at[at])
                copy.start()
                q_copies.append((True, copy))
            else:
                q_copies.append((False, send(src, dst, q_send.at[at], q_recv.at[at], device(tx, tz, y, tc))))

    for load in loads:
        load.wait()
    for h in range(2):
        for way, to in enumerate(ways):
            part = way
            copies2[part, h].wait_recv()
            total = own[1 + 2 * way, h, part].astype(F32) + land2[part, h].astype(F32)
            send1[way, h] = total.astype(BF16)
            at = (way * 2 + part) * 2 + h
            copies1[way, part, h] = send(
                send1.at[way, h], land1.at[way, part, h], s1_send.at[at], s1_recv.at[at], to
            )

    f_copies = []

    def final(dx, part, out, total):
        fin[dx, part] = total.T.astype(BF16)
        for dz in range(2):
            tz = (z + dz) % 2
            src = fin.at[dx, part, rows_at(tz * ROWS, ROWS), :]
            dst = out.at[:, columns(head)]
            at = (dx * 2 + part) * 2 + dz
            if dx == 0 and dz == 0:
                copy = pltpu.make_async_copy(src, dst, f_recv.at[at])
                copy.start()
                f_copies.append((True, copy))
            else:
                to = device((x + dx) % NX, tz, y, (c + dx) % 2)
                f_copies.append((False, send(src, dst, f_send.at[at], f_recv.at[at], to)))

    for load in near_loads:
        load.wait()
    for dx in (2, 0):
        h = ((x + dx) % NX) // 2
        for part, out in ((0, dk_out), (1, dv_out)):
            total = near[0, h, part].astype(F32)
            for n in range(1, 4):
                total = total + near[n, h, part].astype(F32)
            final(dx, part, out, total)
    for h in range(2):
        for way in range(2):
            for part in range(2):
                copies1[way, part, h].wait_recv()
    for dx in (1, 3):
        h = ((x + dx) % NX) // 2
        for part, out in ((0, dk_out), (1, dv_out)):
            total = own[0, h, part].astype(F32) + land1[0, part, h].astype(F32) + land1[1, part, h].astype(F32)
            final(dx, part, out, total)

    for local, copy in q_copies + f_copies:
        if local:
            copy.wait()
        else:
            copy.wait_recv()
    for copy in sends:
        copy.wait_send()


def scatter(*arrays):
    hbm = pl.BlockSpec(memory_space=pl.ANY)
    dma = pltpu.SemaphoreType.DMA
    return pl.pallas_call(
        scatter_kernel,
        out_shape=(
            jax.ShapeDtypeStruct((ROWS, 2048), BF16),
            jax.ShapeDtypeStruct((ROWS, 1024), BF16),
            jax.ShapeDtypeStruct((ROWS, 1024), BF16),
        ),
        in_specs=[hbm] * len(arrays),
        out_specs=(hbm,) * 3,
        scratch_shapes=[
            pltpu.VMEM((NY, 2, 2, HD, KT), BF16),
            pltpu.VMEM((NY, 2, 2, HD, KT), BF16),
            pltpu.VMEM((2, 2, HD, KT), BF16),
            pltpu.VMEM((2, 2, HD, KT), BF16),
            pltpu.VMEM((2, 2, 2, HD, KT), BF16),
            pltpu.VMEM((NX, 2, KT, HD), BF16),
            pltpu.VMEM((8, QT, HD), BF16),
            pltpu.VMEM((8, QT, HD), BF16),
            pltpu.VMEM((8, QT, HD), BF16),
            dma((NY,)), dma((NY,)), dma,
            dma, dma,
            dma((4,)), dma((4,)),
            dma((8,)), dma((8,)),
            dma((16,)), dma((16,)),
            dma((16,)), dma((16,)),
        ],
        compiler_params=pltpu.CompilerParams(collective_id=1, has_side_effects=True, vmem_limit_bytes=VMEM_LIMIT),
        name="scatter_grads",
    )(*arrays)


def store_kernel(*refs):
    count = len(refs) // 2
    sems = refs[-1]
    copies = [pltpu.make_async_copy(refs[n], refs[count + n], sems.at[n]) for n in range(count)]
    for copy in copies:
        copy.start()
    for copy in copies:
        copy.wait()


def store(*arrays):
    hbm = pl.BlockSpec(memory_space=pl.ANY)
    return pl.pallas_call(
        store_kernel,
        out_shape=tuple(jax.ShapeDtypeStruct(array.shape, array.dtype) for array in arrays),
        in_specs=[hbm] * len(arrays),
        out_specs=(hbm,) * len(arrays),
        scratch_shapes=[pltpu.SemaphoreType.DMA((len(arrays),))],
        compiler_params=pltpu.CompilerParams(vmem_limit_bytes=VMEM_LIMIT),
        name="store_grads",
    )(*arrays)


def body(
    query_states,
    key_states,
    value_states,
    attn_output,
    output_grad,
    logsumexp,
    block_order,
    doc_lengths,
):
    arrays = gather(query_states, key_states, value_states, attn_output, output_grad, logsumexp)
    dq, *near = tiles(0, block_order, doc_lengths, arrays)
    for d in (2, 1, 3):
        pairs = [(2 * plane + core, 2 * ((plane + d) % NY) + core) for plane in range(NY) for core in range(2)]
        near[d] = lax.ppermute(near[d], "ka", pairs)
    dq, dkv = tiles(1, block_order, doc_lengths, arrays, (dq,))
    return store(*scatter(dq, dkv, *near))


def solution(mesh):
    placed = (
        P(("pb", "ka"), "ha"),
        P(("ka", "pb"), "ha"),
        P(("ka", "pb"), "ha"),
        P(("pb", "ka"), "ha"),
        P(("pb", "ka"), "ha"),
        P("ha", ("pb", "ka")),
        P("ha"),
        P("ha"),
    )
    return jax.shard_map(
        body,
        mesh=mesh,
        in_specs=placed,
        out_specs=(P(("pb", "ka"), "ha"), P(("ka", "pb"), "ha"), P(("ka", "pb"), "ha")),
        check_vma=False,
    )
```

```python
from functools import partial
import math

import jax
import jax.numpy as jnp
from jax import lax
from jax.experimental import pallas as pl
from jax.experimental.pallas import tpu as pltpu
from jax.sharding import PartitionSpec as P

HD = 128
BLK = 512
ROWS = 128
NX, NY = 4, 4
VMEM_LIMIT = 60 << 20
BF16 = jnp.bfloat16
F32 = jnp.float32

softcap = 50.0
score_scale = 144.0 ** (-0.5)
log2e = math.log2(math.e)

ORDER = (0, 1, 3, 2)
CHUNKS = ((0, 0), (2, 1), (2, 0), (1, 1), (3, 1), (0, 1), (1, 0), (3, 0))
PASS = ((0,), (1,), (2, 3), (4, 5))
QT = 256
KT = 256
STEP = 32


def place():
    pb, ka = lax.axis_index("pb"), lax.axis_index("ka")
    return pb // 2, pb % 2, ka // 2, ka % 2


def device(x, z, y, c):
    return {"pb": 2 * x + z, "ka": 2 * y + c}


def remote(src, dst, send, recv, to):
    return pltpu.make_async_remote_copy(
        src_ref=src,
        dst_ref=dst,
        send_sem=send,
        recv_sem=recv,
        device_id=to,
        device_id_type=pl.DeviceIdType.MESH,
    )


def enter(x, z, y, c):
    barrier = pltpu.get_barrier_semaphore()
    for dx in range(NX):
        for dz in range(2):
            for dc in range(2):
                if (dx, dz, dc) != (0, 0, 0):
                    to = device((x + dx) % NX, (z + dz) % 2, y, (c + dc) % 2)
                    pl.semaphore_signal(barrier, inc=1, device_id=to, device_id_type=pl.DeviceIdType.MESH)
    for dy in (1, 3):
        to = device(x, z, (y + dy) % NY, c)
        pl.semaphore_signal(barrier, inc=1, device_id=to, device_id_type=pl.DeviceIdType.MESH)
    pl.semaphore_wait(barrier, 17)


def columns(head, count=1):
    return pl.ds(pl.multiple_of(head * HD, HD), count * HD)


def rows_at(start, count):
    return pl.ds(pl.multiple_of(start, ROWS), count)


def gather_kernel(
    q_ref, k_ref, v_ref, o_ref, g_ref, lse_ref,
    q2_ref, g2_ref, qt_ref, gt_ref, lb_ref, db_ref, kv_ref,
    o_v, g_v, aux_v, qh_v, gh_v, auxh_v, q2_v, g2_v, qt_v, gt_v, lb_v, db_v,
    load_sem, kv_send, kv_recv, y_send, y_recv, y2_send, y2_recv, q_send, q_recv, s_send, s_recv,
    a_send, a_recv, out_sem,
):
    x, z, y, c = place()
    loads = [
        pltpu.make_async_copy(o_ref, o_v, load_sem.at[0]),
        pltpu.make_async_copy(g_ref, g_v, load_sem.at[1]),
    ]
    for load in loads:
        load.start()
    enter(x, z, y, c)

    sibling = device(x, z, y, 1 - c)
    up, down = device(x, z, (y + 1) % NY, c), device(x, z, (y + 3) % NY, c)
    sends = []

    def send(src, dst, send_sem, recv_sem, to):
        copy = remote(src, dst, send_sem, recv_sem, to)
        copy.start()
        sends.append(copy)
        return copy

    def keep(src, dst, sem):
        copy = pltpu.make_async_copy(src, dst, sem)
        copy.start()
        return copy

    kv_copies = {}
    for dx, dz in ((0, 0), (0, 1), (1, 0), (3, 0), (1, 1), (3, 1), (2, 0), (2, 1)):
            tx, tz = (x + dx) % NX, (z + dz) % 2
            for part, ref in enumerate((k_ref, v_ref)):
                src = ref.at[:, columns(2 * tx + tz)]
                dst = kv_ref.at[y, c, x // 2, rows_at(z * ROWS, ROWS), pl.ds(part * HD, HD)]
                at = (dx * 2 + dz) * 2 + part
                if at < 2:
                    kv_copies[dx, dz, part] = keep(src, dst, kv_recv.at[at])
                else:
                    to = device(tx, tz, y, (c + dx) % 2)
                    kv_copies[dx, dz, part] = send(src, dst, kv_send.at[at], kv_recv.at[at], to)

    def block(plane, dx):
        return plane, (c + dx) % 2, ((x + NX - dx) % NX) // 2

    first, q_copies = {}, {}
    for dx in ORDER:
        for dz in range(2):
            for part in range(2):
                copy = kv_copies[dx, dz, part]
                if dx == 0 and dz == 0:
                    copy.wait()
                else:
                    copy.wait_recv()
        rows = kv_ref.at[block(y, dx)]
        for way, to in ((0, up), (1, down)):
            at = way * NX + dx
            first[way, dx] = send(rows, rows, y_send.at[at], y_recv.at[at], to)
        for j, (jx, jz) in enumerate(CHUNKS):
            if dx != 0:
                continue
            tx, tz = (x + jx) % NX, (z + jz) % 2
            for kind, (ref, out) in enumerate(((q_ref, qh_v), (g_ref, gh_v))):
                src = ref.at[:, columns(2 * (2 * tx + tz), 2)]
                dst = out.at[2 * x + z, rows_at(c * ROWS, ROWS), :]
                at = 2 * j + kind
                if j == 0:
                    q_copies[j, kind] = keep(src, dst, q_recv.at[at])
                else:
                    q_copies[j, kind] = send(src, dst, q_send.at[at], q_recv.at[at], device(tx, tz, y, c))

    for load in loads:
        load.wait()
    delta = jnp.zeros((16, ROWS), F32)
    for h in range(16):
        cols = pl.ds(h * HD, HD)
        prod = g_v[:, cols].astype(F32) * o_v[:, cols].astype(F32)
        high = prod.astype(BF16)
        low = (prod - high.astype(F32)).astype(BF16)
        pick = jnp.where(lax.broadcasted_iota(jnp.int32, (16, HD), 0) == h, 1.0, 0.0).astype(BF16)
        delta = delta + (nt(pick, high) + nt(pick, low))
    for h in range(8):
        aux_v[h, 0:2, :] = lse_ref[2 * h : 2 * h + 2, :] * log2e
        aux_v[h, 2:4, :] = delta[2 * h : 2 * h + 2, :]
        aux_v[h, 4:8, :] = jnp.zeros((4, ROWS), F32)
    a_copies = []
    for j, (dx, dz) in enumerate(CHUNKS):
        tx, tz = (x + dx) % NX, (z + dz) % 2
        for dc in range(2):
            src, dst, at = aux_v.at[2 * tx + tz], auxh_v.at[2 * (2 * x + z) + c], 2 * j + dc
            if at == 0:
                a_copies.append(keep(src, dst, a_recv.at[at]))
            else:
                a_copies.append(send(src, dst, a_send.at[at], a_recv.at[at], device(tx, tz, y, (c + dc) % 2)))

    passed = {}

    def chunk_of(j):
        dx, dz = CHUNKS[j]
        return 2 * ((x + NX - dx) % NX) + (z + 2 - dz) % 2

    def pass_on(j):
        for kind, out in enumerate((qh_v, gh_v)):
            if j == 0:
                q_copies[j, kind].wait()
            else:
                q_copies[j, kind].wait_recv()
            rows = out.at[chunk_of(j), rows_at(c * ROWS, ROWS), :]
            at = 2 * j + kind
            passed[j, kind] = send(rows, rows, s_send.at[at], s_recv.at[at], sibling)

    second = {}
    for n, dx in enumerate(ORDER):
        for j in PASS[n]:
            pass_on(j)
        for way, (plane, to) in enumerate((((y + 3) % NY, up), ((y + 1) % NY, down))):
            first[way, dx].wait_recv()
            at = way * NX + dx
            half = kv_ref.at[block(plane, dx)].at[:, pl.ds(way * HD, HD)]
            second[way, dx] = send(half, half, y2_send.at[at], y2_recv.at[at], to)

    for n, copy in enumerate(a_copies):
        if n == 0:
            copy.wait()
        else:
            copy.wait_recv()
    outs = []
    for j in range(len(CHUNKS) + 1):
        if j < len(CHUNKS) and (j, 0) not in passed:
            pass_on(j)
        if j > 0:
            i = chunk_of(j - 1)
            for kind in range(2):
                passed[j - 1, kind].wait_recv()
            for h in range(2):
                rows = slice(h * QT, (h + 1) * QT)
                for whole, split, turned in ((qh_v, q2_v, qt_v), (gh_v, g2_v, gt_v)):
                    part = whole[i, :, h * HD : (h + 1) * HD]
                    split[i, rows, :] = part
                    turned[i, :, rows] = part.T
            for n in range(2):
                spread = auxh_v[2 * i + n].T
                for h in range(2):
                    rows = slice(h * QT + n * ROWS, h * QT + (n + 1) * ROWS)
                    lb_v[i, rows, :] = jnp.broadcast_to(spread[:, h : h + 1], (ROWS, HD))
                    db_v[i, rows, :] = jnp.broadcast_to(spread[:, 2 + h : 3 + h], (ROWS, HD))
            for n, (src, dst) in enumerate(
                ((q2_v, q2_ref), (g2_v, g2_ref), (qt_v, qt_ref), (gt_v, gt_ref), (lb_v, lb_ref), (db_v, db_ref))
            ):
                outs.append(keep(src.at[i], dst.at[i], out_sem.at[j - 1, n]))

    for copy in second.values():
        copy.wait_recv()
    for copy in sends:
        copy.wait_send()
    for copy in outs:
        copy.wait()


def gather(q, k, v, o, g, lse):
    hbm = pl.BlockSpec(memory_space=pl.ANY)
    dma = pltpu.SemaphoreType.DMA
    split = (8, 2 * QT, HD)
    turned = (8, HD, 2 * QT)
    return pl.pallas_call(
        gather_kernel,
        out_shape=tuple(
            jax.ShapeDtypeStruct(shape, kind)
            for shape, kind in (
                (split, BF16), (split, BF16), (turned, BF16), (turned, BF16), (split, F32), (split, F32),
                ((NY, 2, 2, KT, 2 * HD), BF16),
            )
        ),
        in_specs=[hbm] * 5 + [pl.BlockSpec(memory_space=pltpu.VMEM)],
        out_specs=(hbm,) * 7,
        scratch_shapes=[
            pltpu.VMEM((ROWS, 2048), BF16),
            pltpu.VMEM((ROWS, 2048), BF16),
            pltpu.VMEM((8, 8, ROWS), F32),
            pltpu.VMEM((8, QT, 2 * HD), BF16),
            pltpu.VMEM((8, QT, 2 * HD), BF16),
            pltpu.VMEM((16, 8, ROWS), F32),
            pltpu.VMEM(split, BF16),
            pltpu.VMEM(split, BF16),
            pltpu.VMEM(turned, BF16),
            pltpu.VMEM(turned, BF16),
            pltpu.VMEM(split, F32),
            pltpu.VMEM(split, F32),
            dma((2,)),
            dma((16,)), dma((16,)),
            dma((8,)), dma((8,)),
            dma((8,)), dma((8,)),
            dma((16,)), dma((16,)),
            dma((16,)), dma((16,)),
            dma((16,)), dma((16,)),
            dma((8, 6)),
        ],
        compiler_params=pltpu.CompilerParams(collective_id=0, has_side_effects=True, vmem_limit_bytes=VMEM_LIMIT),
        name="gather_heads",
    )(q, k, v, o, g, lse)


def nt(a, b):
    return lax.dot_general(a, b, (((1,), (1,)), ((), ())), preferred_element_type=F32)


def nn(a, b):
    return jnp.dot(a, b, preferred_element_type=F32)


def tile_kernel(
    order_ref, lens_ref, q2_ref, g2_ref, qt_ref, gt_ref, lb_ref, db_ref, kv_ref,
    dq_ref, dkv_ref,
    q_v, g_v, qt_v, gt_v, lb_v, db_v, kv_v, acc_q, acc_k, acc_v, dq_v, dkv_v,
    s_a, s_b, dp_a, dp_b, p_a, p_b, ds_a, ds_b, tile_q, tile_k, tile_at, tile_cut, sems,
):
    x, z, y, c = place()
    loads = [
        pltpu.make_async_copy(src, dst, sems.at[n])
        for n, (src, dst) in enumerate(
            (
                (kv_ref, kv_v), (q2_ref, q_v), (g2_ref, g_v),
                (lb_ref, lb_v), (db_ref, db_v), (qt_ref, qt_v), (gt_ref, gt_v),
            )
        )
    ]
    for load in loads:
        load.start()
    starts = [lens_ref[0], lens_ref[0] + lens_ref[1], lens_ref[0] + lens_ref[1] + lens_ref[2]]

    def low_of(p):
        low = jnp.zeros_like(p)
        for start in starts:
            low = jnp.where(p >= start, start, low)
        return low

    base = [order_ref[2 * i + y // 2] * BLK + (y % 2) * QT for i in range(8)]
    first_low = [low_of(base[i]) for i in range(8)]
    last_low = [low_of(base[i] + (QT - 1)) for i in range(8)]

    def list_slot(slot, count):
        key = order_ref[slot] * BLK + ((x + c + slot // 2) % 2) * KT
        for i in range(8):
            needed = jnp.logical_and(key < base[i] + QT, key + KT > first_low[i])
            whole = jnp.logical_and(key + KT <= base[i] + 1, key >= last_low[i])
            tile_q[count] = i
            tile_k[count] = slot
            tile_at[count] = key - base[i]
            tile_cut[count] = jnp.where(whole, 0, 1)
            count = count + needed.astype(jnp.int32)
        return count

    count = lax.fori_loop(0, 16, list_slot, 0)
    for n in range(2):
        tile_q[count + n] = 0
        tile_k[count + n] = 0
        tile_at[count + n] = 1 << 20
        tile_cut[count + n] = 1
    pairs = (count + 1) // 2
    last = jnp.maximum(2 * pairs - 1, 1)

    def clear(i, _):
        acc_q[i] = jnp.zeros((2 * QT, HD), F32)
        for n in range(2):
            acc_k[2 * i + n] = jnp.zeros((HD, KT), F32)
            acc_v[2 * i + n] = jnp.zeros((HD, KT), F32)
        return 0

    lax.fori_loop(0, 8, clear, 0)

    def keys(t):
        return kv_v[tile_k[t], :, 0:HD]

    def values(t):
        return kv_v[tile_k[t], :, HD : 2 * HD]

    def scores(t, s_ref, dp_ref):
        i = tile_q[t]

        def piece(out, left, right, h):
            rows = slice(h * QT, (h + 1) * QT)
            out[rows, :] = nt(left[i, rows, :], right(t))

        return [
            partial(piece, out, left, right, h)
            for out, left, right in ((s_ref, q_v, keys), (dp_ref, g_v, values))
            for h in range(2)
        ]

    def weigh(t, s_ref, dp_ref, p_ref, ds_ref, cut):
        i, at = tile_q[t], tile_at[t]
        if cut:
            query_base = order_ref[2 * i + y // 2] * BLK + (y % 2) * QT
        step = STEP

        def piece(r):
            lse = lb_v[i, r : r + step, :]
            delta = db_v[i, r : r + step, :]
            lse = jnp.concatenate([lse] * (KT // HD), axis=1)
            delta = jnp.concatenate([delta] * (KT // HD), axis=1)
            th = jnp.tanh(s_ref[r : r + step, :] * (score_scale / softcap))
            p = jnp.exp2(th * (softcap * log2e) - lse)
            if cut:
                row = lax.broadcasted_iota(jnp.int32, (step, HD), 0) + r % QT
                low = low_of(row + query_base) - query_base
                row = jnp.concatenate([row] * (KT // HD), axis=1)
                low = jnp.concatenate([low] * (KT // HD), axis=1)
                key = lax.broadcasted_iota(jnp.int32, (step, KT), 1) + at
                p = jnp.where((key <= row) & (key >= low), p, 0.0)
            ds = p * (dp_ref[r : r + step, :] - delta) * ((1.0 - th * th) * score_scale)
            p_ref[r : r + step, :] = p.astype(BF16)
            ds_ref[r : r + step, :] = ds.astype(BF16)

        return [partial(piece, r) for r in range(0, 2 * QT, step)]

    def gradients(t, p_ref, ds_ref):
        i, slot = tile_q[t], tile_k[t]

        def key_piece(out, left, right):
            out[slot] += nn(left[i], right[...])

        def query_piece(h):
            rows = slice(h * QT, (h + 1) * QT)
            acc_q[i, rows, :] += nn(ds_ref[rows, :], keys(t))

        return [
            partial(key_piece, acc_v, gt_v, p_ref),
            partial(key_piece, acc_k, qt_v, ds_ref),
            partial(query_piece, 0),
            partial(query_piece, 1),
        ]

    def run(*lists):
        marked = [((n + 0.5) / len(pieces), m, piece) for m, pieces in enumerate(lists) for n, piece in enumerate(pieces)]
        for _, _, piece in sorted(marked, key=lambda entry: entry[:2]):
            piece()

    buffers = ((s_a, dp_a, p_a, ds_a), (s_b, dp_b, p_b, ds_b))

    def step(t, parity):
        s0, dp0, p0, ds0 = buffers[parity]
        s1, dp1, p1, ds1 = buffers[1 - parity]
        middle = jnp.minimum(t + 1, last)

        def whole_step(cut):
            run(
                scores(jnp.minimum(t + 2, last), s0, dp0) + gradients(t, p0, ds0),
                weigh(middle, s1, dp1, p1, ds1, cut),
            )

        pl.when(tile_cut[middle] == 0)(lambda: whole_step(False))
        pl.when(tile_cut[middle] != 0)(lambda: whole_step(True))

    for load in loads[:3]:
        load.wait()
    run(scores(0, s_a, dp_a))
    for load in loads[3:5]:
        load.wait()
    run(scores(1, s_b, dp_b), weigh(0, s_a, dp_a, p_a, ds_a, True))
    for load in loads[5:]:
        load.wait()

    def pair(n, _):
        step(2 * n, 0)
        step(2 * n + 1, 1)
        return 0

    lax.fori_loop(0, pairs, pair, 0)

    outs = [pltpu.make_async_copy(dq_v, dq_ref, sems.at[0])]
    for d in range(NY):
        plane = (y + d) % NY
        for q in range(4):
            slot = 4 * plane + 2 * ((c + q // 2) % 2) + q % 2
            dkv_v[d, q, 0] = acc_k[slot].astype(BF16)
            dkv_v[d, q, 1] = acc_v[slot].astype(BF16)
        outs.append(pltpu.make_async_copy(dkv_v.at[d], dkv_ref.at[d], sems.at[1 + d]))
        outs[-1].start()
    for i in range(8):
        for h in range(2):
            dq_v[h, i] = acc_q[i, h * QT : (h + 1) * QT, :].astype(BF16)
    outs[0].start()
    for out in outs:
        out.wait()


def tiles(order, lens, *arrays):
    smem = pl.BlockSpec(memory_space=pltpu.SMEM)
    hbm = pl.BlockSpec(memory_space=pl.ANY)
    split = (8, 2 * QT, HD)
    turned = (8, HD, 2 * QT)
    wide = pltpu.VMEM((2 * QT, KT), F32)
    narrow = pltpu.VMEM((2 * QT, KT), BF16)
    listed = pltpu.SMEM((136,), jnp.int32)
    return pl.pallas_call(
        tile_kernel,
        out_shape=(
            jax.ShapeDtypeStruct((2, 8, QT, HD), BF16),
            jax.ShapeDtypeStruct((NY, 4, 2, HD, KT), BF16),
        ),
        in_specs=[smem, smem] + [hbm] * len(arrays),
        out_specs=(hbm, hbm),
        scratch_shapes=[
            pltpu.VMEM(split, BF16),
            pltpu.VMEM(split, BF16),
            pltpu.VMEM(turned, BF16),
            pltpu.VMEM(turned, BF16),
            pltpu.VMEM(split, F32),
            pltpu.VMEM(split, F32),
            pltpu.VMEM((16, KT, 2 * HD), BF16),
            pltpu.VMEM(split, F32),
            pltpu.VMEM((16, HD, KT), F32),
            pltpu.VMEM((16, HD, KT), F32),
            pltpu.VMEM((2, 8, QT, HD), BF16),
            pltpu.VMEM((NY, 4, 2, HD, KT), BF16),
            wide, wide, wide, wide,
            narrow, narrow, narrow, narrow,
            listed, listed, listed, listed,
            pltpu.SemaphoreType.DMA((7,)),
        ],
        compiler_params=pltpu.CompilerParams(vmem_limit_bytes=VMEM_LIMIT),
        name="tiles",
    )(order, lens, *arrays)


SLOTS = (2, 3, 0, 1)


def scatter_kernel(
    dq_ref, dkv_ref,
    dq_out, dk_out, dv_out,
    own, land2, send1, land1, fin, mine, theirs, dq_v,
    load_sem, mine_sem, sib_send, sib_recv, s2_send, s2_recv, s1_send, s1_recv, f_send, f_recv, q_send, q_recv,
):
    x, z, y, c = place()
    head = 2 * x + z
    loads = [pltpu.make_async_copy(dkv_ref.at[d], own.at[d], load_sem.at[d]) for d in range(NY)]
    mine_load = pltpu.make_async_copy(dq_ref.at[c], mine, mine_sem)
    for load in [mine_load] + loads:
        load.start()
    enter(x, z, y, c)
    sibling = device(x, z, y, 1 - c)
    ways = (device(x, z, (y + 1) % NY, c), device(x, z, (y + 3) % NY, c))
    sends = []

    def send(src, dst, send_sem, recv_sem, to):
        copy = remote(src, dst, send_sem, recv_sem, to)
        copy.start()
        sends.append(copy)
        return copy

    copies2, copies1 = {}, {}
    for h in SLOTS:
        for part, to in enumerate(ways):
            at = part * 4 + h
            copies2[part, h] = send(dkv_ref.at[2, h, part], land2.at[part, h], s2_send.at[at], s2_recv.at[at], to)
    sib_copy = send(dq_ref.at[1 - c], theirs, sib_send, sib_recv, sibling)
    for h in SLOTS:
        for way, to in enumerate(ways):
            part = 1 - way
            at = (way * 2 + part) * 4 + h
            copies1[way, part, h] = send(
                dkv_ref.at[1 + 2 * way, h, part], land1.at[way, part, h], s1_send.at[at], s1_recv.at[at], to
            )

    mine_load.wait()
    sib_copy.wait_recv()
    q_copies = []
    for dx, dz in CHUNKS:
        tx, tz = (x + dx) % NX, (z + dz) % 2
        i = 2 * tx + tz
        dq_v[i] = (mine[i].astype(F32) + theirs[i].astype(F32)).astype(BF16)
        for dc in range(2):
            tc = (c + dc) % 2
            src = dq_v.at[i, rows_at(tc * ROWS, ROWS), :]
            dst = dq_out.at[:, columns(2 * head + c)]
            at = (dx * 2 + dz) * 2 + dc
            if at == 0:
                copy = pltpu.make_async_copy(src, dst, q_recv.at[at])
                copy.start()
                q_copies.append((True, copy))
            else:
                q_copies.append((False, send(src, dst, q_send.at[at], q_recv.at[at], device(tx, tz, y, tc))))

    for load in loads:
        load.wait()
    for h in SLOTS:
        for way, to in enumerate(ways):
            part = way
            copies2[part, h].wait_recv()
            total = own[1 + 2 * way, h, part].astype(F32) + land2[part, h].astype(F32)
            send1[way, h] = total.astype(BF16)
            at = (way * 2 + part) * 4 + h
            copies1[way, part, h] = send(
                send1.at[way, h], land1.at[way, part, h], s1_send.at[at], s1_recv.at[at], to
            )

    f_copies = []

    def final(dx, part, out, total):
        fin[dx, part] = total.T.astype(BF16)
        for dz in range(2):
            tz = (z + dz) % 2
            src = fin.at[dx, part, rows_at(tz * ROWS, ROWS), :]
            dst = out.at[:, columns(head)]
            at = (dx * 2 + part) * 2 + dz
            if dx == 0 and dz == 0:
                copy = pltpu.make_async_copy(src, dst, f_recv.at[at])
                copy.start()
                f_copies.append((True, copy))
            else:
                to = device((x + dx) % NX, tz, y, (c + dx) % 2)
                f_copies.append((False, send(src, dst, f_send.at[at], f_recv.at[at], to)))

    for dx in (3, 1, 2, 0):
        h = ((x + dx) % NX) // 2
        q = 2 * (dx % 2) + h
        if dx in (3, 2):
            for n in (0, 1):
                for way in range(2):
                    for part in range(2):
                        copies1[way, part, 2 * (dx % 2) + n].wait_recv()
        for part, out in ((0, dk_out), (1, dv_out)):
            total = own[0, q, part].astype(F32) + land1[0, part, q].astype(F32) + land1[1, part, q].astype(F32)
            final(dx, part, out, total)

    for local, copy in q_copies + f_copies:
        if local:
            copy.wait()
        else:
            copy.wait_recv()
    for copy in sends:
        copy.wait_send()


def scatter(*arrays):
    hbm = pl.BlockSpec(memory_space=pl.ANY)
    dma = pltpu.SemaphoreType.DMA
    return pl.pallas_call(
        scatter_kernel,
        out_shape=(
            jax.ShapeDtypeStruct((ROWS, 2048), BF16),
            jax.ShapeDtypeStruct((ROWS, 1024), BF16),
            jax.ShapeDtypeStruct((ROWS, 1024), BF16),
        ),
        in_specs=[hbm] * len(arrays),
        out_specs=(hbm,) * 3,
        scratch_shapes=[
            pltpu.VMEM((NY, 4, 2, HD, KT), BF16),
            pltpu.VMEM((2, 4, HD, KT), BF16),
            pltpu.VMEM((2, 4, HD, KT), BF16),
            pltpu.VMEM((2, 2, 4, HD, KT), BF16),
            pltpu.VMEM((NX, 2, KT, HD), BF16),
            pltpu.VMEM((8, QT, HD), BF16),
            pltpu.VMEM((8, QT, HD), BF16),
            pltpu.VMEM((8, QT, HD), BF16),
            dma((NY,)), dma,
            dma, dma,
            dma((8,)), dma((8,)),
            dma((16,)), dma((16,)),
            dma((16,)), dma((16,)),
            dma((16,)), dma((16,)),
        ],
        compiler_params=pltpu.CompilerParams(collective_id=1, has_side_effects=True, vmem_limit_bytes=VMEM_LIMIT),
        name="scatter_grads",
    )(*arrays)


def store_kernel(*refs):
    count = len(refs) // 3
    ins, outs, held, (load_sem, store_sem) = refs[:count], refs[count : 2 * count], refs[2 * count : 3 * count], refs[-2:]
    loads = [pltpu.make_async_copy(ins[n], held[n], load_sem.at[n]) for n in range(count)]
    stores = [pltpu.make_async_copy(held[n], outs[n], store_sem.at[n]) for n in range(count)]
    for load in loads:
        load.start()
    for n in range(count):
        loads[n].wait()
        stores[n].start()
    for copy in stores:
        copy.wait()


def store(*arrays):
    hbm = pl.BlockSpec(memory_space=pl.ANY)
    sems = pltpu.SemaphoreType.DMA((len(arrays),))
    return pl.pallas_call(
        store_kernel,
        out_shape=tuple(jax.ShapeDtypeStruct(array.shape, array.dtype) for array in arrays),
        in_specs=[hbm] * len(arrays),
        out_specs=(hbm,) * len(arrays),
        scratch_shapes=[pltpu.VMEM(array.shape, array.dtype) for array in arrays] + [sems, sems],
        compiler_params=pltpu.CompilerParams(vmem_limit_bytes=VMEM_LIMIT),
        name="store_grads",
    )(*arrays)


def body(
    query_states,
    key_states,
    value_states,
    attn_output,
    output_grad,
    logsumexp,
    block_order,
    doc_lengths,
):
    arrays = gather(query_states, key_states, value_states, attn_output, output_grad, logsumexp)
    dq, dkv = tiles(block_order, doc_lengths, *arrays[:-1], arrays[-1].reshape(16, KT, 2 * HD))
    return store(*scatter(dq, dkv))


def solution(mesh):
    placed = (
        P(("pb", "ka"), "ha"),
        P(("ka", "pb"), "ha"),
        P(("ka", "pb"), "ha"),
        P(("pb", "ka"), "ha"),
        P(("pb", "ka"), "ha"),
        P("ha", ("pb", "ka")),
        P("ha"),
        P("ha"),
    )
    return jax.shard_map(
        body,
        mesh=mesh,
        in_specs=placed,
        out_specs=(P(("pb", "ka"), "ha"), P(("ka", "pb"), "ha"), P(("ka", "pb"), "ha")),
        check_vma=False,
    )
```

```python
from functools import partial
import math

import jax
import jax.numpy as jnp
from jax import lax
from jax.experimental import pallas as pl
from jax.experimental.pallas import tpu as pltpu
from jax.sharding import PartitionSpec as P

HD = 128
BLK = 512
ROWS = 128
NX, NY = 4, 4
VMEM_LIMIT = 60 << 20
BF16 = jnp.bfloat16
F32 = jnp.float32

softcap = 50.0
score_scale = 144.0 ** (-0.5)
log2e = math.log2(math.e)

ORDER = (0, 1, 3, 2)
CHUNKS = ((0, 0), (2, 1), (2, 0), (1, 1), (3, 1), (0, 1), (1, 0), (3, 0))
PASS = ((0,), (1,), (2, 3), (4, 5))
QT = 256
KT = 256
STEP = 32
MR = 256


def place():
    pb, ka = lax.axis_index("pb"), lax.axis_index("ka")
    return pb // 2, pb % 2, ka // 2, ka % 2


def device(x, z, y, c):
    return {"pb": 2 * x + z, "ka": 2 * y + c}


def remote(src, dst, send, recv, to):
    return pltpu.make_async_remote_copy(
        src_ref=src,
        dst_ref=dst,
        send_sem=send,
        recv_sem=recv,
        device_id=to,
        device_id_type=pl.DeviceIdType.MESH,
    )


def enter(x, z, y, c):
    barrier = pltpu.get_barrier_semaphore()
    for dx in range(NX):
        for dz in range(2):
            for dc in range(2):
                if (dx, dz, dc) != (0, 0, 0):
                    to = device((x + dx) % NX, (z + dz) % 2, y, (c + dc) % 2)
                    pl.semaphore_signal(barrier, inc=1, device_id=to, device_id_type=pl.DeviceIdType.MESH)
    for dy in (1, 3):
        to = device(x, z, (y + dy) % NY, c)
        pl.semaphore_signal(barrier, inc=1, device_id=to, device_id_type=pl.DeviceIdType.MESH)
    pl.semaphore_wait(barrier, 17)


def columns(head, count=1):
    return pl.ds(pl.multiple_of(head * HD, HD), count * HD)


def rows_at(start, count):
    return pl.ds(pl.multiple_of(start, ROWS), count)


def gather_kernel(
    q_ref, k_ref, v_ref, o_ref, g_ref, lse_ref,
    q2_ref, g2_ref, qt_ref, gt_ref, auxh_ref, kv_ref,
    o_v, g_v, aux_v, qh_v, gh_v, q2_v, g2_v, qt_v, gt_v,
    load_sem, kv_send, kv_recv, y_send, y_recv, y2_send, y2_recv, q_send, q_recv, s_send, s_recv,
    a_send, a_recv, out_sem,
):
    x, z, y, c = place()
    loads = [
        pltpu.make_async_copy(o_ref, o_v, load_sem.at[0]),
        pltpu.make_async_copy(g_ref, g_v, load_sem.at[1]),
    ]
    for load in loads:
        load.start()
    enter(x, z, y, c)

    sibling = device(x, z, y, 1 - c)
    up, down = device(x, z, (y + 1) % NY, c), device(x, z, (y + 3) % NY, c)
    sends = []

    def send(src, dst, send_sem, recv_sem, to):
        copy = remote(src, dst, send_sem, recv_sem, to)
        copy.start()
        sends.append(copy)
        return copy

    def keep(src, dst, sem):
        copy = pltpu.make_async_copy(src, dst, sem)
        copy.start()
        return copy

    kv_copies = {}
    for dx, dz in ((0, 0), (0, 1), (1, 0), (3, 0), (1, 1), (3, 1), (2, 0), (2, 1)):
            tx, tz = (x + dx) % NX, (z + dz) % 2
            for part, ref in enumerate((k_ref, v_ref)):
                src = ref.at[:, columns(2 * tx + tz)]
                dst = kv_ref.at[y, c, x // 2, rows_at(z * ROWS, ROWS), pl.ds(part * HD, HD)]
                at = (dx * 2 + dz) * 2 + part
                if at < 2:
                    kv_copies[dx, dz, part] = keep(src, dst, kv_recv.at[at])
                else:
                    to = device(tx, tz, y, (c + dx) % 2)
                    kv_copies[dx, dz, part] = send(src, dst, kv_send.at[at], kv_recv.at[at], to)

    def block(plane, dx):
        return plane, (c + dx) % 2, ((x + NX - dx) % NX) // 2

    first, q_copies = {}, {}
    for dx in ORDER:
        for dz in range(2):
            for part in range(2):
                copy = kv_copies[dx, dz, part]
                if dx == 0 and dz == 0:
                    copy.wait()
                else:
                    copy.wait_recv()
        rows = kv_ref.at[block(y, dx)]
        for way, to in ((0, up), (1, down)):
            at = way * NX + dx
            first[way, dx] = send(rows, rows, y_send.at[at], y_recv.at[at], to)
        for j, (jx, jz) in enumerate(CHUNKS):
            if dx != 0:
                continue
            tx, tz = (x + jx) % NX, (z + jz) % 2
            for kind, (ref, out) in enumerate(((q_ref, qh_v), (g_ref, gh_v))):
                src = ref.at[:, columns(2 * (2 * tx + tz), 2)]
                dst = out.at[2 * x + z, rows_at(c * ROWS, ROWS), :]
                at = 2 * j + kind
                if j == 0:
                    q_copies[j, kind] = keep(src, dst, q_recv.at[at])
                else:
                    q_copies[j, kind] = send(src, dst, q_send.at[at], q_recv.at[at], device(tx, tz, y, c))

    for load in loads:
        load.wait()
    delta = jnp.zeros((16, ROWS), F32)
    for h in range(16):
        cols = pl.ds(h * HD, HD)
        prod = g_v[:, cols].astype(F32) * o_v[:, cols].astype(F32)
        high = prod.astype(BF16)
        low = (prod - high.astype(F32)).astype(BF16)
        pick = jnp.where(lax.broadcasted_iota(jnp.int32, (16, HD), 0) == h, 1.0, 0.0).astype(BF16)
        delta = delta + (nt(pick, high) + nt(pick, low))
    for h in range(8):
        aux_v[h, 0:2, :] = lse_ref[2 * h : 2 * h + 2, :] * log2e
        aux_v[h, 2:4, :] = delta[2 * h : 2 * h + 2, :]
        aux_v[h, 4:8, :] = jnp.zeros((4, ROWS), F32)
    a_copies = []
    for j, (dx, dz) in enumerate(CHUNKS):
        tx, tz = (x + dx) % NX, (z + dz) % 2
        for dc in range(2):
            src, dst, at = aux_v.at[2 * tx + tz], auxh_ref.at[2 * (2 * x + z) + c], 2 * j + dc
            if at == 0:
                a_copies.append(keep(src, dst, a_recv.at[at]))
            else:
                a_copies.append(send(src, dst, a_send.at[at], a_recv.at[at], device(tx, tz, y, (c + dc) % 2)))

    passed = {}

    def chunk_of(j):
        dx, dz = CHUNKS[j]
        return 2 * ((x + NX - dx) % NX) + (z + 2 - dz) % 2

    def pass_on(j):
        for kind, out in enumerate((qh_v, gh_v)):
            if j == 0:
                q_copies[j, kind].wait()
            else:
                q_copies[j, kind].wait_recv()
            rows = out.at[chunk_of(j), rows_at(c * ROWS, ROWS), :]
            at = 2 * j + kind
            passed[j, kind] = send(rows, rows, s_send.at[at], s_recv.at[at], sibling)

    second = {}
    for n, dx in enumerate(ORDER):
        for j in PASS[n]:
            pass_on(j)
        for way, (plane, to) in enumerate((((y + 3) % NY, up), ((y + 1) % NY, down))):
            first[way, dx].wait_recv()
            at = way * NX + dx
            half = kv_ref.at[block(plane, dx)].at[:, pl.ds(way * HD, HD)]
            second[way, dx] = send(half, half, y2_send.at[at], y2_recv.at[at], to)

    for n, copy in enumerate(a_copies):
        if n == 0:
            copy.wait()
        else:
            copy.wait_recv()
    outs = []
    for j in range(len(CHUNKS) + 1):
        if j < len(CHUNKS) and (j, 0) not in passed:
            pass_on(j)
        if j > 0:
            i = chunk_of(j - 1)
            for kind in range(2):
                passed[j - 1, kind].wait_recv()
            for h in range(2):
                rows = slice(h * QT, (h + 1) * QT)
                for whole, split, turned in ((qh_v, q2_v, qt_v), (gh_v, g2_v, gt_v)):
                    part = whole[i, :, h * HD : (h + 1) * HD]
                    split[i, rows, :] = part
                    turned[i, :, rows] = part.T
            for n, (src, dst) in enumerate(
                ((q2_v, q2_ref), (g2_v, g2_ref), (qt_v, qt_ref), (gt_v, gt_ref))
            ):
                outs.append(keep(src.at[i], dst.at[i], out_sem.at[j - 1, n]))

    for copy in second.values():
        copy.wait_recv()
    for copy in sends:
        copy.wait_send()
    for copy in outs:
        copy.wait()


def gather(q, k, v, o, g, lse):
    hbm = pl.BlockSpec(memory_space=pl.ANY)
    dma = pltpu.SemaphoreType.DMA
    split = (8, 2 * QT, HD)
    turned = (8, HD, 2 * QT)
    return pl.pallas_call(
        gather_kernel,
        out_shape=tuple(
            jax.ShapeDtypeStruct(shape, kind)
            for shape, kind in (
                (split, BF16), (split, BF16), (turned, BF16), (turned, BF16), ((16, 8, ROWS), F32),
                ((NY, 2, 2, KT, 2 * HD), BF16),
            )
        ),
        in_specs=[hbm] * 5 + [pl.BlockSpec(memory_space=pltpu.VMEM)],
        out_specs=(hbm,) * 6,
        scratch_shapes=[
            pltpu.VMEM((ROWS, 2048), BF16),
            pltpu.VMEM((ROWS, 2048), BF16),
            pltpu.VMEM((8, 8, ROWS), F32),
            pltpu.VMEM((8, QT, 2 * HD), BF16),
            pltpu.VMEM((8, QT, 2 * HD), BF16),
            pltpu.VMEM(split, BF16),
            pltpu.VMEM(split, BF16),
            pltpu.VMEM(turned, BF16),
            pltpu.VMEM(turned, BF16),
            dma((2,)),
            dma((16,)), dma((16,)),
            dma((8,)), dma((8,)),
            dma((8,)), dma((8,)),
            dma((16,)), dma((16,)),
            dma((16,)), dma((16,)),
            dma((16,)), dma((16,)),
            dma((8, 4)),
        ],
        compiler_params=pltpu.CompilerParams(collective_id=0, has_side_effects=True, vmem_limit_bytes=VMEM_LIMIT),
        name="gather_heads",
    )(q, k, v, o, g, lse)


def nt(a, b):
    return lax.dot_general(a, b, (((1,), (1,)), ((), ())), preferred_element_type=F32)


def nn(a, b):
    return jnp.dot(a, b, preferred_element_type=F32)


def tile_kernel(
    order_ref, lens_ref, q2_ref, g2_ref, qt_ref, gt_ref, aux_ref, kv_ref,
    dq_ref, dkv_ref,
    q_v, g_v, qt_v, gt_v, aux_v, lb_v, db_v, kv_v, acc_q, acc_k, acc_v, dq_v, dkv_v,
    p_a, p_b, ds_a, ds_b, tile_list, cut_list, sems,
):
    x, z, y, c = place()
    loads = [
        pltpu.make_async_copy(src, dst, sems.at[n])
        for n, (src, dst) in enumerate(
            (
                (aux_ref, aux_v), (kv_ref, kv_v), (q2_ref, q_v), (g2_ref, g_v), (qt_ref, qt_v), (gt_ref, gt_v),
            )
        )
    ]
    for load in loads:
        load.start()
    starts = [lens_ref[0], lens_ref[0] + lens_ref[1], lens_ref[0] + lens_ref[1] + lens_ref[2]]

    def low_of(p):
        low = jnp.zeros_like(p)
        for start in starts:
            low = jnp.where(p >= start, start, low)
        return low

    base = [order_ref[2 * i + y // 2] * BLK + (y % 2) * QT for i in range(8)]
    first_low = [low_of(base[i]) for i in range(8)]
    last_low = [low_of(base[i] + (QT - 1)) for i in range(8)]

    def list_slot(slot, counts):
        key = order_ref[slot] * BLK + ((x + c + slot // 2) % 2) * KT
        wholes, cuts = counts
        for i in range(8):
            needed = jnp.logical_and(key < base[i] + QT, key + KT > first_low[i])
            whole = jnp.logical_and(key + KT <= base[i] + 1, key >= last_low[i])
            entry = slot * 8 + i
            tile_list[wholes] = entry
            cut_list[cuts] = entry
            wholes = wholes + jnp.logical_and(needed, whole).astype(jnp.int32)
            cuts = cuts + jnp.logical_and(needed, jnp.logical_not(whole)).astype(jnp.int32)
        return wholes, cuts

    wholes, cuts = lax.fori_loop(0, 16, list_slot, (0, 0))

    def append(n, _):
        tile_list[wholes + n] = cut_list[n]
        return 0

    lax.fori_loop(0, cuts, append, 0)
    count = wholes + cuts
    for n in range(2):
        tile_list[count + n] = 0
    pairs = (count + 1) // 2
    last = jnp.maximum(2 * pairs - 1, 1)

    def clear(i, _):
        acc_q[i] = jnp.zeros((2 * QT, HD), F32)
        for n in range(2):
            acc_k[2 * i + n] = jnp.zeros((HD, KT), F32)
            acc_v[2 * i + n] = jnp.zeros((HD, KT), F32)
        return 0

    lax.fori_loop(0, 8, clear, 0)

    def keys(t):
        return kv_v[tile_list[t] // 8, :, 0:HD]

    def values(t):
        return kv_v[tile_list[t] // 8, :, HD : 2 * HD]

    def weigh(t, p_ref, ds_ref, cut):
        i, slot = tile_list[t] % 8, tile_list[t] // 8
        if cut:
            query_base = order_ref[2 * i + y // 2] * BLK + (y % 2) * QT
            at = order_ref[slot] * BLK + ((x + c + slot // 2) % 2) * KT - query_base
            at = jnp.where(t < count, at, 1 << 20)
        step = STEP
        held = {}

        def score(n):
            rows = slice(n * MR, (n + 1) * MR)
            held[n] = (nt(q_v[i, rows, :], keys(t)), nt(g_v[i, rows, :], values(t)))

        def piece(r):
            n, o = r // MR, r % MR
            raw, dprob = held[n][0][o : o + step], held[n][1][o : o + step]
            lse = lb_v[i, r : r + step, :]
            delta = db_v[i, r : r + step, :]
            lse = jnp.concatenate([lse] * (KT // HD), axis=1)
            delta = jnp.concatenate([delta] * (KT // HD), axis=1)
            th = jnp.tanh(raw * (score_scale / softcap))
            p = jnp.exp2(th * (softcap * log2e) - lse)
            if cut:
                row = lax.broadcasted_iota(jnp.int32, (step, HD), 0) + r % QT
                low = low_of(row + query_base) - query_base
                row = jnp.concatenate([row] * (KT // HD), axis=1)
                low = jnp.concatenate([low] * (KT // HD), axis=1)
                key = lax.broadcasted_iota(jnp.int32, (step, KT), 1) + at
                p = jnp.where((key <= row) & (key >= low), p, 0.0)
            ds = p * (dprob - delta) * ((1.0 - th * th) * score_scale)
            p_ref[r : r + step, :] = p.astype(BF16)
            ds_ref[r : r + step, :] = ds.astype(BF16)

        count_m = 2 * QT // MR
        out = [partial(score, 0)]
        for n in range(count_m):
            if n + 1 < count_m:
                out.append(partial(score, n + 1))
            out += [partial(piece, r) for r in range(n * MR, (n + 1) * MR, step)]
        return out

    def gradients(t, p_ref, ds_ref):
        i, slot = tile_list[t] % 8, tile_list[t] // 8

        def key_piece(out, left, right):
            out[slot] += nn(left[i], right[...])

        def query_piece(h):
            rows = slice(h * QT, (h + 1) * QT)
            acc_q[i, rows, :] += nn(ds_ref[rows, :], keys(t))

        return [
            partial(key_piece, acc_v, gt_v, p_ref),
            partial(key_piece, acc_k, qt_v, ds_ref),
            partial(query_piece, 0),
            partial(query_piece, 1),
        ]

    def run(*lists):
        marked = [((n + 0.5) / len(pieces), m, piece) for m, pieces in enumerate(lists) for n, piece in enumerate(pieces)]
        for _, _, piece in sorted(marked, key=lambda entry: entry[:2]):
            piece()

    def step(t, old, new, cut):
        run(weigh(jnp.minimum(t + 1, last), *new, cut), gradients(t, *old))

    def pair(n, _):
        def steps(cut):
            step(2 * n, (p_a, ds_a), (p_b, ds_b), cut)
            step(2 * n + 1, (p_b, ds_b), (p_a, ds_a), cut)

        whole = 2 * n + 2 < wholes
        pl.when(whole)(lambda: steps(False))
        pl.when(jnp.logical_not(whole))(lambda: steps(True))
        return 0

    loads[0].wait()

    def spread_chunk(i, _):
        for n in range(2):
            turned = aux_v[2 * i + n].T
            for h in range(2):
                rows = slice(h * QT + n * ROWS, h * QT + (n + 1) * ROWS)
                lb_v[i, rows, :] = jnp.broadcast_to(turned[:, h : h + 1], (ROWS, HD))
                db_v[i, rows, :] = jnp.broadcast_to(turned[:, 2 + h : 3 + h], (ROWS, HD))
        return 0

    lax.fori_loop(0, 8, spread_chunk, 0)
    for load in loads[1:4]:
        load.wait()
    run(weigh(0, p_a, ds_a, True))
    for load in loads[4:]:
        load.wait()

    lax.fori_loop(0, pairs, pair, 0)

    outs = [pltpu.make_async_copy(dq_v, dq_ref, sems.at[0])]
    for d in range(NY):
        plane = (y + d) % NY
        for q in range(4):
            slot = 4 * plane + 2 * ((c + q // 2) % 2) + q % 2
            dkv_v[d, q, 0] = acc_k[slot].astype(BF16)
            dkv_v[d, q, 1] = acc_v[slot].astype(BF16)
        outs.append(pltpu.make_async_copy(dkv_v.at[d], dkv_ref.at[d], sems.at[1 + d]))
        outs[-1].start()
    for i in range(8):
        for h in range(2):
            dq_v[h, i] = acc_q[i, h * QT : (h + 1) * QT, :].astype(BF16)
    outs[0].start()
    for out in outs:
        out.wait()


def tiles(order, lens, *arrays):
    smem = pl.BlockSpec(memory_space=pltpu.SMEM)
    hbm = pl.BlockSpec(memory_space=pl.ANY)
    split = (8, 2 * QT, HD)
    turned = (8, HD, 2 * QT)
    narrow = pltpu.VMEM((2 * QT, KT), BF16)
    listed = pltpu.SMEM((136,), jnp.int32)
    return pl.pallas_call(
        tile_kernel,
        out_shape=(
            jax.ShapeDtypeStruct((2, 8, QT, HD), BF16),
            jax.ShapeDtypeStruct((NY, 4, 2, HD, KT), BF16),
        ),
        in_specs=[smem, smem] + [hbm] * len(arrays),
        out_specs=(hbm, hbm),
        scratch_shapes=[
            pltpu.VMEM(split, BF16),
            pltpu.VMEM(split, BF16),
            pltpu.VMEM(turned, BF16),
            pltpu.VMEM(turned, BF16),
            pltpu.VMEM((16, 8, ROWS), F32),
            pltpu.VMEM(split, F32),
            pltpu.VMEM(split, F32),
            pltpu.VMEM((16, KT, 2 * HD), BF16),
            pltpu.VMEM(split, F32),
            pltpu.VMEM((16, HD, KT), F32),
            pltpu.VMEM((16, HD, KT), F32),
            pltpu.VMEM((2, 8, QT, HD), BF16),
            pltpu.VMEM((NY, 4, 2, HD, KT), BF16),
            narrow, narrow, narrow, narrow,
            listed, listed,
            pltpu.SemaphoreType.DMA((7,)),
        ],
        compiler_params=pltpu.CompilerParams(vmem_limit_bytes=VMEM_LIMIT),
        name="tiles",
    )(order, lens, *arrays)


SLOTS = (2, 3, 0, 1)


def scatter_kernel(
    dq_ref, dkv_ref,
    dq_out, dk_out, dv_out,
    own, land2, send1, land1, fin, mine, theirs, dq_v,
    load_sem, mine_sem, sib_send, sib_recv, s2_send, s2_recv, s1_send, s1_recv, f_send, f_recv, q_send, q_recv,
):
    x, z, y, c = place()
    head = 2 * x + z
    loads = [pltpu.make_async_copy(dkv_ref.at[d], own.at[d], load_sem.at[d]) for d in range(NY)]
    mine_load = pltpu.make_async_copy(dq_ref.at[c], mine, mine_sem)
    for load in [mine_load] + loads:
        load.start()
    enter(x, z, y, c)
    sibling = device(x, z, y, 1 - c)
    ways = (device(x, z, (y + 1) % NY, c), device(x, z, (y + 3) % NY, c))
    sends = []

    def send(src, dst, send_sem, recv_sem, to):
        copy = remote(src, dst, send_sem, recv_sem, to)
        copy.start()
        sends.append(copy)
        return copy

    copies2, copies1 = {}, {}
    for h in SLOTS:
        for part, to in enumerate(ways):
            at = part * 4 + h
            copies2[part, h] = send(dkv_ref.at[2, h, part], land2.at[part, h], s2_send.at[at], s2_recv.at[at], to)
    sib_copy = send(dq_ref.at[1 - c], theirs, sib_send, sib_recv, sibling)
    for h in SLOTS:
        for way, to in enumerate(ways):
            part = 1 - way
            at = (way * 2 + part) * 4 + h
            copies1[way, part, h] = send(
                dkv_ref.at[1 + 2 * way, h, part], land1.at[way, part, h], s1_send.at[at], s1_recv.at[at], to
            )

    mine_load.wait()
    sib_copy.wait_recv()
    q_copies = []
    for dx, dz in CHUNKS:
        tx, tz = (x + dx) % NX, (z + dz) % 2
        i = 2 * tx + tz
        dq_v[i] = (mine[i].astype(F32) + theirs[i].astype(F32)).astype(BF16)
        for dc in range(2):
            tc = (c + dc) % 2
            src = dq_v.at[i, rows_at(tc * ROWS, ROWS), :]
            dst = dq_out.at[:, columns(2 * head + c)]
            at = (dx * 2 + dz) * 2 + dc
            if at == 0:
                copy = pltpu.make_async_copy(src, dst, q_recv.at[at])
                copy.start()
                q_copies.append((True, copy))
            else:
                q_copies.append((False, send(src, dst, q_send.at[at], q_recv.at[at], device(tx, tz, y, tc))))

    for load in loads:
        load.wait()
    for h in SLOTS:
        for way, to in enumerate(ways):
            part = way
            copies2[part, h].wait_recv()
            total = own[1 + 2 * way, h, part].astype(F32) + land2[part, h].astype(F32)
            send1[way, h] = total.astype(BF16)
            at = (way * 2 + part) * 4 + h
            copies1[way, part, h] = send(
                send1.at[way, h], land1.at[way, part, h], s1_send.at[at], s1_recv.at[at], to
            )

    f_copies = []

    def final(dx, part, out, total):
        fin[dx, part] = total.T.astype(BF16)
        for dz in range(2):
            tz = (z + dz) % 2
            src = fin.at[dx, part, rows_at(tz * ROWS, ROWS), :]
            dst = out.at[:, columns(head)]
            at = (dx * 2 + part) * 2 + dz
            if dx == 0 and dz == 0:
                copy = pltpu.make_async_copy(src, dst, f_recv.at[at])
                copy.start()
                f_copies.append((True, copy))
            else:
                to = device((x + dx) % NX, tz, y, (c + dx) % 2)
                f_copies.append((False, send(src, dst, f_send.at[at], f_recv.at[at], to)))

    for dx in (3, 1, 2, 0):
        h = ((x + dx) % NX) // 2
        q = 2 * (dx % 2) + h
        if dx in (3, 2):
            for n in (0, 1):
                for way in range(2):
                    for part in range(2):
                        copies1[way, part, 2 * (dx % 2) + n].wait_recv()
        for part, out in ((0, dk_out), (1, dv_out)):
            total = own[0, q, part].astype(F32) + land1[0, part, q].astype(F32) + land1[1, part, q].astype(F32)
            final(dx, part, out, total)

    for local, copy in q_copies + f_copies:
        if local:
            copy.wait()
        else:
            copy.wait_recv()
    for copy in sends:
        copy.wait_send()


def scatter(*arrays):
    hbm = pl.BlockSpec(memory_space=pl.ANY)
    dma = pltpu.SemaphoreType.DMA
    return pl.pallas_call(
        scatter_kernel,
        out_shape=(
            jax.ShapeDtypeStruct((ROWS, 2048), BF16),
            jax.ShapeDtypeStruct((ROWS, 1024), BF16),
            jax.ShapeDtypeStruct((ROWS, 1024), BF16),
        ),
        in_specs=[hbm] * len(arrays),
        out_specs=(hbm,) * 3,
        scratch_shapes=[
            pltpu.VMEM((NY, 4, 2, HD, KT), BF16),
            pltpu.VMEM((2, 4, HD, KT), BF16),
            pltpu.VMEM((2, 4, HD, KT), BF16),
            pltpu.VMEM((2, 2, 4, HD, KT), BF16),
            pltpu.VMEM((NX, 2, KT, HD), BF16),
            pltpu.VMEM((8, QT, HD), BF16),
            pltpu.VMEM((8, QT, HD), BF16),
            pltpu.VMEM((8, QT, HD), BF16),
            dma((NY,)), dma,
            dma, dma,
            dma((8,)), dma((8,)),
            dma((16,)), dma((16,)),
            dma((16,)), dma((16,)),
            dma((16,)), dma((16,)),
        ],
        compiler_params=pltpu.CompilerParams(collective_id=1, has_side_effects=True, vmem_limit_bytes=VMEM_LIMIT),
        name="scatter_grads",
    )(*arrays)


def store_kernel(*refs):
    count = len(refs) // 3
    ins, outs, held, (load_sem, store_sem) = refs[:count], refs[count : 2 * count], refs[2 * count : 3 * count], refs[-2:]
    loads = [pltpu.make_async_copy(ins[n], held[n], load_sem.at[n]) for n in range(count)]
    stores = [pltpu.make_async_copy(held[n], outs[n], store_sem.at[n]) for n in range(count)]
    for load in loads:
        load.start()
    for n in range(count):
        loads[n].wait()
        stores[n].start()
    for copy in stores:
        copy.wait()


def store(*arrays):
    hbm = pl.BlockSpec(memory_space=pl.ANY)
    sems = pltpu.SemaphoreType.DMA((len(arrays),))
    return pl.pallas_call(
        store_kernel,
        out_shape=tuple(jax.ShapeDtypeStruct(array.shape, array.dtype) for array in arrays),
        in_specs=[hbm] * len(arrays),
        out_specs=(hbm,) * len(arrays),
        scratch_shapes=[pltpu.VMEM(array.shape, array.dtype) for array in arrays] + [sems, sems],
        compiler_params=pltpu.CompilerParams(vmem_limit_bytes=VMEM_LIMIT),
        name="store_grads",
    )(*arrays)


def body(
    query_states,
    key_states,
    value_states,
    attn_output,
    output_grad,
    logsumexp,
    block_order,
    doc_lengths,
):
    arrays = gather(query_states, key_states, value_states, attn_output, output_grad, logsumexp)
    dq, dkv = tiles(block_order, doc_lengths, *arrays[:-1], arrays[-1].reshape(16, KT, 2 * HD))
    return store(*scatter(dq, dkv))


def solution(mesh):
    placed = (
        P(("pb", "ka"), "ha"),
        P(("ka", "pb"), "ha"),
        P(("ka", "pb"), "ha"),
        P(("pb", "ka"), "ha"),
        P(("pb", "ka"), "ha"),
        P("ha", ("pb", "ka")),
        P("ha"),
        P("ha"),
    )
    return jax.shard_map(
        body,
        mesh=mesh,
        in_specs=placed,
        out_specs=(P(("pb", "ka"), "ha"), P(("ka", "pb"), "ha"), P(("ka", "pb"), "ha")),
        check_vma=False,
    )
```

```python
from functools import partial
import math

import jax
import jax.numpy as jnp
from jax import lax
from jax.experimental import pallas as pl
from jax.experimental.pallas import tpu as pltpu
from jax.sharding import PartitionSpec as P

HD = 128
BLK = 512
ROWS = 128
NX, NY = 4, 4
VMEM_LIMIT = 60 << 20
BF16 = jnp.bfloat16
F32 = jnp.float32

softcap = 50.0
score_scale = 144.0 ** (-0.5)
log2e = math.log2(math.e)

ORDER = (0, 1, 3, 2)
CHUNKS = ((0, 0), (2, 1), (2, 0), (1, 1), (3, 1), (0, 1), (1, 0), (3, 0))
PASS = ((0,), (1,), (2, 3), (4, 5))
QT = 256
KT = 256
STEP = 32
MR = 256


def place():
    pb, ka = lax.axis_index("pb"), lax.axis_index("ka")
    return pb // 2, pb % 2, ka // 2, ka % 2


def device(x, z, y, c):
    return {"pb": 2 * x + z, "ka": 2 * y + c}


def remote(src, dst, send, recv, to):
    return pltpu.make_async_remote_copy(
        src_ref=src,
        dst_ref=dst,
        send_sem=send,
        recv_sem=recv,
        device_id=to,
        device_id_type=pl.DeviceIdType.MESH,
    )


def enter(x, z, y, c):
    barrier = pltpu.get_barrier_semaphore()
    for dx in range(NX):
        for dz in range(2):
            for dc in range(2):
                if (dx, dz, dc) != (0, 0, 0):
                    to = device((x + dx) % NX, (z + dz) % 2, y, (c + dc) % 2)
                    pl.semaphore_signal(barrier, inc=1, device_id=to, device_id_type=pl.DeviceIdType.MESH)
    for dy in (1, 3):
        to = device(x, z, (y + dy) % NY, c)
        pl.semaphore_signal(barrier, inc=1, device_id=to, device_id_type=pl.DeviceIdType.MESH)
    pl.semaphore_wait(barrier, 17)


def columns(head, count=1):
    return pl.ds(pl.multiple_of(head * HD, HD), count * HD)


def rows_at(start, count):
    return pl.ds(pl.multiple_of(start, ROWS), count)


def gather_kernel(
    q_ref, k_ref, v_ref, o_ref, g_ref, lse_ref,
    q2_ref, g2_ref, qt_ref, gt_ref, auxh_ref, kv_ref,
    o_v, g_v, aux_v, qh_v, gh_v, q2_v, g2_v, qt_v, gt_v,
    load_sem, kv_send, kv_recv, y_send, y_recv, y2_send, y2_recv, q_send, q_recv, s_send, s_recv,
    a_send, a_recv, out_sem,
):
    x, z, y, c = place()
    loads = [
        pltpu.make_async_copy(o_ref, o_v, load_sem.at[0]),
        pltpu.make_async_copy(g_ref, g_v, load_sem.at[1]),
    ]
    for load in loads:
        load.start()
    enter(x, z, y, c)

    sibling = device(x, z, y, 1 - c)
    up, down = device(x, z, (y + 1) % NY, c), device(x, z, (y + 3) % NY, c)
    sends = []

    def send(src, dst, send_sem, recv_sem, to):
        copy = remote(src, dst, send_sem, recv_sem, to)
        copy.start()
        sends.append(copy)
        return copy

    def keep(src, dst, sem):
        copy = pltpu.make_async_copy(src, dst, sem)
        copy.start()
        return copy

    kv_copies = {}
    for dx, dz in ((0, 0), (0, 1), (1, 0), (3, 0), (1, 1), (3, 1), (2, 0), (2, 1)):
            tx, tz = (x + dx) % NX, (z + dz) % 2
            for part, ref in enumerate((k_ref, v_ref)):
                src = ref.at[:, columns(2 * tx + tz)]
                dst = kv_ref.at[y, c, x // 2, rows_at(z * ROWS, ROWS), pl.ds(part * HD, HD)]
                at = (dx * 2 + dz) * 2 + part
                if at < 2:
                    kv_copies[dx, dz, part] = keep(src, dst, kv_recv.at[at])
                else:
                    to = device(tx, tz, y, (c + dx) % 2)
                    kv_copies[dx, dz, part] = send(src, dst, kv_send.at[at], kv_recv.at[at], to)

    own_rows = kv_ref.at[y, c, x // 2, rows_at(z * ROWS, ROWS), :]
    other_rows = kv_ref.at[y, c, x // 2, rows_at((1 - z) * ROWS, ROWS), :]
    kv_copies[0, 0, 0].wait()
    kv_copies[0, 0, 1].wait()
    own_first = [
        send(own_rows, own_rows, y_send.at[8 + way], y_recv.at[8 + way], to) for way, to in enumerate((up, down))
    ]

    def block(plane, dx):
        return plane, (c + dx) % 2, ((x + NX - dx) % NX) // 2

    first, q_copies = {}, {}
    for dx in ORDER:
        for dz in range(2):
            for part in range(2):
                if dx != 0 or dz != 0:
                    kv_copies[dx, dz, part].wait_recv()
        rows = other_rows if dx == 0 else kv_ref.at[block(y, dx)]
        for way, to in ((0, up), (1, down)):
            at = way * NX + dx
            first[way, dx] = send(rows, rows, y_send.at[at], y_recv.at[at], to)
        for j, (jx, jz) in enumerate(CHUNKS):
            if dx != 0:
                continue
            tx, tz = (x + jx) % NX, (z + jz) % 2
            for kind, (ref, out) in enumerate(((q_ref, qh_v), (g_ref, gh_v))):
                src = ref.at[:, columns(2 * (2 * tx + tz), 2)]
                dst = out.at[2 * x + z, rows_at(c * ROWS, ROWS), :]
                at = 2 * j + kind
                if j == 0:
                    q_copies[j, kind] = keep(src, dst, q_recv.at[at])
                else:
                    q_copies[j, kind] = send(src, dst, q_send.at[at], q_recv.at[at], device(tx, tz, y, c))

    for load in loads:
        load.wait()
    delta = jnp.zeros((16, ROWS), F32)
    for h in range(16):
        cols = pl.ds(h * HD, HD)
        prod = g_v[:, cols].astype(F32) * o_v[:, cols].astype(F32)
        high = prod.astype(BF16)
        low = (prod - high.astype(F32)).astype(BF16)
        pick = jnp.where(lax.broadcasted_iota(jnp.int32, (16, HD), 0) == h, 1.0, 0.0).astype(BF16)
        delta = delta + (nt(pick, high) + nt(pick, low))
    for h in range(8):
        aux_v[h, 0:2, :] = lse_ref[2 * h : 2 * h + 2, :] * log2e
        aux_v[h, 2:4, :] = delta[2 * h : 2 * h + 2, :]
        aux_v[h, 4:8, :] = jnp.zeros((4, ROWS), F32)
    a_copies = []
    for j, (dx, dz) in enumerate(CHUNKS):
        tx, tz = (x + dx) % NX, (z + dz) % 2
        for dc in range(2):
            src, dst, at = aux_v.at[2 * tx + tz], auxh_ref.at[2 * (2 * x + z) + c], 2 * j + dc
            if at == 0:
                a_copies.append(keep(src, dst, a_recv.at[at]))
            else:
                a_copies.append(send(src, dst, a_send.at[at], a_recv.at[at], device(tx, tz, y, (c + dc) % 2)))

    passed = {}

    def chunk_of(j):
        dx, dz = CHUNKS[j]
        return 2 * ((x + NX - dx) % NX) + (z + 2 - dz) % 2

    def pass_on(j):
        for kind, out in enumerate((qh_v, gh_v)):
            if j == 0:
                q_copies[j, kind].wait()
            else:
                q_copies[j, kind].wait_recv()
            rows = out.at[chunk_of(j), rows_at(c * ROWS, ROWS), :]
            at = 2 * j + kind
            passed[j, kind] = send(rows, rows, s_send.at[at], s_recv.at[at], sibling)

    second = {}
    for n, dx in enumerate(ORDER):
        for j in PASS[n]:
            pass_on(j)
        for way, (plane, to) in enumerate((((y + 3) % NY, up), ((y + 1) % NY, down))):
            first[way, dx].wait_recv()
            if dx == 0:
                own_first[way].wait_recv()
            at = way * NX + dx
            half = kv_ref.at[block(plane, dx)].at[:, pl.ds(way * HD, HD)]
            second[way, dx] = send(half, half, y2_send.at[at], y2_recv.at[at], to)

    for n, copy in enumerate(a_copies):
        if n == 0:
            copy.wait()
        else:
            copy.wait_recv()
    outs = []
    for j in range(len(CHUNKS) + 1):
        if j < len(CHUNKS) and (j, 0) not in passed:
            pass_on(j)
        if j > 0:
            i = chunk_of(j - 1)
            for kind in range(2):
                passed[j - 1, kind].wait_recv()
            for h in range(2):
                rows = slice(h * QT, (h + 1) * QT)
                for whole, split, turned in ((qh_v, q2_v, qt_v), (gh_v, g2_v, gt_v)):
                    part = whole[i, :, h * HD : (h + 1) * HD]
                    split[i, rows, :] = part
                    turned[i, :, rows] = part.T
            for n, (src, dst) in enumerate(
                ((q2_v, q2_ref), (g2_v, g2_ref), (qt_v, qt_ref), (gt_v, gt_ref))
            ):
                outs.append(keep(src.at[i], dst.at[i], out_sem.at[j - 1, n]))

    for copy in second.values():
        copy.wait_recv()
    for copy in sends:
        copy.wait_send()
    for copy in outs:
        copy.wait()


def gather(q, k, v, o, g, lse):
    hbm = pl.BlockSpec(memory_space=pl.ANY)
    dma = pltpu.SemaphoreType.DMA
    split = (8, 2 * QT, HD)
    turned = (8, HD, 2 * QT)
    return pl.pallas_call(
        gather_kernel,
        out_shape=tuple(
            jax.ShapeDtypeStruct(shape, kind)
            for shape, kind in (
                (split, BF16), (split, BF16), (turned, BF16), (turned, BF16), ((16, 8, ROWS), F32),
                ((NY, 2, 2, KT, 2 * HD), BF16),
            )
        ),
        in_specs=[hbm] * 5 + [pl.BlockSpec(memory_space=pltpu.VMEM)],
        out_specs=(hbm,) * 6,
        scratch_shapes=[
            pltpu.VMEM((ROWS, 2048), BF16),
            pltpu.VMEM((ROWS, 2048), BF16),
            pltpu.VMEM((8, 8, ROWS), F32),
            pltpu.VMEM((8, QT, 2 * HD), BF16),
            pltpu.VMEM((8, QT, 2 * HD), BF16),
            pltpu.VMEM(split, BF16),
            pltpu.VMEM(split, BF16),
            pltpu.VMEM(turned, BF16),
            pltpu.VMEM(turned, BF16),
            dma((2,)),
            dma((16,)), dma((16,)),
            dma((10,)), dma((10,)),
            dma((8,)), dma((8,)),
            dma((16,)), dma((16,)),
            dma((16,)), dma((16,)),
            dma((16,)), dma((16,)),
            dma((8, 4)),
        ],
        compiler_params=pltpu.CompilerParams(collective_id=0, has_side_effects=True, vmem_limit_bytes=VMEM_LIMIT),
        name="gather_heads",
    )(q, k, v, o, g, lse)


def nt(a, b):
    return lax.dot_general(a, b, (((1,), (1,)), ((), ())), preferred_element_type=F32)


def nn(a, b):
    return jnp.dot(a, b, preferred_element_type=F32)


def tile_kernel(
    order_ref, lens_ref, q2_ref, g2_ref, qt_ref, gt_ref, aux_ref, kv_ref,
    dq_ref, dkv_ref,
    q_v, g_v, qt_v, gt_v, aux_v, lb_v, db_v, kv_v, acc_q, acc_k, acc_v, dq_v, dkv_v,
    p_a, p_b, ds_a, ds_b, tile_list, cut_list, sems,
):
    x, z, y, c = place()
    loads = [
        pltpu.make_async_copy(src, dst, sems.at[n])
        for n, (src, dst) in enumerate(
            (
                (aux_ref, aux_v), (kv_ref, kv_v), (q2_ref, q_v), (g2_ref, g_v), (qt_ref, qt_v), (gt_ref, gt_v),
            )
        )
    ]
    for load in loads:
        load.start()
    starts = [lens_ref[0], lens_ref[0] + lens_ref[1], lens_ref[0] + lens_ref[1] + lens_ref[2]]

    def low_of(p):
        low = jnp.zeros_like(p)
        for start in starts:
            low = jnp.where(p >= start, start, low)
        return low

    base = [order_ref[2 * i + y // 2] * BLK + (y % 2) * QT for i in range(8)]
    first_low = [low_of(base[i]) for i in range(8)]
    last_low = [low_of(base[i] + (QT - 1)) for i in range(8)]

    def list_slot(slot, counts):
        key = order_ref[slot] * BLK + ((x + c + slot // 2) % 2) * KT
        wholes, cuts = counts
        for i in range(8):
            needed = jnp.logical_and(key < base[i] + QT, key + KT > first_low[i])
            whole = jnp.logical_and(key + KT <= base[i] + 1, key >= last_low[i])
            entry = slot * 8 + i
            tile_list[wholes] = entry
            cut_list[cuts] = entry
            wholes = wholes + jnp.logical_and(needed, whole).astype(jnp.int32)
            cuts = cuts + jnp.logical_and(needed, jnp.logical_not(whole)).astype(jnp.int32)
        return wholes, cuts

    def prepare(slot, counts):
        turned = aux_v[slot].T
        for h in range(2):
            rows = pl.ds(pl.multiple_of(h * QT + (slot % 2) * ROWS, ROWS), ROWS)
            lb_v[slot // 2, rows, :] = jnp.broadcast_to(turned[:, h : h + 1], (ROWS, HD))
            db_v[slot // 2, rows, :] = jnp.broadcast_to(turned[:, 2 + h : 3 + h], (ROWS, HD))
            acc_q[slot // 2, rows, :] = jnp.zeros((ROWS, HD), F32)
        acc_k[slot] = jnp.zeros((HD, KT), F32)
        acc_v[slot] = jnp.zeros((HD, KT), F32)
        return list_slot(slot, counts)

    loads[0].wait()
    wholes, cuts = lax.fori_loop(0, 16, prepare, (0, 0), unroll=16)

    def append(n, _):
        tile_list[wholes + n] = cut_list[n]
        return 0

    lax.fori_loop(0, cuts, append, 0)
    count = wholes + cuts
    for n in range(2):
        tile_list[count + n] = 0
    pairs = (count + 1) // 2
    last = jnp.maximum(2 * pairs - 1, 1)

    def keys(t):
        return kv_v[tile_list[t] // 8, :, 0:HD]

    def values(t):
        return kv_v[tile_list[t] // 8, :, HD : 2 * HD]

    def weigh(t, p_ref, ds_ref, cut):
        i, slot = tile_list[t] % 8, tile_list[t] // 8
        if cut:
            query_base = order_ref[2 * i + y // 2] * BLK + (y % 2) * QT
            at = order_ref[slot] * BLK + ((x + c + slot // 2) % 2) * KT - query_base
            at = jnp.where(t < count, at, 1 << 20)
        step = STEP
        held = {}

        def score(n):
            rows = slice(n * MR, (n + 1) * MR)
            held[n] = (nt(q_v[i, rows, :], keys(t)), nt(g_v[i, rows, :], values(t)))

        def piece(r):
            n, o = r // MR, r % MR
            raw, dprob = held[n][0][o : o + step], held[n][1][o : o + step]
            lse = lb_v[i, r : r + step, :]
            delta = db_v[i, r : r + step, :]
            lse = jnp.concatenate([lse] * (KT // HD), axis=1)
            delta = jnp.concatenate([delta] * (KT // HD), axis=1)
            th = jnp.tanh(raw * (score_scale / softcap))
            p = jnp.exp2(th * (softcap * log2e) - lse)
            if cut:
                row = lax.broadcasted_iota(jnp.int32, (step, HD), 0) + r % QT
                low = low_of(row + query_base) - query_base
                row = jnp.concatenate([row] * (KT // HD), axis=1)
                low = jnp.concatenate([low] * (KT // HD), axis=1)
                key = lax.broadcasted_iota(jnp.int32, (step, KT), 1) + at
                p = jnp.where((key <= row) & (key >= low), p, 0.0)
            ds = p * (dprob - delta) * ((1.0 - th * th) * score_scale)
            p_ref[r : r + step, :] = p.astype(BF16)
            ds_ref[r : r + step, :] = ds.astype(BF16)

        count_m = 2 * QT // MR
        out = [partial(score, 0)]
        for n in range(count_m):
            if n + 1 < count_m:
                out.append(partial(score, n + 1))
            out += [partial(piece, r) for r in range(n * MR, (n + 1) * MR, step)]
        return out

    def gradients(t, p_ref, ds_ref):
        i, slot = tile_list[t] % 8, tile_list[t] // 8

        def key_piece(out, left, right):
            out[slot] += nn(left[i], right[...])

        def query_piece(h):
            rows = slice(h * QT, (h + 1) * QT)
            acc_q[i, rows, :] += nn(ds_ref[rows, :], keys(t))

        return [
            partial(key_piece, acc_v, gt_v, p_ref),
            partial(key_piece, acc_k, qt_v, ds_ref),
            partial(query_piece, 0),
            partial(query_piece, 1),
        ]

    def run(*lists):
        marked = [((n + 0.5) / len(pieces), m, piece) for m, pieces in enumerate(lists) for n, piece in enumerate(pieces)]
        for _, _, piece in sorted(marked, key=lambda entry: entry[:2]):
            piece()

    def step(t, old, new, cut):
        run(weigh(jnp.minimum(t + 1, last), *new, cut), gradients(t, *old))

    def pair(n, _):
        def steps(cut):
            step(2 * n, (p_a, ds_a), (p_b, ds_b), cut)
            step(2 * n + 1, (p_b, ds_b), (p_a, ds_a), cut)

        whole = 2 * n + 2 < wholes
        pl.when(whole)(lambda: steps(False))
        pl.when(jnp.logical_not(whole))(lambda: steps(True))
        return 0

    for load in loads[1:4]:
        load.wait()
    run(weigh(0, p_a, ds_a, True))
    for load in loads[4:]:
        load.wait()

    lax.fori_loop(0, pairs, pair, 0)

    outs = [pltpu.make_async_copy(dq_v, dq_ref, sems.at[0])]
    for d in range(NY):
        plane = (y + d) % NY
        for q in range(4):
            slot = 4 * plane + 2 * ((c + q // 2) % 2) + q % 2
            dkv_v[d, q, 0] = acc_k[slot].astype(BF16)
            dkv_v[d, q, 1] = acc_v[slot].astype(BF16)
        outs.append(pltpu.make_async_copy(dkv_v.at[d], dkv_ref.at[d], sems.at[1 + d]))
        outs[-1].start()
    for i in range(8):
        for h in range(2):
            dq_v[h, i] = acc_q[i, h * QT : (h + 1) * QT, :].astype(BF16)
    outs[0].start()
    for out in outs:
        out.wait()


def tiles(order, lens, *arrays):
    smem = pl.BlockSpec(memory_space=pltpu.SMEM)
    hbm = pl.BlockSpec(memory_space=pl.ANY)
    split = (8, 2 * QT, HD)
    turned = (8, HD, 2 * QT)
    narrow = pltpu.VMEM((2 * QT, KT), BF16)
    listed = pltpu.SMEM((136,), jnp.int32)
    return pl.pallas_call(
        tile_kernel,
        out_shape=(
            jax.ShapeDtypeStruct((2, 8, QT, HD), BF16),
            jax.ShapeDtypeStruct((NY, 4, 2, HD, KT), BF16),
        ),
        in_specs=[smem, smem] + [hbm] * len(arrays),
        out_specs=(hbm, hbm),
        scratch_shapes=[
            pltpu.VMEM(split, BF16),
            pltpu.VMEM(split, BF16),
            pltpu.VMEM(turned, BF16),
            pltpu.VMEM(turned, BF16),
            pltpu.VMEM((16, 8, ROWS), F32),
            pltpu.VMEM(split, F32),
            pltpu.VMEM(split, F32),
            pltpu.VMEM((16, KT, 2 * HD), BF16),
            pltpu.VMEM(split, F32),
            pltpu.VMEM((16, HD, KT), F32),
            pltpu.VMEM((16, HD, KT), F32),
            pltpu.VMEM((2, 8, QT, HD), BF16),
            pltpu.VMEM((NY, 4, 2, HD, KT), BF16),
            narrow, narrow, narrow, narrow,
            listed, listed,
            pltpu.SemaphoreType.DMA((7,)),
        ],
        compiler_params=pltpu.CompilerParams(vmem_limit_bytes=VMEM_LIMIT),
        name="tiles",
    )(order, lens, *arrays)


SLOTS = (3, 1, 2, 0)


def scatter_kernel(
    dq_ref, dkv_ref,
    dq_out, dk_out, dv_out,
    own, land2, send1, land1, fin, mine, theirs, dq_v,
    load_sem, mine_sem, sib_send, sib_recv, s2_send, s2_recv, s1_send, s1_recv, f_send, f_recv, q_send, q_recv,
):
    x, z, y, c = place()
    head = 2 * x + z
    loads = [pltpu.make_async_copy(dkv_ref.at[d], own.at[d], load_sem.at[d]) for d in range(NY)]
    mine_load = pltpu.make_async_copy(dq_ref.at[c], mine, mine_sem)
    for load in [mine_load] + loads:
        load.start()
    enter(x, z, y, c)
    sibling = device(x, z, y, 1 - c)
    ways = (device(x, z, (y + 1) % NY, c), device(x, z, (y + 3) % NY, c))
    sends = []

    def send(src, dst, send_sem, recv_sem, to):
        copy = remote(src, dst, send_sem, recv_sem, to)
        copy.start()
        sends.append(copy)
        return copy

    copies2, copies1 = {}, {}
    slot = {dx: 2 * (dx % 2) + ((x + dx) % NX) // 2 for dx in SLOTS}
    for h in SLOTS:
        for part, to in enumerate(ways):
            at = part * 4 + h
            copies2[part, h] = send(dkv_ref.at[2, slot[h], part], land2.at[part, h], s2_send.at[at], s2_recv.at[at], to)
    sib_copy = send(dq_ref.at[1 - c], theirs, sib_send, sib_recv, sibling)
    for h in SLOTS:
        for way, to in enumerate(ways):
            part = 1 - way
            at = (way * 2 + part) * 4 + h
            copies1[way, part, h] = send(
                dkv_ref.at[1 + 2 * way, slot[h], part], land1.at[way, part, h], s1_send.at[at], s1_recv.at[at], to
            )

    mine_load.wait()
    sib_copy.wait_recv()
    q_copies = []
    for dx, dz in CHUNKS:
        tx, tz = (x + dx) % NX, (z + dz) % 2
        i = 2 * tx + tz
        dq_v[i] = (mine[i].astype(F32) + theirs[i].astype(F32)).astype(BF16)
        for dc in range(2):
            tc = (c + dc) % 2
            src = dq_v.at[i, rows_at(tc * ROWS, ROWS), :]
            dst = dq_out.at[:, columns(2 * head + c)]
            at = (dx * 2 + dz) * 2 + dc
            if at == 0:
                copy = pltpu.make_async_copy(src, dst, q_recv.at[at])
                copy.start()
                q_copies.append((True, copy))
            else:
                q_copies.append((False, send(src, dst, q_send.at[at], q_recv.at[at], device(tx, tz, y, tc))))

    for load in loads:
        load.wait()
    for h in SLOTS:
        for way, to in enumerate(ways):
            part = way
            copies2[part, h].wait_recv()
            total = own[1 + 2 * way, slot[h], part].astype(F32) + land2[part, h].astype(F32)
            send1[way, h] = total.astype(BF16)
            at = (way * 2 + part) * 4 + h
            copies1[way, part, h] = send(
                send1.at[way, h], land1.at[way, part, h], s1_send.at[at], s1_recv.at[at], to
            )

    f_copies = []

    def final(dx, part, out, total):
        fin[dx, part] = total.T.astype(BF16)
        for dz in range(2):
            tz = (z + dz) % 2
            src = fin.at[dx, part, rows_at(tz * ROWS, ROWS), :]
            dst = out.at[:, columns(head)]
            at = (dx * 2 + part) * 2 + dz
            if dx == 0 and dz == 0:
                copy = pltpu.make_async_copy(src, dst, f_recv.at[at])
                copy.start()
                f_copies.append((True, copy))
            else:
                to = device((x + dx) % NX, tz, y, (c + dx) % 2)
                f_copies.append((False, send(src, dst, f_send.at[at], f_recv.at[at], to)))

    for dx in SLOTS:
        for part, out in ((0, dk_out), (1, dv_out)):
            for way in range(2):
                copies1[way, part, dx].wait_recv()
            total = own[0, slot[dx], part].astype(F32) + land1[0, part, dx].astype(F32) + land1[1, part, dx].astype(F32)
            final(dx, part, out, total)

    for local, copy in q_copies + f_copies:
        if local:
            copy.wait()
        else:
            copy.wait_recv()
    for copy in sends:
        copy.wait_send()


def scatter(*arrays):
    hbm = pl.BlockSpec(memory_space=pl.ANY)
    dma = pltpu.SemaphoreType.DMA
    return pl.pallas_call(
        scatter_kernel,
        out_shape=(
            jax.ShapeDtypeStruct((ROWS, 2048), BF16),
            jax.ShapeDtypeStruct((ROWS, 1024), BF16),
            jax.ShapeDtypeStruct((ROWS, 1024), BF16),
        ),
        in_specs=[hbm] * len(arrays),
        out_specs=(hbm,) * 3,
        scratch_shapes=[
            pltpu.VMEM((NY, 4, 2, HD, KT), BF16),
            pltpu.VMEM((2, 4, HD, KT), BF16),
            pltpu.VMEM((2, 4, HD, KT), BF16),
            pltpu.VMEM((2, 2, 4, HD, KT), BF16),
            pltpu.VMEM((NX, 2, KT, HD), BF16),
            pltpu.VMEM((8, QT, HD), BF16),
            pltpu.VMEM((8, QT, HD), BF16),
            pltpu.VMEM((8, QT, HD), BF16),
            dma((NY,)), dma,
            dma, dma,
            dma((8,)), dma((8,)),
            dma((16,)), dma((16,)),
            dma((16,)), dma((16,)),
            dma((16,)), dma((16,)),
        ],
        compiler_params=pltpu.CompilerParams(collective_id=1, has_side_effects=True, vmem_limit_bytes=VMEM_LIMIT),
        name="scatter_grads",
    )(*arrays)


def store_kernel(*refs):
    count = len(refs) // 3
    ins, outs, held, (load_sem, store_sem) = refs[:count], refs[count : 2 * count], refs[2 * count : 3 * count], refs[-2:]
    loads = [pltpu.make_async_copy(ins[n], held[n], load_sem.at[n]) for n in range(count)]
    stores = [pltpu.make_async_copy(held[n], outs[n], store_sem.at[n]) for n in range(count)]
    for load in loads:
        load.start()
    for n in range(count):
        loads[n].wait()
        stores[n].start()
    for copy in stores:
        copy.wait()


def store(*arrays):
    hbm = pl.BlockSpec(memory_space=pl.ANY)
    sems = pltpu.SemaphoreType.DMA((len(arrays),))
    return pl.pallas_call(
        store_kernel,
        out_shape=tuple(jax.ShapeDtypeStruct(array.shape, array.dtype) for array in arrays),
        in_specs=[hbm] * len(arrays),
        out_specs=(hbm,) * len(arrays),
        scratch_shapes=[pltpu.VMEM(array.shape, array.dtype) for array in arrays] + [sems, sems],
        compiler_params=pltpu.CompilerParams(vmem_limit_bytes=VMEM_LIMIT),
        name="store_grads",
    )(*arrays)


def body(
    query_states,
    key_states,
    value_states,
    attn_output,
    output_grad,
    logsumexp,
    block_order,
    doc_lengths,
):
    arrays = gather(query_states, key_states, value_states, attn_output, output_grad, logsumexp)
    dq, dkv = tiles(block_order, doc_lengths, *arrays[:-1], arrays[-1].reshape(16, KT, 2 * HD))
    return store(*scatter(dq, dkv))


def solution(mesh):
    placed = (
        P(("pb", "ka"), "ha"),
        P(("ka", "pb"), "ha"),
        P(("ka", "pb"), "ha"),
        P(("pb", "ka"), "ha"),
        P(("pb", "ka"), "ha"),
        P("ha", ("pb", "ka")),
        P("ha"),
        P("ha"),
    )
    return jax.shard_map(
        body,
        mesh=mesh,
        in_specs=placed,
        out_specs=(P(("pb", "ka"), "ha"), P(("ka", "pb"), "ha"), P(("ka", "pb"), "ha")),
        check_vma=False,
    )
```

```python
from functools import partial
import math

import jax
import jax.numpy as jnp
from jax import lax
from jax.experimental import pallas as pl
from jax.experimental.pallas import tpu as pltpu
from jax.sharding import PartitionSpec as P

HD = 128
BLK = 512
ROWS = 128
NX, NY = 4, 4
VMEM_LIMIT = 60 << 20
BF16 = jnp.bfloat16
F32 = jnp.float32

softcap = 50.0
score_scale = 144.0 ** (-0.5)
log2e = math.log2(math.e)

ORDER = (0, 1, 3, 2)
CHUNKS = ((0, 0), (2, 1), (2, 0), (1, 1), (3, 1), (0, 1), (1, 0), (3, 0))
PASS = ((0,), (1,), (2, 3), (4, 5))
QT = 256
KT = 256
STEP = 32


def place():
    pb, ka = lax.axis_index("pb"), lax.axis_index("ka")
    return pb // 2, pb % 2, ka // 2, ka % 2


def device(x, z, y, c):
    return {"pb": 2 * x + z, "ka": 2 * y + c}


def remote(src, dst, send, recv, to):
    return pltpu.make_async_remote_copy(
        src_ref=src,
        dst_ref=dst,
        send_sem=send,
        recv_sem=recv,
        device_id=to,
        device_id_type=pl.DeviceIdType.MESH,
    )


def enter(x, z, y, c):
    barrier = pltpu.get_barrier_semaphore()
    for dx in range(NX):
        for dz in range(2):
            for dc in range(2):
                if (dx, dz, dc) != (0, 0, 0):
                    to = device((x + dx) % NX, (z + dz) % 2, y, (c + dc) % 2)
                    pl.semaphore_signal(barrier, inc=1, device_id=to, device_id_type=pl.DeviceIdType.MESH)
    for dy in (1, 3):
        to = device(x, z, (y + dy) % NY, c)
        pl.semaphore_signal(barrier, inc=1, device_id=to, device_id_type=pl.DeviceIdType.MESH)
    pl.semaphore_wait(barrier, 17)


def columns(head, count=1):
    return pl.ds(pl.multiple_of(head * HD, HD), count * HD)


def rows_at(start, count):
    return pl.ds(pl.multiple_of(start, ROWS), count)


def gather_kernel(
    q_ref, k_ref, v_ref, o_ref, g_ref, lse_ref,
    qh_ref, gh_ref, auxh_ref, kv_ref,
    o_v, g_v, aux_v,
    load_sem, kv_send, kv_recv, y_send, y_recv, y2_send, y2_recv, q_send, q_recv, s_send, s_recv,
    a_send, a_recv,
):
    x, z, y, c = place()
    loads = [
        pltpu.make_async_copy(o_ref, o_v, load_sem.at[0]),
        pltpu.make_async_copy(g_ref, g_v, load_sem.at[1]),
    ]
    for load in loads:
        load.start()
    enter(x, z, y, c)

    sibling = device(x, z, y, 1 - c)
    up, down = device(x, z, (y + 1) % NY, c), device(x, z, (y + 3) % NY, c)
    sends = []

    def send(src, dst, send_sem, recv_sem, to):
        copy = remote(src, dst, send_sem, recv_sem, to)
        copy.start()
        sends.append(copy)
        return copy

    def keep(src, dst, sem):
        copy = pltpu.make_async_copy(src, dst, sem)
        copy.start()
        return copy

    kv_copies = {}
    for dx, dz in ((0, 0), (0, 1), (1, 0), (3, 0), (1, 1), (3, 1), (2, 0), (2, 1)):
            tx, tz = (x + dx) % NX, (z + dz) % 2
            for part, ref in enumerate((k_ref, v_ref)):
                src = ref.at[:, columns(2 * tx + tz)]
                dst = kv_ref.at[y, c, x // 2, rows_at(z * ROWS, ROWS), pl.ds(part * HD, HD)]
                at = (dx * 2 + dz) * 2 + part
                if at < 2:
                    kv_copies[dx, dz, part] = keep(src, dst, kv_recv.at[at])
                else:
                    to = device(tx, tz, y, (c + dx) % 2)
                    kv_copies[dx, dz, part] = send(src, dst, kv_send.at[at], kv_recv.at[at], to)

    own_rows = kv_ref.at[y, c, x // 2, rows_at(z * ROWS, ROWS), :]
    other_rows = kv_ref.at[y, c, x // 2, rows_at((1 - z) * ROWS, ROWS), :]
    kv_copies[0, 0, 0].wait()
    kv_copies[0, 0, 1].wait()
    own_first = [
        send(own_rows, own_rows, y_send.at[8 + way], y_recv.at[8 + way], to) for way, to in enumerate((up, down))
    ]

    def block(plane, dx):
        return plane, (c + dx) % 2, ((x + NX - dx) % NX) // 2

    first, q_copies = {}, {}
    for dx in ORDER:
        for dz in range(2):
            for part in range(2):
                if dx != 0 or dz != 0:
                    kv_copies[dx, dz, part].wait_recv()
        rows = other_rows if dx == 0 else kv_ref.at[block(y, dx)]
        for way, to in ((0, up), (1, down)):
            at = way * NX + dx
            first[way, dx] = send(rows, rows, y_send.at[at], y_recv.at[at], to)
        for j, (jx, jz) in enumerate(CHUNKS):
            if dx != 0:
                continue
            tx, tz = (x + jx) % NX, (z + jz) % 2
            for kind, (ref, out) in enumerate(((q_ref, qh_ref), (g_ref, gh_ref))):
                src = ref.at[:, columns(2 * (2 * tx + tz), 2)]
                dst = out.at[2 * x + z, rows_at(c * ROWS, ROWS), :]
                at = 2 * j + kind
                if j == 0:
                    q_copies[j, kind] = keep(src, dst, q_recv.at[at])
                else:
                    q_copies[j, kind] = send(src, dst, q_send.at[at], q_recv.at[at], device(tx, tz, y, c))

    for load in loads:
        load.wait()
    delta = jnp.zeros((16, ROWS), F32)
    for h in range(16):
        cols = pl.ds(h * HD, HD)
        prod = g_v[:, cols].astype(F32) * o_v[:, cols].astype(F32)
        high = prod.astype(BF16)
        low = (prod - high.astype(F32)).astype(BF16)
        pick = jnp.where(lax.broadcasted_iota(jnp.int32, (16, HD), 0) == h, 1.0, 0.0).astype(BF16)
        delta = delta + (nt(pick, high) + nt(pick, low))
    for h in range(8):
        aux_v[h, 0:2, :] = lse_ref[2 * h : 2 * h + 2, :] * log2e
        aux_v[h, 2:4, :] = delta[2 * h : 2 * h + 2, :]
        aux_v[h, 4:8, :] = jnp.zeros((4, ROWS), F32)
    a_copies = []
    for j, (dx, dz) in enumerate(CHUNKS):
        tx, tz = (x + dx) % NX, (z + dz) % 2
        for dc in range(2):
            src, dst, at = aux_v.at[2 * tx + tz], auxh_ref.at[2 * (2 * x + z) + c], 2 * j + dc
            if at == 0:
                a_copies.append(keep(src, dst, a_recv.at[at]))
            else:
                a_copies.append(send(src, dst, a_send.at[at], a_recv.at[at], device(tx, tz, y, (c + dc) % 2)))

    passed = {}

    def chunk_of(j):
        dx, dz = CHUNKS[j]
        return 2 * ((x + NX - dx) % NX) + (z + 2 - dz) % 2

    def pass_on(j):
        for kind, out in enumerate((qh_ref, gh_ref)):
            if j == 0:
                q_copies[j, kind].wait()
            else:
                q_copies[j, kind].wait_recv()
            rows = out.at[chunk_of(j), rows_at(c * ROWS, ROWS), :]
            at = 2 * j + kind
            passed[j, kind] = send(rows, rows, s_send.at[at], s_recv.at[at], sibling)

    second = {}
    for n, dx in enumerate(ORDER):
        for j in PASS[n]:
            pass_on(j)
        for way, (plane, to) in enumerate((((y + 3) % NY, up), ((y + 1) % NY, down))):
            first[way, dx].wait_recv()
            if dx == 0:
                own_first[way].wait_recv()
            at = way * NX + dx
            half = kv_ref.at[block(plane, dx)].at[:, pl.ds(way * HD, HD)]
            second[way, dx] = send(half, half, y2_send.at[at], y2_recv.at[at], to)

    for j in range(len(CHUNKS)):
        if (j, 0) not in passed:
            pass_on(j)
    for n, copy in enumerate(a_copies):
        if n == 0:
            copy.wait()
        else:
            copy.wait_recv()
    for copy in passed.values():
        copy.wait_recv()
    for copy in second.values():
        copy.wait_recv()
    for copy in sends:
        copy.wait_send()


def gather(q, k, v, o, g, lse):
    hbm = pl.BlockSpec(memory_space=pl.ANY)
    dma = pltpu.SemaphoreType.DMA
    both = (8, QT, 2 * HD)
    return pl.pallas_call(
        gather_kernel,
        out_shape=tuple(
            jax.ShapeDtypeStruct(shape, kind)
            for shape, kind in (
                (both, BF16), (both, BF16), ((16, 8, ROWS), F32),
                ((NY, 2, 2, KT, 2 * HD), BF16),
            )
        ),
        in_specs=[hbm] * 5 + [pl.BlockSpec(memory_space=pltpu.VMEM)],
        out_specs=(hbm,) * 4,
        scratch_shapes=[
            pltpu.VMEM((ROWS, 2048), BF16),
            pltpu.VMEM((ROWS, 2048), BF16),
            pltpu.VMEM((8, 8, ROWS), F32),
            dma((2,)),
            dma((16,)), dma((16,)),
            dma((10,)), dma((10,)),
            dma((8,)), dma((8,)),
            dma((16,)), dma((16,)),
            dma((16,)), dma((16,)),
            dma((16,)), dma((16,)),
        ],
        compiler_params=pltpu.CompilerParams(collective_id=0, has_side_effects=True, vmem_limit_bytes=VMEM_LIMIT),
        name="gather_heads",
    )(q, k, v, o, g, lse)


def nt(a, b):
    return lax.dot_general(a, b, (((1,), (1,)), ((), ())), preferred_element_type=F32)


def nn(a, b):
    return jnp.dot(a, b, preferred_element_type=F32)


def tile_kernel(
    order_ref, lens_ref, qh_ref, gh_ref, aux_ref, kv_ref,
    dq_ref, dkv_ref,
    q_v, g_v, qt_v, gt_v, aux_v, lb_v, db_v, kv_v, acc_q, acc_k, acc_v, dq_v, dkv_v,
    p_a, p_b, ds_a, ds_b, tile_list, cut_list, sems,
):
    x, z, y, c = place()
    loads = [
        pltpu.make_async_copy(src, dst, sems.at[n])
        for n, (src, dst) in enumerate(
            (
                (aux_ref, aux_v), (qh_ref, q_v), (gh_ref, g_v), (kv_ref, kv_v),
            )
        )
    ]
    for load in loads:
        load.start()
    starts = [lens_ref[0], lens_ref[0] + lens_ref[1], lens_ref[0] + lens_ref[1] + lens_ref[2]]

    def low_of(p):
        low = jnp.zeros_like(p)
        for start in starts:
            low = jnp.where(p >= start, start, low)
        return low

    base = [order_ref[2 * i + y // 2] * BLK + (y % 2) * QT for i in range(8)]
    first_low = [low_of(base[i]) for i in range(8)]
    last_low = [low_of(base[i] + (QT - 1)) for i in range(8)]

    def list_slot(slot, counts):
        key = order_ref[slot] * BLK + ((x + c + slot // 2) % 2) * KT
        wholes, cuts = counts
        for i in range(8):
            needed = jnp.logical_and(key < base[i] + QT, key + KT > first_low[i])
            whole = jnp.logical_and(key + KT <= base[i] + 1, key >= last_low[i])
            entry = slot * 8 + i
            tile_list[wholes] = entry
            cut_list[cuts] = entry
            wholes = wholes + jnp.logical_and(needed, whole).astype(jnp.int32)
            cuts = cuts + jnp.logical_and(needed, jnp.logical_not(whole)).astype(jnp.int32)
        return wholes, cuts

    def prepare(slot, counts):
        turned = aux_v[slot].T
        for h in range(2):
            rows = pl.ds(pl.multiple_of(h * QT + (slot % 2) * ROWS, ROWS), ROWS)
            lb_v[slot // 2, rows, :] = jnp.broadcast_to(turned[:, h : h + 1], (ROWS, HD))
            db_v[slot // 2, rows, :] = jnp.broadcast_to(turned[:, 2 + h : 3 + h], (ROWS, HD))
            acc_q[slot // 2, rows, :] = jnp.zeros((ROWS, HD), F32)
        acc_k[slot] = jnp.zeros((HD, KT), F32)
        acc_v[slot] = jnp.zeros((HD, KT), F32)
        return list_slot(slot, counts)

    loads[0].wait()
    wholes, cuts = lax.fori_loop(0, 16, prepare, (0, 0), unroll=16)

    def append(n, _):
        tile_list[wholes + n] = cut_list[n]
        return 0

    lax.fori_loop(0, cuts, append, 0)
    count = wholes + cuts
    for n in range(2):
        tile_list[count + n] = 0
    pairs = (count + 1) // 2
    last = jnp.maximum(2 * pairs - 1, 1)

    def keys(t):
        return kv_v[tile_list[t] // 8, :, 0:HD]

    def values(t):
        return kv_v[tile_list[t] // 8, :, HD : 2 * HD]

    def weigh(t, p_ref, ds_ref, cut):
        i, slot = tile_list[t] % 8, tile_list[t] // 8
        if cut:
            query_base = order_ref[2 * i + y // 2] * BLK + (y % 2) * QT
            at = order_ref[slot] * BLK + ((x + c + slot // 2) % 2) * KT - query_base
            at = jnp.where(t < count, at, 1 << 20)
        step = STEP
        held = {}

        def score(n):
            cols = slice(n * HD, (n + 1) * HD)
            held[n] = (nt(q_v[i, :, cols], keys(t)), nt(g_v[i, :, cols], values(t)))

        def piece(r):
            n, o = r // QT, r % QT
            raw, dprob = held[n][0][o : o + step], held[n][1][o : o + step]
            lse = lb_v[i, r : r + step, :]
            delta = db_v[i, r : r + step, :]
            lse = jnp.concatenate([lse] * (KT // HD), axis=1)
            delta = jnp.concatenate([delta] * (KT // HD), axis=1)
            th = jnp.tanh(raw * (score_scale / softcap))
            p = jnp.exp2(th * (softcap * log2e) - lse)
            if cut:
                row = lax.broadcasted_iota(jnp.int32, (step, HD), 0) + r % QT
                low = low_of(row + query_base) - query_base
                row = jnp.concatenate([row] * (KT // HD), axis=1)
                low = jnp.concatenate([low] * (KT // HD), axis=1)
                key = lax.broadcasted_iota(jnp.int32, (step, KT), 1) + at
                p = jnp.where((key <= row) & (key >= low), p, 0.0)
            ds = p * (dprob - delta) * ((1.0 - th * th) * score_scale)
            p_ref[r : r + step, :] = p.astype(BF16)
            ds_ref[r : r + step, :] = ds.astype(BF16)

        return [partial(score, 0), partial(score, 1)] + [partial(piece, r) for r in range(0, 2 * QT, step)]

    def gradients(t, p_ref, ds_ref):
        i, slot = tile_list[t] % 8, tile_list[t] // 8

        def key_piece(out, left, right):
            out[slot] += nn(left[i], right[...])

        def query_piece(h):
            rows = slice(h * QT, (h + 1) * QT)
            acc_q[i, rows, :] += nn(ds_ref[rows, :], keys(t))

        return [
            partial(key_piece, acc_v, gt_v, p_ref),
            partial(key_piece, acc_k, qt_v, ds_ref),
            partial(query_piece, 0),
            partial(query_piece, 1),
        ]

    def run(*lists):
        marked = [((n + 0.5) / len(pieces), m, piece) for m, pieces in enumerate(lists) for n, piece in enumerate(pieces)]
        for _, _, piece in sorted(marked, key=lambda entry: entry[:2]):
            piece()

    def step(t, old, new, cut):
        run(weigh(jnp.minimum(t + 1, last), *new, cut), gradients(t, *old))

    def pair(n, _):
        def steps(cut):
            step(2 * n, (p_a, ds_a), (p_b, ds_b), cut)
            step(2 * n + 1, (p_b, ds_b), (p_a, ds_a), cut)

        whole = 2 * n + 2 < wholes
        pl.when(whole)(lambda: steps(False))
        pl.when(jnp.logical_not(whole))(lambda: steps(True))
        return 0

    for kind, (whole, turned) in enumerate(((q_v, qt_v), (g_v, gt_v))):
        loads[1 + kind].wait()
        for i in range(8):
            for h in range(2):
                turned[i, :, h * QT : (h + 1) * QT] = whole[i, :, h * HD : (h + 1) * HD].T
    loads[3].wait()
    run(weigh(0, p_a, ds_a, True))

    lax.fori_loop(0, pairs, pair, 0)

    outs = [pltpu.make_async_copy(dq_v, dq_ref, sems.at[0])]
    for d in range(NY):
        plane = (y + d) % NY
        for q in range(4):
            slot = 4 * plane + 2 * ((c + q // 2) % 2) + q % 2
            dkv_v[d, q, 0] = acc_k[slot].astype(BF16)
            dkv_v[d, q, 1] = acc_v[slot].astype(BF16)
        outs.append(pltpu.make_async_copy(dkv_v.at[d], dkv_ref.at[d], sems.at[1 + d]))
        outs[-1].start()
    for i in range(8):
        for h in range(2):
            dq_v[h, i] = acc_q[i, h * QT : (h + 1) * QT, :].astype(BF16)
    outs[0].start()
    for out in outs:
        out.wait()


def tiles(order, lens, *arrays):
    smem = pl.BlockSpec(memory_space=pltpu.SMEM)
    hbm = pl.BlockSpec(memory_space=pl.ANY)
    split = (8, 2 * QT, HD)
    turned = (8, HD, 2 * QT)
    narrow = pltpu.VMEM((2 * QT, KT), BF16)
    listed = pltpu.SMEM((136,), jnp.int32)
    return pl.pallas_call(
        tile_kernel,
        out_shape=(
            jax.ShapeDtypeStruct((2, 8, QT, HD), BF16),
            jax.ShapeDtypeStruct((NY, 4, 2, HD, KT), BF16),
        ),
        in_specs=[smem, smem] + [hbm] * len(arrays),
        out_specs=(hbm, hbm),
        scratch_shapes=[
            pltpu.VMEM((8, QT, 2 * HD), BF16),
            pltpu.VMEM((8, QT, 2 * HD), BF16),
            pltpu.VMEM(turned, BF16),
            pltpu.VMEM(turned, BF16),
            pltpu.VMEM((16, 8, ROWS), F32),
            pltpu.VMEM(split, F32),
            pltpu.VMEM(split, F32),
            pltpu.VMEM((16, KT, 2 * HD), BF16),
            pltpu.VMEM(split, F32),
            pltpu.VMEM((16, HD, KT), F32),
            pltpu.VMEM((16, HD, KT), F32),
            pltpu.VMEM((2, 8, QT, HD), BF16),
            pltpu.VMEM((NY, 4, 2, HD, KT), BF16),
            narrow, narrow, narrow, narrow,
            listed, listed,
            pltpu.SemaphoreType.DMA((5,)),
        ],
        compiler_params=pltpu.CompilerParams(vmem_limit_bytes=VMEM_LIMIT),
        name="tiles",
    )(order, lens, *arrays)


SLOTS = (3, 1, 2, 0)


def scatter_kernel(
    dq_ref, dkv_ref,
    dq_out, dk_out, dv_out,
    own, land2, send1, land1, fin, mine, theirs, dq_v,
    load_sem, mine_sem, sib_send, sib_recv, s2_send, s2_recv, s1_send, s1_recv, f_send, f_recv, q_send, q_recv,
):
    x, z, y, c = place()
    head = 2 * x + z
    loads = [pltpu.make_async_copy(dkv_ref.at[d], own.at[d], load_sem.at[d]) for d in range(NY)]
    mine_load = pltpu.make_async_copy(dq_ref.at[c], mine, mine_sem)
    for load in [mine_load] + loads:
        load.start()
    enter(x, z, y, c)
    sibling = device(x, z, y, 1 - c)
    ways = (device(x, z, (y + 1) % NY, c), device(x, z, (y + 3) % NY, c))
    sends = []

    def send(src, dst, send_sem, recv_sem, to):
        copy = remote(src, dst, send_sem, recv_sem, to)
        copy.start()
        sends.append(copy)
        return copy

    copies2, copies1 = {}, {}
    slot = {dx: 2 * (dx % 2) + ((x + dx) % NX) // 2 for dx in SLOTS}
    for h in SLOTS:
        for part, to in enumerate(ways):
            at = part * 4 + h
            copies2[part, h] = send(dkv_ref.at[2, slot[h], part], land2.at[part, h], s2_send.at[at], s2_recv.at[at], to)
    sib_copy = send(dq_ref.at[1 - c], theirs, sib_send, sib_recv, sibling)
    for h in SLOTS:
        for way, to in enumerate(ways):
            part = 1 - way
            at = (way * 2 + part) * 4 + h
            copies1[way, part, h] = send(
                dkv_ref.at[1 + 2 * way, slot[h], part], land1.at[way, part, h], s1_send.at[at], s1_recv.at[at], to
            )

    mine_load.wait()
    sib_copy.wait_recv()
    q_copies = []
    for dx, dz in CHUNKS:
        tx, tz = (x + dx) % NX, (z + dz) % 2
        i = 2 * tx + tz
        dq_v[i] = (mine[i].astype(F32) + theirs[i].astype(F32)).astype(BF16)
        for dc in range(2):
            tc = (c + dc) % 2
            src = dq_v.at[i, rows_at(tc * ROWS, ROWS), :]
            dst = dq_out.at[:, columns(2 * head + c)]
            at = (dx * 2 + dz) * 2 + dc
            if at == 0:
                copy = pltpu.make_async_copy(src, dst, q_recv.at[at])
                copy.start()
                q_copies.append((True, copy))
            else:
                q_copies.append((False, send(src, dst, q_send.at[at], q_recv.at[at], device(tx, tz, y, tc))))

    for load in loads:
        load.wait()
    for h in SLOTS:
        for way, to in enumerate(ways):
            part = way
            copies2[part, h].wait_recv()
            total = own[1 + 2 * way, slot[h], part].astype(F32) + land2[part, h].astype(F32)
            send1[way, h] = total.astype(BF16)
            at = (way * 2 + part) * 4 + h
            copies1[way, part, h] = send(
                send1.at[way, h], land1.at[way, part, h], s1_send.at[at], s1_recv.at[at], to
            )

    f_copies = []

    def final(dx, part, out, total):
        fin[dx, part] = total.T.astype(BF16)
        for dz in range(2):
            tz = (z + dz) % 2
            src = fin.at[dx, part, rows_at(tz * ROWS, ROWS), :]
            dst = out.at[:, columns(head)]
            at = (dx * 2 + part) * 2 + dz
            if dx == 0 and dz == 0:
                copy = pltpu.make_async_copy(src, dst, f_recv.at[at])
                copy.start()
                f_copies.append((True, copy))
            else:
                to = device((x + dx) % NX, tz, y, (c + dx) % 2)
                f_copies.append((False, send(src, dst, f_send.at[at], f_recv.at[at], to)))

    for dx in SLOTS:
        for part, out in ((0, dk_out), (1, dv_out)):
            for way in range(2):
                copies1[way, part, dx].wait_recv()
            total = own[0, slot[dx], part].astype(F32) + land1[0, part, dx].astype(F32) + land1[1, part, dx].astype(F32)
            final(dx, part, out, total)

    for local, copy in q_copies + f_copies:
        if local:
            copy.wait()
        else:
            copy.wait_recv()
    for copy in sends:
        copy.wait_send()


def scatter(*arrays):
    hbm = pl.BlockSpec(memory_space=pl.ANY)
    dma = pltpu.SemaphoreType.DMA
    return pl.pallas_call(
        scatter_kernel,
        out_shape=(
            jax.ShapeDtypeStruct((ROWS, 2048), BF16),
            jax.ShapeDtypeStruct((ROWS, 1024), BF16),
            jax.ShapeDtypeStruct((ROWS, 1024), BF16),
        ),
        in_specs=[hbm] * len(arrays),
        out_specs=(hbm,) * 3,
        scratch_shapes=[
            pltpu.VMEM((NY, 4, 2, HD, KT), BF16),
            pltpu.VMEM((2, 4, HD, KT), BF16),
            pltpu.VMEM((2, 4, HD, KT), BF16),
            pltpu.VMEM((2, 2, 4, HD, KT), BF16),
            pltpu.VMEM((NX, 2, KT, HD), BF16),
            pltpu.VMEM((8, QT, HD), BF16),
            pltpu.VMEM((8, QT, HD), BF16),
            pltpu.VMEM((8, QT, HD), BF16),
            dma((NY,)), dma,
            dma, dma,
            dma((8,)), dma((8,)),
            dma((16,)), dma((16,)),
            dma((16,)), dma((16,)),
            dma((16,)), dma((16,)),
        ],
        compiler_params=pltpu.CompilerParams(collective_id=1, has_side_effects=True, vmem_limit_bytes=VMEM_LIMIT),
        name="scatter_grads",
    )(*arrays)


def store_kernel(*refs):
    count = len(refs) // 3
    ins, outs, held, (load_sem, store_sem) = refs[:count], refs[count : 2 * count], refs[2 * count : 3 * count], refs[-2:]
    loads = [pltpu.make_async_copy(ins[n], held[n], load_sem.at[n]) for n in range(count)]
    stores = [pltpu.make_async_copy(held[n], outs[n], store_sem.at[n]) for n in range(count)]
    for load in loads:
        load.start()
    for n in range(count):
        loads[n].wait()
        stores[n].start()
    for copy in stores:
        copy.wait()


def store(*arrays):
    hbm = pl.BlockSpec(memory_space=pl.ANY)
    sems = pltpu.SemaphoreType.DMA((len(arrays),))
    return pl.pallas_call(
        store_kernel,
        out_shape=tuple(jax.ShapeDtypeStruct(array.shape, array.dtype) for array in arrays),
        in_specs=[hbm] * len(arrays),
        out_specs=(hbm,) * len(arrays),
        scratch_shapes=[pltpu.VMEM(array.shape, array.dtype) for array in arrays] + [sems, sems],
        compiler_params=pltpu.CompilerParams(vmem_limit_bytes=VMEM_LIMIT),
        name="store_grads",
    )(*arrays)


def body(
    query_states,
    key_states,
    value_states,
    attn_output,
    output_grad,
    logsumexp,
    block_order,
    doc_lengths,
):
    arrays = gather(query_states, key_states, value_states, attn_output, output_grad, logsumexp)
    dq, dkv = tiles(block_order, doc_lengths, *arrays[:-1], arrays[-1].reshape(16, KT, 2 * HD))
    return store(*scatter(dq, dkv))


def solution(mesh):
    placed = (
        P(("pb", "ka"), "ha"),
        P(("ka", "pb"), "ha"),
        P(("ka", "pb"), "ha"),
        P(("pb", "ka"), "ha"),
        P(("pb", "ka"), "ha"),
        P("ha", ("pb", "ka")),
        P("ha"),
        P("ha"),
    )
    return jax.shard_map(
        body,
        mesh=mesh,
        in_specs=placed,
        out_specs=(P(("pb", "ka"), "ha"), P(("ka", "pb"), "ha"), P(("ka", "pb"), "ha")),
        check_vma=False,
    )
```

```python
from functools import partial
import math

import jax
import jax.numpy as jnp
from jax import lax
from jax.experimental import pallas as pl
from jax.experimental.pallas import tpu as pltpu
from jax.sharding import PartitionSpec as P

HD = 128
BLK = 512
ROWS = 128
NX, NY = 4, 4
VMEM_LIMIT = 60 << 20
BF16 = jnp.bfloat16
F32 = jnp.float32

softcap = 50.0
score_scale = 144.0 ** (-0.5)
log2e = math.log2(math.e)

ORDER = (0, 1, 3, 2)
CHUNKS = ((0, 0), (2, 1), (2, 0), (1, 1), (3, 1), (0, 1), (1, 0), (3, 0))
PASS = ((0,), (1,), (2, 3), (4, 5))
QT = 256
KT = 256
STEP = 32


def place():
    pb, ka = lax.axis_index("pb"), lax.axis_index("ka")
    return pb // 2, pb % 2, ka // 2, ka % 2


def device(x, z, y, c):
    return {"pb": 2 * x + z, "ka": 2 * y + c}


def remote(src, dst, send, recv, to):
    return pltpu.make_async_remote_copy(
        src_ref=src,
        dst_ref=dst,
        send_sem=send,
        recv_sem=recv,
        device_id=to,
        device_id_type=pl.DeviceIdType.MESH,
    )


def enter(x, z, y, c):
    barrier = pltpu.get_barrier_semaphore()
    for dx in range(NX):
        for dz in range(2):
            for dc in range(2):
                if (dx, dz, dc) != (0, 0, 0):
                    to = device((x + dx) % NX, (z + dz) % 2, y, (c + dc) % 2)
                    pl.semaphore_signal(barrier, inc=1, device_id=to, device_id_type=pl.DeviceIdType.MESH)
    for dy in (1, 3):
        to = device(x, z, (y + dy) % NY, c)
        pl.semaphore_signal(barrier, inc=1, device_id=to, device_id_type=pl.DeviceIdType.MESH)
    pl.semaphore_wait(barrier, 17)


def columns(head, count=1):
    return pl.ds(pl.multiple_of(head * HD, HD), count * HD)


def rows_at(start, count):
    return pl.ds(pl.multiple_of(start, ROWS), count)


def gather_kernel(
    q_ref, k_ref, v_ref, o_ref, g_ref, lse_ref,
    qh_ref, gh_ref, auxh_ref, kv_ref,
    o_v, g_v, aux_v,
    load_sem, kv_send, kv_recv, y_send, y_recv, y2_send, y2_recv, q_send, q_recv, s_send, s_recv,
    a_send, a_recv,
):
    x, z, y, c = place()
    loads = [
        pltpu.make_async_copy(o_ref, o_v, load_sem.at[0]),
        pltpu.make_async_copy(g_ref, g_v, load_sem.at[1]),
    ]
    for load in loads:
        load.start()
    enter(x, z, y, c)

    sibling = device(x, z, y, 1 - c)
    up, down = device(x, z, (y + 1) % NY, c), device(x, z, (y + 3) % NY, c)
    sends = []

    def send(src, dst, send_sem, recv_sem, to):
        copy = remote(src, dst, send_sem, recv_sem, to)
        copy.start()
        sends.append(copy)
        return copy

    def keep(src, dst, sem):
        copy = pltpu.make_async_copy(src, dst, sem)
        copy.start()
        return copy

    kv_copies = {}
    for dx, dz in ((0, 0), (0, 1), (1, 0), (3, 0), (1, 1), (3, 1), (2, 0), (2, 1)):
            tx, tz = (x + dx) % NX, (z + dz) % 2
            for part, ref in enumerate((k_ref, v_ref)):
                src = ref.at[:, columns(2 * tx + tz)]
                dst = kv_ref.at[y, c, x // 2, rows_at(z * ROWS, ROWS), pl.ds(part * HD, HD)]
                at = (dx * 2 + dz) * 2 + part
                if at < 2:
                    kv_copies[dx, dz, part] = keep(src, dst, kv_recv.at[at])
                else:
                    to = device(tx, tz, y, (c + dx) % 2)
                    kv_copies[dx, dz, part] = send(src, dst, kv_send.at[at], kv_recv.at[at], to)

    own_rows = kv_ref.at[y, c, x // 2, rows_at(z * ROWS, ROWS), :]
    other_rows = kv_ref.at[y, c, x // 2, rows_at((1 - z) * ROWS, ROWS), :]
    kv_copies[0, 0, 0].wait()
    kv_copies[0, 0, 1].wait()
    own_first = [
        send(own_rows, own_rows, y_send.at[8 + way], y_recv.at[8 + way], to) for way, to in enumerate((up, down))
    ]

    def block(plane, dx):
        return plane, (c + dx) % 2, ((x + NX - dx) % NX) // 2

    first, q_copies = {}, {}
    for dx in ORDER:
        for dz in range(2):
            for part in range(2):
                if dx != 0 or dz != 0:
                    kv_copies[dx, dz, part].wait_recv()
        rows = other_rows if dx == 0 else kv_ref.at[block(y, dx)]
        for way, to in ((0, up), (1, down)):
            at = way * NX + dx
            first[way, dx] = send(rows, rows, y_send.at[at], y_recv.at[at], to)
        for j, (jx, jz) in enumerate(CHUNKS):
            if dx != 0:
                continue
            tx, tz = (x + jx) % NX, (z + jz) % 2
            for kind, (ref, out) in enumerate(((q_ref, qh_ref), (g_ref, gh_ref))):
                src = ref.at[:, columns(2 * (2 * tx + tz), 2)]
                dst = out.at[2 * x + z, rows_at(c * ROWS, ROWS), :]
                at = 2 * j + kind
                if j == 0:
                    q_copies[j, kind] = keep(src, dst, q_recv.at[at])
                else:
                    q_copies[j, kind] = send(src, dst, q_send.at[at], q_recv.at[at], device(tx, tz, y, c))

    for load in loads:
        load.wait()
    delta = jnp.zeros((16, ROWS), F32)
    for h in range(16):
        cols = pl.ds(h * HD, HD)
        prod = g_v[:, cols].astype(F32) * o_v[:, cols].astype(F32)
        high = prod.astype(BF16)
        low = (prod - high.astype(F32)).astype(BF16)
        pick = jnp.where(lax.broadcasted_iota(jnp.int32, (16, HD), 0) == h, 1.0, 0.0).astype(BF16)
        delta = delta + (nt(pick, high) + nt(pick, low))
    for h in range(8):
        aux_v[h, 0:2, :] = lse_ref[2 * h : 2 * h + 2, :] * log2e
        aux_v[h, 2:4, :] = delta[2 * h : 2 * h + 2, :]
        aux_v[h, 4:8, :] = jnp.zeros((4, ROWS), F32)
    a_copies = []
    for j, (dx, dz) in enumerate(CHUNKS):
        tx, tz = (x + dx) % NX, (z + dz) % 2
        for dc in range(2):
            src, dst, at = aux_v.at[2 * tx + tz], auxh_ref.at[2 * (2 * x + z) + c], 2 * j + dc
            if at == 0:
                a_copies.append(keep(src, dst, a_recv.at[at]))
            else:
                a_copies.append(send(src, dst, a_send.at[at], a_recv.at[at], device(tx, tz, y, (c + dc) % 2)))

    passed = {}

    def chunk_of(j):
        dx, dz = CHUNKS[j]
        return 2 * ((x + NX - dx) % NX) + (z + 2 - dz) % 2

    def pass_on(j):
        for kind, out in enumerate((qh_ref, gh_ref)):
            if j == 0:
                q_copies[j, kind].wait()
            else:
                q_copies[j, kind].wait_recv()
            rows = out.at[chunk_of(j), rows_at(c * ROWS, ROWS), :]
            at = 2 * j + kind
            passed[j, kind] = send(rows, rows, s_send.at[at], s_recv.at[at], sibling)

    second = {}
    for n, dx in enumerate(ORDER):
        for j in PASS[n]:
            pass_on(j)
        for way, (plane, to) in enumerate((((y + 3) % NY, up), ((y + 1) % NY, down))):
            first[way, dx].wait_recv()
            if dx == 0:
                own_first[way].wait_recv()
            at = way * NX + dx
            half = kv_ref.at[block(plane, dx)].at[:, pl.ds(way * HD, HD)]
            second[way, dx] = send(half, half, y2_send.at[at], y2_recv.at[at], to)

    for j in range(len(CHUNKS)):
        if (j, 0) not in passed:
            pass_on(j)
    for n, copy in enumerate(a_copies):
        if n == 0:
            copy.wait()
        else:
            copy.wait_recv()
    for copy in passed.values():
        copy.wait_recv()
    for copy in second.values():
        copy.wait_recv()
    for copy in sends:
        copy.wait_send()


def gather(q, k, v, o, g, lse):
    hbm = pl.BlockSpec(memory_space=pl.ANY)
    dma = pltpu.SemaphoreType.DMA
    both = (8, QT, 2 * HD)
    return pl.pallas_call(
        gather_kernel,
        out_shape=tuple(
            jax.ShapeDtypeStruct(shape, kind)
            for shape, kind in (
                (both, BF16), (both, BF16), ((16, 8, ROWS), F32),
                ((NY, 2, 2, KT, 2 * HD), BF16),
            )
        ),
        in_specs=[hbm] * 5 + [pl.BlockSpec(memory_space=pltpu.VMEM)],
        out_specs=(hbm,) * 4,
        scratch_shapes=[
            pltpu.VMEM((ROWS, 2048), BF16),
            pltpu.VMEM((ROWS, 2048), BF16),
            pltpu.VMEM((8, 8, ROWS), F32),
            dma((2,)),
            dma((16,)), dma((16,)),
            dma((10,)), dma((10,)),
            dma((8,)), dma((8,)),
            dma((16,)), dma((16,)),
            dma((16,)), dma((16,)),
            dma((16,)), dma((16,)),
        ],
        compiler_params=pltpu.CompilerParams(collective_id=0, has_side_effects=True, vmem_limit_bytes=VMEM_LIMIT),
        name="gather_heads",
    )(q, k, v, o, g, lse)


def nt(a, b):
    return lax.dot_general(a, b, (((1,), (1,)), ((), ())), preferred_element_type=F32)


def nn(a, b):
    return jnp.dot(a, b, preferred_element_type=F32)


def tile_kernel(
    order_ref, lens_ref, qh_ref, gh_ref, aux_ref, kv_ref,
    dq_ref, dkv_ref,
    q_v, g_v, qt_v, gt_v, aux_v, lb_v, db_v, kv_v, acc_q, acc_k, acc_v, dq_v, dkv_v,
    p_a, p_b, ds_a, ds_b, tile_list, cut_list, sems,
):
    x, z, y, c = place()
    loads = [
        pltpu.make_async_copy(src, dst, sems.at[n])
        for n, (src, dst) in enumerate(
            (
                (aux_ref, aux_v), (qh_ref, q_v), (gh_ref, g_v), (kv_ref, kv_v),
            )
        )
    ]
    for load in loads:
        load.start()
    starts = [lens_ref[0], lens_ref[0] + lens_ref[1], lens_ref[0] + lens_ref[1] + lens_ref[2]]

    def low_of(p):
        low = jnp.zeros_like(p)
        for start in starts:
            low = jnp.where(p >= start, start, low)
        return low

    base = [order_ref[2 * i + y // 2] * BLK + (y % 2) * QT for i in range(8)]
    first_low = [low_of(base[i]) for i in range(8)]
    last_low = [low_of(base[i] + (QT - 1)) for i in range(8)]

    def list_slot(slot, counts):
        key = order_ref[slot] * BLK + ((x + c + slot // 2) % 2) * KT
        wholes, cuts = counts
        for i in range(8):
            needed = jnp.logical_and(key < base[i] + QT, key + KT > first_low[i])
            whole = jnp.logical_and(key + KT <= base[i] + 1, key >= last_low[i])
            entry = slot * 8 + i
            tile_list[wholes] = entry
            cut_list[cuts] = entry
            wholes = wholes + jnp.logical_and(needed, whole).astype(jnp.int32)
            cuts = cuts + jnp.logical_and(needed, jnp.logical_not(whole)).astype(jnp.int32)
        return wholes, cuts

    def prepare(slot, counts):
        turned = aux_v[slot].T
        for h in range(2):
            rows = pl.ds(pl.multiple_of(h * QT + (slot % 2) * ROWS, ROWS), ROWS)
            lb_v[slot // 2, rows, :] = jnp.broadcast_to(turned[:, h : h + 1], (ROWS, HD))
            db_v[slot // 2, rows, :] = jnp.broadcast_to(turned[:, 2 + h : 3 + h], (ROWS, HD))
            acc_q[slot // 2, rows, :] = jnp.zeros((ROWS, HD), F32)
        acc_k[slot] = jnp.zeros((HD, KT), F32)
        acc_v[slot] = jnp.zeros((HD, KT), F32)
        return list_slot(slot, counts)

    loads[0].wait()
    wholes, cuts = lax.fori_loop(0, 16, prepare, (0, 0), unroll=16)

    def append(n, _):
        tile_list[wholes + n] = cut_list[n]
        return 0

    lax.fori_loop(0, cuts, append, 0)
    count = wholes + cuts
    for n in range(2):
        tile_list[count + n] = 0
    pairs = (count + 1) // 2
    last = jnp.maximum(2 * pairs - 1, 1)

    def keys(t):
        return kv_v[tile_list[t] // 8, :, 0:HD]

    def values(t):
        return kv_v[tile_list[t] // 8, :, HD : 2 * HD]

    def weigh(t, p_ref, ds_ref, cut):
        i, slot = tile_list[t] % 8, tile_list[t] // 8
        if cut:
            query_base = order_ref[2 * i + y // 2] * BLK + (y % 2) * QT
            at = order_ref[slot] * BLK + ((x + c + slot // 2) % 2) * KT - query_base
            at = jnp.where(t < count, at, 1 << 20)
        step = STEP
        held = {}

        def score(n):
            cols = slice(n * HD, (n + 1) * HD)
            held[n] = (nt(q_v[i, :, cols], keys(t)), nt(g_v[i, :, cols], values(t)))

        def piece(r):
            n, o = r // QT, r % QT
            raw, dprob = held[n][0][o : o + step], held[n][1][o : o + step]
            lse = lb_v[i, r : r + step, :]
            delta = db_v[i, r : r + step, :]
            lse = jnp.concatenate([lse] * (KT // HD), axis=1)
            delta = jnp.concatenate([delta] * (KT // HD), axis=1)
            th = jnp.tanh(raw * (score_scale / softcap))
            p = jnp.exp2(th * (softcap * log2e) - lse)
            if cut:
                row = lax.broadcasted_iota(jnp.int32, (step, HD), 0) + r % QT
                low = low_of(row + query_base) - query_base
                row = jnp.concatenate([row] * (KT // HD), axis=1)
                low = jnp.concatenate([low] * (KT // HD), axis=1)
                key = lax.broadcasted_iota(jnp.int32, (step, KT), 1) + at
                p = jnp.where((key <= row) & (key >= low), p, 0.0)
            ds = p * (dprob - delta) * ((1.0 - th * th) * score_scale)
            p_ref[r : r + step, :] = p.astype(BF16)
            ds_ref[r : r + step, :] = ds.astype(BF16)

        return [partial(score, 0)] + [partial(piece, r) for r in range(0, QT // 2, step)] + [partial(score, 1)] + [partial(piece, r) for r in range(QT // 2, 2 * QT, step)]

    def gradients(t, p_ref, ds_ref):
        i, slot = tile_list[t] % 8, tile_list[t] // 8

        def key_piece(out, left, right):
            out[slot] += nn(left[i], right[...])

        def query_piece(h):
            rows = slice(h * QT, (h + 1) * QT)
            acc_q[i, rows, :] += nn(ds_ref[rows, :], keys(t))

        return [
            partial(key_piece, acc_v, gt_v, p_ref),
            partial(key_piece, acc_k, qt_v, ds_ref),
            partial(query_piece, 0),
            partial(query_piece, 1),
        ]

    def run(*lists):
        marked = [((n + 0.5) / len(pieces), m, piece) for m, pieces in enumerate(lists) for n, piece in enumerate(pieces)]
        for _, _, piece in sorted(marked, key=lambda entry: entry[:2]):
            piece()

    def step(t, old, new, cut):
        run(weigh(jnp.minimum(t + 1, last), *new, cut), gradients(t, *old))

    def pair(n, _):
        def steps(cut):
            step(2 * n, (p_a, ds_a), (p_b, ds_b), cut)
            step(2 * n + 1, (p_b, ds_b), (p_a, ds_a), cut)

        whole = 2 * n + 2 < wholes
        pl.when(whole)(lambda: steps(False))
        pl.when(jnp.logical_not(whole))(lambda: steps(True))
        return 0

    def turn(whole, turned, i):
        for h in range(2):
            turned[i, :, h * QT : (h + 1) * QT] = whole[i, :, h * HD : (h + 1) * HD].T

    for load in loads[1:]:
        load.wait()
    run(
        weigh(0, p_a, ds_a, True),
        [partial(turn, whole, turned, i) for whole, turned in ((q_v, qt_v), (g_v, gt_v)) for i in range(8)],
    )

    lax.fori_loop(0, pairs, pair, 0)

    outs = [pltpu.make_async_copy(dq_v, dq_ref, sems.at[0])]
    for d in range(NY):
        plane = (y + d) % NY
        for q in range(4):
            slot = 4 * plane + 2 * ((c + q // 2) % 2) + q % 2
            dkv_v[d, q, 0] = acc_k[slot].astype(BF16)
            dkv_v[d, q, 1] = acc_v[slot].astype(BF16)
        outs.append(pltpu.make_async_copy(dkv_v.at[d], dkv_ref.at[d], sems.at[1 + d]))
        outs[-1].start()
    for i in range(8):
        for h in range(2):
            dq_v[h, i] = acc_q[i, h * QT : (h + 1) * QT, :].astype(BF16)
    outs[0].start()
    for out in outs:
        out.wait()


def tiles(order, lens, *arrays):
    smem = pl.BlockSpec(memory_space=pltpu.SMEM)
    hbm = pl.BlockSpec(memory_space=pl.ANY)
    split = (8, 2 * QT, HD)
    turned = (8, HD, 2 * QT)
    narrow = pltpu.VMEM((2 * QT, KT), BF16)
    listed = pltpu.SMEM((136,), jnp.int32)
    return pl.pallas_call(
        tile_kernel,
        out_shape=(
            jax.ShapeDtypeStruct((2, 8, QT, HD), BF16),
            jax.ShapeDtypeStruct((NY, 4, 2, HD, KT), BF16),
        ),
        in_specs=[smem, smem] + [hbm] * len(arrays),
        out_specs=(hbm, hbm),
        scratch_shapes=[
            pltpu.VMEM((8, QT, 2 * HD), BF16),
            pltpu.VMEM((8, QT, 2 * HD), BF16),
            pltpu.VMEM(turned, BF16),
            pltpu.VMEM(turned, BF16),
            pltpu.VMEM((16, 8, ROWS), F32),
            pltpu.VMEM(split, F32),
            pltpu.VMEM(split, F32),
            pltpu.VMEM((16, KT, 2 * HD), BF16),
            pltpu.VMEM(split, F32),
            pltpu.VMEM((16, HD, KT), F32),
            pltpu.VMEM((16, HD, KT), F32),
            pltpu.VMEM((2, 8, QT, HD), BF16),
            pltpu.VMEM((NY, 4, 2, HD, KT), BF16),
            narrow, narrow, narrow, narrow,
            listed, listed,
            pltpu.SemaphoreType.DMA((5,)),
        ],
        compiler_params=pltpu.CompilerParams(vmem_limit_bytes=VMEM_LIMIT),
        name="tiles",
    )(order, lens, *arrays)


SLOTS = (3, 1, 2, 0)


def scatter_kernel(
    dq_ref, dkv_ref,
    dq_out, dk_out, dv_out,
    own, land2, send1, land1, fin, mine, theirs, dq_v,
    load_sem, mine_sem, sib_send, sib_recv, s2_send, s2_recv, s1_send, s1_recv, f_send, f_recv, q_send, q_recv,
):
    x, z, y, c = place()
    head = 2 * x + z
    loads = [pltpu.make_async_copy(dkv_ref.at[d], own.at[d], load_sem.at[d]) for d in range(NY)]
    mine_load = pltpu.make_async_copy(dq_ref.at[c], mine, mine_sem)
    for load in [mine_load] + loads:
        load.start()
    enter(x, z, y, c)
    sibling = device(x, z, y, 1 - c)
    ways = (device(x, z, (y + 1) % NY, c), device(x, z, (y + 3) % NY, c))
    sends = []

    def send(src, dst, send_sem, recv_sem, to):
        copy = remote(src, dst, send_sem, recv_sem, to)
        copy.start()
        sends.append(copy)
        return copy

    copies2, copies1 = {}, {}
    slot = {dx: 2 * (dx % 2) + ((x + dx) % NX) // 2 for dx in SLOTS}
    for h in SLOTS:
        for part, to in enumerate(ways):
            at = part * 4 + h
            copies2[part, h] = send(dkv_ref.at[2, slot[h], part], land2.at[part, h], s2_send.at[at], s2_recv.at[at], to)
    sib_copy = send(dq_ref.at[1 - c], theirs, sib_send, sib_recv, sibling)
    for h in SLOTS:
        for way, to in enumerate(ways):
            part = 1 - way
            at = (way * 2 + part) * 4 + h
            copies1[way, part, h] = send(
                dkv_ref.at[1 + 2 * way, slot[h], part], land1.at[way, part, h], s1_send.at[at], s1_recv.at[at], to
            )

    mine_load.wait()
    sib_copy.wait_recv()
    q_copies = []
    for dx, dz in CHUNKS:
        tx, tz = (x + dx) % NX, (z + dz) % 2
        i = 2 * tx + tz
        dq_v[i] = (mine[i].astype(F32) + theirs[i].astype(F32)).astype(BF16)
        for dc in range(2):
            tc = (c + dc) % 2
            src = dq_v.at[i, rows_at(tc * ROWS, ROWS), :]
            dst = dq_out.at[:, columns(2 * head + c)]
            at = (dx * 2 + dz) * 2 + dc
            if at == 0:
                copy = pltpu.make_async_copy(src, dst, q_recv.at[at])
                copy.start()
                q_copies.append((True, copy))
            else:
                q_copies.append((False, send(src, dst, q_send.at[at], q_recv.at[at], device(tx, tz, y, tc))))

    for load in loads:
        load.wait()
    for h in SLOTS:
        for way, to in enumerate(ways):
            part = way
            copies2[part, h].wait_recv()
            total = own[1 + 2 * way, slot[h], part].astype(F32) + land2[part, h].astype(F32)
            send1[way, h] = total.astype(BF16)
            at = (way * 2 + part) * 4 + h
            copies1[way, part, h] = send(
                send1.at[way, h], land1.at[way, part, h], s1_send.at[at], s1_recv.at[at], to
            )

    f_copies = []

    def final(dx, part, out, total):
        fin[dx, part] = total.T.astype(BF16)
        for dz in range(2):
            tz = (z + dz) % 2
            src = fin.at[dx, part, rows_at(tz * ROWS, ROWS), :]
            dst = out.at[:, columns(head)]
            at = (dx * 2 + part) * 2 + dz
            if dx == 0 and dz == 0:
                copy = pltpu.make_async_copy(src, dst, f_recv.at[at])
                copy.start()
                f_copies.append((True, copy))
            else:
                to = device((x + dx) % NX, tz, y, (c + dx) % 2)
                f_copies.append((False, send(src, dst, f_send.at[at], f_recv.at[at], to)))

    for dx in SLOTS:
        for part, out in ((0, dk_out), (1, dv_out)):
            for way in range(2):
                copies1[way, part, dx].wait_recv()
            total = own[0, slot[dx], part].astype(F32) + land1[0, part, dx].astype(F32) + land1[1, part, dx].astype(F32)
            final(dx, part, out, total)

    for local, copy in q_copies + f_copies:
        if local:
            copy.wait()
        else:
            copy.wait_recv()
    for copy in sends:
        copy.wait_send()


def scatter(*arrays):
    hbm = pl.BlockSpec(memory_space=pl.ANY)
    dma = pltpu.SemaphoreType.DMA
    return pl.pallas_call(
        scatter_kernel,
        out_shape=(
            jax.ShapeDtypeStruct((ROWS, 2048), BF16),
            jax.ShapeDtypeStruct((ROWS, 1024), BF16),
            jax.ShapeDtypeStruct((ROWS, 1024), BF16),
        ),
        in_specs=[hbm] * len(arrays),
        out_specs=(hbm,) * 3,
        scratch_shapes=[
            pltpu.VMEM((NY, 4, 2, HD, KT), BF16),
            pltpu.VMEM((2, 4, HD, KT), BF16),
            pltpu.VMEM((2, 4, HD, KT), BF16),
            pltpu.VMEM((2, 2, 4, HD, KT), BF16),
            pltpu.VMEM((NX, 2, KT, HD), BF16),
            pltpu.VMEM((8, QT, HD), BF16),
            pltpu.VMEM((8, QT, HD), BF16),
            pltpu.VMEM((8, QT, HD), BF16),
            dma((NY,)), dma,
            dma, dma,
            dma((8,)), dma((8,)),
            dma((16,)), dma((16,)),
            dma((16,)), dma((16,)),
            dma((16,)), dma((16,)),
        ],
        compiler_params=pltpu.CompilerParams(collective_id=1, has_side_effects=True, vmem_limit_bytes=VMEM_LIMIT),
        name="scatter_grads",
    )(*arrays)


def store_kernel(*refs):
    count = len(refs) // 3
    ins, outs, held, (load_sem, store_sem) = refs[:count], refs[count : 2 * count], refs[2 * count : 3 * count], refs[-2:]
    loads = [pltpu.make_async_copy(ins[n], held[n], load_sem.at[n]) for n in range(count)]
    stores = [pltpu.make_async_copy(held[n], outs[n], store_sem.at[n]) for n in range(count)]
    for load in loads:
        load.start()
    for n in range(count):
        loads[n].wait()
        stores[n].start()
    for copy in stores:
        copy.wait()


def store(*arrays):
    hbm = pl.BlockSpec(memory_space=pl.ANY)
    sems = pltpu.SemaphoreType.DMA((len(arrays),))
    return pl.pallas_call(
        store_kernel,
        out_shape=tuple(jax.ShapeDtypeStruct(array.shape, array.dtype) for array in arrays),
        in_specs=[hbm] * len(arrays),
        out_specs=(hbm,) * len(arrays),
        scratch_shapes=[pltpu.VMEM(array.shape, array.dtype) for array in arrays] + [sems, sems],
        compiler_params=pltpu.CompilerParams(vmem_limit_bytes=VMEM_LIMIT),
        name="store_grads",
    )(*arrays)


def body(
    query_states,
    key_states,
    value_states,
    attn_output,
    output_grad,
    logsumexp,
    block_order,
    doc_lengths,
):
    arrays = gather(query_states, key_states, value_states, attn_output, output_grad, logsumexp)
    dq, dkv = tiles(block_order, doc_lengths, *arrays[:-1], arrays[-1].reshape(16, KT, 2 * HD))
    return store(*scatter(dq, dkv))


def solution(mesh):
    placed = (
        P(("pb", "ka"), "ha"),
        P(("ka", "pb"), "ha"),
        P(("ka", "pb"), "ha"),
        P(("pb", "ka"), "ha"),
        P(("pb", "ka"), "ha"),
        P("ha", ("pb", "ka")),
        P("ha"),
        P("ha"),
    )
    return jax.shard_map(
        body,
        mesh=mesh,
        in_specs=placed,
        out_specs=(P(("pb", "ka"), "ha"), P(("ka", "pb"), "ha"), P(("ka", "pb"), "ha")),
        check_vma=False,
    )
```

```python
from functools import partial
import math

import jax
import jax.numpy as jnp
from jax import lax
from jax.experimental import pallas as pl
from jax.experimental.pallas import tpu as pltpu
from jax.sharding import PartitionSpec as P

HD = 128
BLK = 512
ROWS = 128
NX, NY = 4, 4
VMEM_LIMIT = 60 << 20
BF16 = jnp.bfloat16
F32 = jnp.float32

softcap = 50.0
score_scale = 144.0 ** (-0.5)
log2e = math.log2(math.e)

ORDER = (0, 1, 3, 2)
CHUNKS = ((0, 0), (2, 1), (2, 0), (1, 1), (3, 1), (0, 1), (1, 0), (3, 0))
PASS = ((0,), (1,), (2, 3), (4, 5))
QT = 256
KT = 256
STEP = 32


def place():
    pb, ka = lax.axis_index("pb"), lax.axis_index("ka")
    return pb // 2, pb % 2, ka // 2, ka % 2


def device(x, z, y, c):
    return {"pb": 2 * x + z, "ka": 2 * y + c}


def remote(src, dst, send, recv, to):
    return pltpu.make_async_remote_copy(
        src_ref=src,
        dst_ref=dst,
        send_sem=send,
        recv_sem=recv,
        device_id=to,
        device_id_type=pl.DeviceIdType.MESH,
    )


def enter(x, z, y, c):
    barrier = pltpu.get_barrier_semaphore()
    for dx in range(NX):
        for dz in range(2):
            for dc in range(2):
                if (dx, dz, dc) != (0, 0, 0):
                    to = device((x + dx) % NX, (z + dz) % 2, y, (c + dc) % 2)
                    pl.semaphore_signal(barrier, inc=1, device_id=to, device_id_type=pl.DeviceIdType.MESH)
    for dy in (1, 3):
        to = device(x, z, (y + dy) % NY, c)
        pl.semaphore_signal(barrier, inc=1, device_id=to, device_id_type=pl.DeviceIdType.MESH)
    pl.semaphore_wait(barrier, 17)


def columns(head, count=1):
    return pl.ds(pl.multiple_of(head * HD, HD), count * HD)


def rows_at(start, count):
    return pl.ds(pl.multiple_of(start, ROWS), count)


def gather_kernel(
    q_ref, k_ref, v_ref, o_ref, g_ref, lse_ref,
    qh_ref, gh_ref, auxh_ref, kv_ref,
    o_v, g_v, aux_v,
    load_sem, kv_send, kv_recv, y_send, y_recv, y2_send, y2_recv, q_send, q_recv, s_send, s_recv,
    a_send, a_recv,
):
    x, z, y, c = place()
    loads = [
        pltpu.make_async_copy(o_ref, o_v, load_sem.at[0]),
        pltpu.make_async_copy(g_ref, g_v, load_sem.at[1]),
    ]
    for load in loads:
        load.start()
    enter(x, z, y, c)

    sibling = device(x, z, y, 1 - c)
    up, down = device(x, z, (y + 1) % NY, c), device(x, z, (y + 3) % NY, c)
    sends = []

    def send(src, dst, send_sem, recv_sem, to):
        copy = remote(src, dst, send_sem, recv_sem, to)
        copy.start()
        sends.append(copy)
        return copy

    def keep(src, dst, sem):
        copy = pltpu.make_async_copy(src, dst, sem)
        copy.start()
        return copy

    kv_copies = {}
    for dx, dz in ((0, 0), (0, 1), (1, 0), (3, 0), (1, 1), (3, 1), (2, 0), (2, 1)):
            tx, tz = (x + dx) % NX, (z + dz) % 2
            for part, ref in enumerate((k_ref, v_ref)):
                src = ref.at[:, columns(2 * tx + tz)]
                dst = kv_ref.at[y, c, x // 2, rows_at(z * ROWS, ROWS), pl.ds(part * HD, HD)]
                at = (dx * 2 + dz) * 2 + part
                if at < 2:
                    kv_copies[dx, dz, part] = keep(src, dst, kv_recv.at[at])
                else:
                    to = device(tx, tz, y, (c + dx) % 2)
                    kv_copies[dx, dz, part] = send(src, dst, kv_send.at[at], kv_recv.at[at], to)

    own_rows = kv_ref.at[y, c, x // 2, rows_at(z * ROWS, ROWS), :]
    other_rows = kv_ref.at[y, c, x // 2, rows_at((1 - z) * ROWS, ROWS), :]
    kv_copies[0, 0, 0].wait()
    kv_copies[0, 0, 1].wait()
    own_first = [
        send(own_rows, own_rows, y_send.at[8 + way], y_recv.at[8 + way], to) for way, to in enumerate((up, down))
    ]

    def block(plane, dx):
        return plane, (c + dx) % 2, ((x + NX - dx) % NX) // 2

    first, q_copies = {}, {}
    for dx in ORDER:
        for dz in range(2):
            for part in range(2):
                if dx != 0 or dz != 0:
                    kv_copies[dx, dz, part].wait_recv()
        rows = other_rows if dx == 0 else kv_ref.at[block(y, dx)]
        for way, to in ((0, up), (1, down)):
            at = way * NX + dx
            first[way, dx] = send(rows, rows, y_send.at[at], y_recv.at[at], to)
        for j, (jx, jz) in enumerate(CHUNKS):
            if dx != 0:
                continue
            tx, tz = (x + jx) % NX, (z + jz) % 2
            for kind, (ref, out) in enumerate(((q_ref, qh_ref), (g_ref, gh_ref))):
                src = ref.at[:, columns(2 * (2 * tx + tz), 2)]
                dst = out.at[2 * x + z, rows_at(c * ROWS, ROWS), :]
                at = 2 * j + kind
                if j == 0:
                    q_copies[j, kind] = keep(src, dst, q_recv.at[at])
                else:
                    q_copies[j, kind] = send(src, dst, q_send.at[at], q_recv.at[at], device(tx, tz, y, c))

    for load in loads:
        load.wait()
    delta = jnp.zeros((16, ROWS), F32)
    for h in range(16):
        cols = pl.ds(h * HD, HD)
        prod = g_v[:, cols].astype(F32) * o_v[:, cols].astype(F32)
        high = prod.astype(BF16)
        low = (prod - high.astype(F32)).astype(BF16)
        pick = jnp.where(lax.broadcasted_iota(jnp.int32, (16, HD), 0) == h, 1.0, 0.0).astype(BF16)
        delta = delta + (nt(pick, high) + nt(pick, low))
    for h in range(8):
        aux_v[h, 0:2, :] = lse_ref[2 * h : 2 * h + 2, :] * log2e
        aux_v[h, 2:4, :] = delta[2 * h : 2 * h + 2, :]
        aux_v[h, 4:8, :] = jnp.zeros((4, ROWS), F32)
    a_copies = []
    for j, (dx, dz) in enumerate(CHUNKS):
        tx, tz = (x + dx) % NX, (z + dz) % 2
        for dc in range(2):
            src, dst, at = aux_v.at[2 * tx + tz], auxh_ref.at[2 * (2 * x + z) + c], 2 * j + dc
            if at == 0:
                a_copies.append(keep(src, dst, a_recv.at[at]))
            else:
                a_copies.append(send(src, dst, a_send.at[at], a_recv.at[at], device(tx, tz, y, (c + dc) % 2)))

    passed = {}

    def chunk_of(j):
        dx, dz = CHUNKS[j]
        return 2 * ((x + NX - dx) % NX) + (z + 2 - dz) % 2

    def pass_on(j):
        for kind, out in enumerate((qh_ref, gh_ref)):
            if j == 0:
                q_copies[j, kind].wait()
            else:
                q_copies[j, kind].wait_recv()
            rows = out.at[chunk_of(j), rows_at(c * ROWS, ROWS), :]
            at = 2 * j + kind
            passed[j, kind] = send(rows, rows, s_send.at[at], s_recv.at[at], sibling)

    second = {}
    for n, dx in enumerate(ORDER):
        for j in PASS[n]:
            pass_on(j)
        for way, (plane, to) in enumerate((((y + 3) % NY, up), ((y + 1) % NY, down))):
            first[way, dx].wait_recv()
            if dx == 0:
                own_first[way].wait_recv()
            at = way * NX + dx
            half = kv_ref.at[block(plane, dx)].at[:, pl.ds(way * HD, HD)]
            second[way, dx] = send(half, half, y2_send.at[at], y2_recv.at[at], to)

    for j in range(len(CHUNKS)):
        if (j, 0) not in passed:
            pass_on(j)
    for n, copy in enumerate(a_copies):
        if n == 0:
            copy.wait()
        else:
            copy.wait_recv()
    for copy in passed.values():
        copy.wait_recv()
    for copy in second.values():
        copy.wait_recv()
    for copy in sends:
        copy.wait_send()


def gather(q, k, v, o, g, lse):
    hbm = pl.BlockSpec(memory_space=pl.ANY)
    dma = pltpu.SemaphoreType.DMA
    both = (8, QT, 2 * HD)
    return pl.pallas_call(
        gather_kernel,
        out_shape=tuple(
            jax.ShapeDtypeStruct(shape, kind)
            for shape, kind in (
                (both, BF16), (both, BF16), ((16, 8, ROWS), F32),
                ((NY, 2, 2, KT, 2 * HD), BF16),
            )
        ),
        in_specs=[hbm] * 5 + [pl.BlockSpec(memory_space=pltpu.VMEM)],
        out_specs=(hbm,) * 4,
        scratch_shapes=[
            pltpu.VMEM((ROWS, 2048), BF16),
            pltpu.VMEM((ROWS, 2048), BF16),
            pltpu.VMEM((8, 8, ROWS), F32),
            dma((2,)),
            dma((16,)), dma((16,)),
            dma((10,)), dma((10,)),
            dma((8,)), dma((8,)),
            dma((16,)), dma((16,)),
            dma((16,)), dma((16,)),
            dma((16,)), dma((16,)),
        ],
        compiler_params=pltpu.CompilerParams(collective_id=0, has_side_effects=True, vmem_limit_bytes=VMEM_LIMIT),
        name="gather_heads",
    )(q, k, v, o, g, lse)


def nt(a, b):
    return lax.dot_general(a, b, (((1,), (1,)), ((), ())), preferred_element_type=F32)


def nn(a, b):
    return jnp.dot(a, b, preferred_element_type=F32)


def tile_kernel(
    order_ref, lens_ref, qh_ref, gh_ref, aux_ref, kv_ref,
    dq_ref, dkv_ref,
    q_v, g_v, qt_v, gt_v, aux_v, lb_v, db_v, kv_v, acc_q, acc_k, acc_v, dq_v, dkv_v,
    p_a, p_b, ds_a, ds_b, tile_list, cut_list, sems,
):
    x, z, y, c = place()
    loads = [
        pltpu.make_async_copy(src, dst, sems.at[n])
        for n, (src, dst) in enumerate(
            (
                (aux_ref, aux_v), (qh_ref, q_v), (gh_ref, g_v), (kv_ref, kv_v),
            )
        )
    ]
    for load in loads:
        load.start()
    starts = [lens_ref[0], lens_ref[0] + lens_ref[1], lens_ref[0] + lens_ref[1] + lens_ref[2]]

    def low_of(p):
        low = jnp.zeros_like(p)
        for start in starts:
            low = jnp.where(p >= start, start, low)
        return low

    base = [order_ref[2 * i + y // 2] * BLK + (y % 2) * QT for i in range(8)]
    first_low = [low_of(base[i]) for i in range(8)]
    last_low = [low_of(base[i] + (QT - 1)) for i in range(8)]

    def list_slot(slot, counts):
        key = order_ref[slot] * BLK + ((x + c + slot // 2) % 2) * KT
        wholes, cuts = counts
        for i in range(8):
            needed = jnp.logical_and(key < base[i] + QT, key + KT > first_low[i])
            whole = jnp.logical_and(key + KT <= base[i] + 1, key >= last_low[i])
            entry = slot * 8 + i
            tile_list[wholes] = entry
            cut_list[cuts] = entry
            wholes = wholes + jnp.logical_and(needed, whole).astype(jnp.int32)
            cuts = cuts + jnp.logical_and(needed, jnp.logical_not(whole)).astype(jnp.int32)
        return wholes, cuts

    def prepare(slot, counts):
        turned = aux_v[slot].T
        for h in range(2):
            rows = pl.ds(pl.multiple_of(h * QT + (slot % 2) * ROWS, ROWS), ROWS)
            lb_v[slot // 2, rows, :] = jnp.broadcast_to(turned[:, h : h + 1], (ROWS, HD))
            db_v[slot // 2, rows, :] = jnp.broadcast_to(turned[:, 2 + h : 3 + h], (ROWS, HD))
            acc_q[slot // 2, rows, :] = jnp.zeros((ROWS, HD), F32)
        acc_k[slot] = jnp.zeros((HD, KT), F32)
        acc_v[slot] = jnp.zeros((HD, KT), F32)
        return list_slot(slot, counts)

    loads[0].wait()
    wholes, cuts = lax.fori_loop(0, 16, prepare, (0, 0), unroll=16)

    def append(n, _):
        tile_list[wholes + n] = cut_list[n]
        return 0

    lax.fori_loop(0, cuts, append, 0)
    count = wholes + cuts
    for n in range(2):
        tile_list[count + n] = 0
    pairs = (count + 1) // 2
    last = jnp.maximum(2 * pairs - 1, 1)

    def keys(t):
        return kv_v[tile_list[t] // 8, :, 0:HD]

    def values(t):
        return kv_v[tile_list[t] // 8, :, HD : 2 * HD]

    def weigh(t, p_ref, ds_ref, cut):
        i, slot = tile_list[t] % 8, tile_list[t] // 8
        if cut:
            query_base = order_ref[2 * i + y // 2] * BLK + (y % 2) * QT
            at = order_ref[slot] * BLK + ((x + c + slot // 2) % 2) * KT - query_base
            at = jnp.where(t < count, at, 1 << 20)
        step = STEP
        held = {}

        def score(n):
            cols = slice(n * HD, (n + 1) * HD)
            held[n] = (nt(q_v[i, :, cols], keys(t)), nt(g_v[i, :, cols], values(t)))

        def piece(r):
            n, o = r // QT, r % QT
            raw, dprob = held[n][0][o : o + step], held[n][1][o : o + step]
            lse = lb_v[i, r : r + step, :]
            delta = db_v[i, r : r + step, :]
            lse = jnp.concatenate([lse] * (KT // HD), axis=1)
            delta = jnp.concatenate([delta] * (KT // HD), axis=1)
            th = jnp.tanh(raw * (score_scale / softcap))
            p = jnp.exp2(th * (softcap * log2e) - lse)
            if cut:
                row = lax.broadcasted_iota(jnp.int32, (step, HD), 0) + r % QT
                low = low_of(row + query_base) - query_base
                row = jnp.concatenate([row] * (KT // HD), axis=1)
                low = jnp.concatenate([low] * (KT // HD), axis=1)
                key = lax.broadcasted_iota(jnp.int32, (step, KT), 1) + at
                p = jnp.where((key <= row) & (key >= low), p, 0.0)
            ds = p * (dprob - delta) * ((1.0 - th * th) * score_scale)
            p_ref[r : r + step, :] = p.astype(BF16)
            ds_ref[r : r + step, :] = ds.astype(BF16)

        return [partial(score, 0)] + [partial(piece, r) for r in range(0, QT // 2, step)] + [partial(score, 1)] + [partial(piece, r) for r in range(QT // 2, 2 * QT, step)]

    def gradients(t, p_ref, ds_ref):
        i, slot = tile_list[t] % 8, tile_list[t] // 8

        def key_piece(out, left, right):
            out[slot] += nn(left[i], right[...])

        def query_piece(h):
            rows = slice(h * QT, (h + 1) * QT)
            acc_q[i, rows, :] += nn(ds_ref[rows, :], keys(t))

        return [
            partial(key_piece, acc_v, gt_v, p_ref),
            partial(key_piece, acc_k, qt_v, ds_ref),
            partial(query_piece, 0),
            partial(query_piece, 1),
        ]

    def run(*lists):
        marked = [((n + 0.5) / len(pieces), m, piece) for m, pieces in enumerate(lists) for n, piece in enumerate(pieces)]
        for _, _, piece in sorted(marked, key=lambda entry: entry[:2]):
            piece()

    def step(t, old, new, cut):
        run(weigh(jnp.minimum(t + 1, last), *new, cut), gradients(t, *old))

    def pair(n, _):
        def steps(cut):
            step(2 * n, (p_a, ds_a), (p_b, ds_b), cut)
            step(2 * n + 1, (p_b, ds_b), (p_a, ds_a), cut)

        whole = 2 * n + 2 < wholes
        pl.when(whole)(lambda: steps(False))
        pl.when(jnp.logical_not(whole))(lambda: steps(True))
        return 0

    def turn(whole, turned, i):
        for h in range(2):
            turned[i, :, h * QT : (h + 1) * QT] = whole[i, :, h * HD : (h + 1) * HD].T

    for load in loads[1:]:
        load.wait()
    run(
        weigh(0, p_a, ds_a, True),
        [partial(turn, whole, turned, i) for whole, turned in ((q_v, qt_v), (g_v, gt_v)) for i in range(8)],
    )

    lax.fori_loop(0, pairs, pair, 0)

    outs = [pltpu.make_async_copy(dq_v, dq_ref, sems.at[0])]
    for d in range(NY):
        plane = (y + d) % NY
        for q in range(4):
            slot = 4 * plane + 2 * ((c + q // 2) % 2) + q % 2
            dkv_v[d, q, 0] = acc_k[slot].astype(BF16)
            dkv_v[d, q, 1] = acc_v[slot].astype(BF16)
        outs.append(pltpu.make_async_copy(dkv_v.at[d], dkv_ref.at[d], sems.at[1 + d]))
        outs[-1].start()
    for i in range(8):
        for h in range(2):
            dq_v[h, i] = acc_q[i, h * QT : (h + 1) * QT, :].astype(BF16)
    outs[0].start()
    for out in outs:
        out.wait()


def tiles(order, lens, *arrays):
    smem = pl.BlockSpec(memory_space=pltpu.SMEM)
    hbm = pl.BlockSpec(memory_space=pl.ANY)
    split = (8, 2 * QT, HD)
    turned = (8, HD, 2 * QT)
    narrow = pltpu.VMEM((2 * QT, KT), BF16)
    listed = pltpu.SMEM((136,), jnp.int32)
    return pl.pallas_call(
        tile_kernel,
        out_shape=(
            jax.ShapeDtypeStruct((2, 8, QT, HD), BF16),
            jax.ShapeDtypeStruct((NY, 4, 2, HD, KT), BF16),
        ),
        in_specs=[smem, smem] + [hbm] * len(arrays),
        out_specs=(hbm, hbm),
        scratch_shapes=[
            pltpu.VMEM((8, QT, 2 * HD), BF16),
            pltpu.VMEM((8, QT, 2 * HD), BF16),
            pltpu.VMEM(turned, BF16),
            pltpu.VMEM(turned, BF16),
            pltpu.VMEM((16, 8, ROWS), F32),
            pltpu.VMEM(split, F32),
            pltpu.VMEM(split, F32),
            pltpu.VMEM((16, KT, 2 * HD), BF16),
            pltpu.VMEM(split, F32),
            pltpu.VMEM((16, HD, KT), F32),
            pltpu.VMEM((16, HD, KT), F32),
            pltpu.VMEM((2, 8, QT, HD), BF16),
            pltpu.VMEM((NY, 4, 2, HD, KT), BF16),
            narrow, narrow, narrow, narrow,
            listed, listed,
            pltpu.SemaphoreType.DMA((5,)),
        ],
        compiler_params=pltpu.CompilerParams(vmem_limit_bytes=VMEM_LIMIT),
        name="tiles",
    )(order, lens, *arrays)


SLOTS = (3, 1, 2, 0)


def scatter_kernel(
    dq_ref, dkv_ref,
    dq_out, dk_out, dv_out,
    own, land2, send1, land1, fin, mine, theirs, dq_v,
    load_sem, mine_sem, sib_send, sib_recv, s2_send, s2_recv, s1_send, s1_recv, f_send, f_recv, q_send, q_recv,
):
    x, z, y, c = place()
    head = 2 * x + z
    loads = [pltpu.make_async_copy(dkv_ref.at[d], own.at[d], load_sem.at[d]) for d in range(NY)]
    mine_load = pltpu.make_async_copy(dq_ref.at[c], mine, mine_sem)
    for load in [mine_load] + loads:
        load.start()
    enter(x, z, y, c)
    sibling = device(x, z, y, 1 - c)
    ways = (device(x, z, (y + 1) % NY, c), device(x, z, (y + 3) % NY, c))
    sends = []

    def send(src, dst, send_sem, recv_sem, to):
        copy = remote(src, dst, send_sem, recv_sem, to)
        copy.start()
        sends.append(copy)
        return copy

    copies2, copies1 = {}, {}
    slot = {dx: 2 * (dx % 2) + ((x + dx) % NX) // 2 for dx in SLOTS}
    for h in SLOTS:
        for part, to in enumerate(ways):
            at = part * 4 + h
            copies2[part, h] = send(dkv_ref.at[2, slot[h], part], land2.at[part, h], s2_send.at[at], s2_recv.at[at], to)
    sib_copy = send(dq_ref.at[1 - c], theirs, sib_send, sib_recv, sibling)
    for h in SLOTS:
        for way, to in enumerate(ways):
            part = 1 - way
            at = (way * 2 + part) * 4 + h
            copies1[way, part, h] = send(
                dkv_ref.at[1 + 2 * way, slot[h], part], land1.at[way, part, h], s1_send.at[at], s1_recv.at[at], to
            )

    for load in loads:
        load.wait()
    for h in SLOTS:
        for way, to in enumerate(ways):
            part = way
            copies2[part, h].wait_recv()
            total = own[1 + 2 * way, slot[h], part].astype(F32) + land2[part, h].astype(F32)
            send1[way, h] = total.astype(BF16)
            at = (way * 2 + part) * 4 + h
            copies1[way, part, h] = send(
                send1.at[way, h], land1.at[way, part, h], s1_send.at[at], s1_recv.at[at], to
            )

    mine_load.wait()
    sib_copy.wait_recv()
    q_copies = []
    for dx, dz in CHUNKS:
        tx, tz = (x + dx) % NX, (z + dz) % 2
        i = 2 * tx + tz
        dq_v[i] = (mine[i].astype(F32) + theirs[i].astype(F32)).astype(BF16)
        for dc in range(2):
            tc = (c + dc) % 2
            src = dq_v.at[i, rows_at(tc * ROWS, ROWS), :]
            dst = dq_out.at[:, columns(2 * head + c)]
            at = (dx * 2 + dz) * 2 + dc
            if at == 0:
                copy = pltpu.make_async_copy(src, dst, q_recv.at[at])
                copy.start()
                q_copies.append((True, copy))
            else:
                q_copies.append((False, send(src, dst, q_send.at[at], q_recv.at[at], device(tx, tz, y, tc))))

    f_copies = []

    def final(dx, part, out, total):
        fin[dx, part] = total.T.astype(BF16)
        for dz in range(2):
            tz = (z + dz) % 2
            src = fin.at[dx, part, rows_at(tz * ROWS, ROWS), :]
            dst = out.at[:, columns(head)]
            at = (dx * 2 + part) * 2 + dz
            if dx == 0 and dz == 0:
                copy = pltpu.make_async_copy(src, dst, f_recv.at[at])
                copy.start()
                f_copies.append((True, copy))
            else:
                to = device((x + dx) % NX, tz, y, (c + dx) % 2)
                f_copies.append((False, send(src, dst, f_send.at[at], f_recv.at[at], to)))

    for dx in SLOTS:
        for part, out in ((0, dk_out), (1, dv_out)):
            for way in range(2):
                copies1[way, part, dx].wait_recv()
            total = own[0, slot[dx], part].astype(F32) + land1[0, part, dx].astype(F32) + land1[1, part, dx].astype(F32)
            final(dx, part, out, total)

    for local, copy in q_copies + f_copies:
        if local:
            copy.wait()
        else:
            copy.wait_recv()
    for copy in sends:
        copy.wait_send()


def scatter(*arrays):
    hbm = pl.BlockSpec(memory_space=pl.ANY)
    dma = pltpu.SemaphoreType.DMA
    return pl.pallas_call(
        scatter_kernel,
        out_shape=(
            jax.ShapeDtypeStruct((ROWS, 2048), BF16),
            jax.ShapeDtypeStruct((ROWS, 1024), BF16),
            jax.ShapeDtypeStruct((ROWS, 1024), BF16),
        ),
        in_specs=[hbm] * len(arrays),
        out_specs=(hbm,) * 3,
        scratch_shapes=[
            pltpu.VMEM((NY, 4, 2, HD, KT), BF16),
            pltpu.VMEM((2, 4, HD, KT), BF16),
            pltpu.VMEM((2, 4, HD, KT), BF16),
            pltpu.VMEM((2, 2, 4, HD, KT), BF16),
            pltpu.VMEM((NX, 2, KT, HD), BF16),
            pltpu.VMEM((8, QT, HD), BF16),
            pltpu.VMEM((8, QT, HD), BF16),
            pltpu.VMEM((8, QT, HD), BF16),
            dma((NY,)), dma,
            dma, dma,
            dma((8,)), dma((8,)),
            dma((16,)), dma((16,)),
            dma((16,)), dma((16,)),
            dma((16,)), dma((16,)),
        ],
        compiler_params=pltpu.CompilerParams(collective_id=1, has_side_effects=True, vmem_limit_bytes=VMEM_LIMIT),
        name="scatter_grads",
    )(*arrays)


def store_kernel(*refs):
    count = len(refs) // 3
    ins, outs, held, (load_sem, store_sem) = refs[:count], refs[count : 2 * count], refs[2 * count : 3 * count], refs[-2:]
    loads = [pltpu.make_async_copy(ins[n], held[n], load_sem.at[n]) for n in range(count)]
    stores = [pltpu.make_async_copy(held[n], outs[n], store_sem.at[n]) for n in range(count)]
    for load in loads:
        load.start()
    for n in range(count):
        loads[n].wait()
        stores[n].start()
    for copy in stores:
        copy.wait()


def store(*arrays):
    hbm = pl.BlockSpec(memory_space=pl.ANY)
    sems = pltpu.SemaphoreType.DMA((len(arrays),))
    return pl.pallas_call(
        store_kernel,
        out_shape=tuple(jax.ShapeDtypeStruct(array.shape, array.dtype) for array in arrays),
        in_specs=[hbm] * len(arrays),
        out_specs=(hbm,) * len(arrays),
        scratch_shapes=[pltpu.VMEM(array.shape, array.dtype) for array in arrays] + [sems, sems],
        compiler_params=pltpu.CompilerParams(vmem_limit_bytes=VMEM_LIMIT),
        name="store_grads",
    )(*arrays)


def body(
    query_states,
    key_states,
    value_states,
    attn_output,
    output_grad,
    logsumexp,
    block_order,
    doc_lengths,
):
    arrays = gather(query_states, key_states, value_states, attn_output, output_grad, logsumexp)
    dq, dkv = tiles(block_order, doc_lengths, *arrays[:-1], arrays[-1].reshape(16, KT, 2 * HD))
    return store(*scatter(dq, dkv))


def solution(mesh):
    placed = (
        P(("pb", "ka"), "ha"),
        P(("ka", "pb"), "ha"),
        P(("ka", "pb"), "ha"),
        P(("pb", "ka"), "ha"),
        P(("pb", "ka"), "ha"),
        P("ha", ("pb", "ka")),
        P("ha"),
        P("ha"),
    )
    return jax.shard_map(
        body,
        mesh=mesh,
        in_specs=placed,
        out_specs=(P(("pb", "ka"), "ha"), P(("ka", "pb"), "ha"), P(("ka", "pb"), "ha")),
        check_vma=False,
    )
```
